32 devices in a mesh: dp: 4 (over y, x), expert: 2 (over core), shard: 4 (over z).
Axes of the slice: x: 2, y: 2, z: 4, core: 2. Of those that a mesh axis runs over, the one named last changes fastest.
Arguments:
- tokens: bfloat16 [2048, 2048], P(('dp', 'expert')), may hold values from -6 to 6
- att_gain: bfloat16 [2048], P(('dp', 'expert')), may hold values from 0.5 to 1.5
- att_router: bfloat16 [2048, 8], P(('dp', 'expert')), may hold values from -0.125 to 0.125
- kv_weight: bfloat16 [2048, 2, 2048], P(('dp', 'expert'), None, 'shard'), may hold values from -0.125 to 0.125
- query_weight: bfloat16 [8, 2048, 2048], P('expert', 'dp', 'shard'), may hold values from -0.125 to 0.125
- out_weight: bfloat16 [8, 2048, 2048], P('expert', 'dp', 'shard'), may hold values from -0.75 to 0.75
- mlp_gain: bfloat16 [2048], P(('dp', 'expert')), may hold values from 0.5 to 1.5
- mlp_router: bfloat16 [2048, 8], P(('dp', 'expert')), may hold values from -0.125 to 0.125
- gate_weight: bfloat16 [8, 2048, 5632], P('expert', 'dp', 'shard'), may hold values from -0.125 to 0.125
- up_weight: bfloat16 [8, 2048, 5632], P('expert', 'dp', 'shard'), may hold values from -0.125 to 0.125
- down_weight: bfloat16 [8, 2048, 5632], P('expert', 'dp', 'shard'), may hold values from -0.078125 to 0.078125
- att_routes: int32 [2048, 2], P(('dp', 'expert')), may hold values from 0 to 7, all different within a row; in each aligned block of 256 rows (0 to 255, 256 to 511, ...) at most 80 rows name the same one
- mlp_routes: int32 [2048, 2], P(('dp', 'expert')), may hold values from 0 to 7, all different within a row; in each aligned block of 256 rows (0 to 255, 256 to 511, ...) at most 80 rows name the same one
- cotangent: bfloat16 [2048, 2048], P(('dp', 'expert')), may hold values from -6 to 6
Outputs:
- layer_out: float32 [2048, 2048], P(('dp', 'expert'))
- aux_loss: float32 [1], replicated
- grad_tokens: float32 [2048, 2048], P(('dp', 'expert'))
- grad_att_gain: float32 [2048], P(('dp', 'expert'))
- grad_att_router: float32 [2048, 8], P(('dp', 'expert'))
- grad_kv_weight: float32 [2048, 2, 2048], P(('dp', 'expert'), None, 'shard')
- grad_query_weight: float32 [8, 2048, 2048], P('expert', 'dp', 'shard')
- grad_out_weight: float32 [8, 2048, 2048], P('expert', 'dp', 'shard')
- grad_mlp_gain: float32 [2048], P(('dp', 'expert'))
- grad_mlp_router: float32 [2048, 8], P(('dp', 'expert'))
- grad_gate_weight: float32 [8, 2048, 5632], P('expert', 'dp', 'shard')
- grad_up_weight: float32 [8, 2048, 5632], P('expert', 'dp', 'shard')
- grad_down_weight: float32 [8, 2048, 5632], P('expert', 'dp', 'shard')
- balance_terms: float32 [2, 8], replicated
The draws below stay inside these ranges and needn't reach their ends.
Inputs may be any that keep to these rules, and one draw needn't show every extreme that they name: `att_routes`: each row names 2 different experts. Within the rows of one index pair of dp and expert no expert is named more than 80 times, and in some such block an expert is named exactly 80 times. `mlp_routes`: each row names 2 different experts. Within the rows of one index pair of dp and expert no expert is named more than 80 times, and in some such block an expert is named exactly 80 times.
All inputs are finite; a program needn't handle non-finite values.
Results may differ from the reference program's by a relative error of at most 0.02.
Values may be sent and summed in bfloat16 or wider, within the bound.
No kernel may reach another device: no remote copies, remote signals or barrier semaphores. Data moves between devices by JAX's collectives and lax.ppermute only.
A program may use at most 384 MiB of HBM per device.

```python
import math
import jax
import jax.numpy as jnp
import numpy as np
from jax import lax

D = 2048
HEADS = 16
HEAD_DIM = 128
EXPERTS = 8
TOPK = 2
FF = 5632
TOK_DEV = 256
CAP = 80
SEQ = 512
TOKENS = 2048
N_DP = 4
N_EXPERT = 2


def block_levels(own_key, shape, cuts, least, largest):
    level = 1.0
    for dim, blocks in cuts:
        draws = jax.random.uniform(jax.random.fold_in(jax.random.fold_in(own_key, 6), dim), (blocks,), jnp.float32, least / len(cuts), largest / len(cuts))
        level = level * jnp.repeat(jnp.exp(draws), shape[dim] // blocks).reshape((-1,) + (1,) * (len(shape) - 1 - dim))
    return level


def assign_block(stream_key, own, number, rows, number_of, top, most, slope):
    ranking = jax.random.permutation(stream_key, number_of)
    heavy_load, common = shares(number_of, rows * top, most, slope, True), shares(number_of, rows * top, most, slope, False)
    places = jnp.arange(number_of)

    def named(sizes, offset_by):
        used = int((sizes > 0).sum())
        fixed = max(1, used // 4)
        shifted = fixed + (places - fixed + offset_by * (used - fixed)) % max(1, number_of - fixed)
        return jnp.zeros((number_of,), jnp.int32).at[ranking[jnp.where(places < fixed, places, shifted)]].set(jnp.asarray(sizes, jnp.int32))

    sizes = jnp.where(number % 4 == 0, named(heavy_load, number // 4), named(common, number - number // 4 - 1))
    mixed = jax.random.permutation(jax.random.fold_in(own, 3), number_of)
    source_of, sink = mixed[0:number_of // 2 * 2:2], mixed[1:number_of // 2 * 2:2]
    slack = jnp.minimum(sizes[source_of] - 1, most - sizes[sink]) // 2
    slack = jnp.where((source_of == ranking[0]) | (sink == ranking[0]) | (sizes[sink] == 0), 0, jnp.maximum(slack, 0))
    shifted = jax.random.randint(jax.random.fold_in(own, 4), (number_of // 2,), 0, 1 << 20) % (slack + 1)
    sizes = sizes.at[source_of].add(-shifted).at[sink].add(shifted)
    items = jnp.searchsorted(jnp.cumsum(sizes), jnp.arange(rows * top), side="right").astype(jnp.int32)
    table = items.reshape(top, rows).T
    table = table[jax.random.permutation(jax.random.fold_in(own, 1), rows)]
    offset_by = jax.random.randint(jax.random.fold_in(own, 2), (rows, 1), 0, top)
    return jnp.take_along_axis(table, (jnp.arange(top)[None, :] + offset_by) % top, axis=1)


def shares(count, total, limit, lean, full):
    loads = [(1 << 20) // math.isqrt(standing ** lean) + 1 for standing in range(1, count + 1)]
    largest = limit if full else min(limit, max(-(-total // count), total * loads[0] // sum(loads)))
    least = 1 if total - largest >= count - 1 else 0
    given, surplus = [largest] + [least] * (count - 1), total - largest - least * (count - 1)
    while surplus > 0:
        free = [i for i in range(1, count) if given[i] < largest] or [i for i in range(1, count) if given[i] < limit]
        mass, left = sum([loads[i] for i in free]), surplus
        for i in free:
            more = min(limit - given[i], max(1, left * loads[i] // mass), surplus)
            given[i] = given[i] + more
            surplus = surplus - more
    return np.array(given)


def scatter_about(stream_key, shape, deviation, most, pieces=(), kind=jnp.bfloat16):
    array = jax.random.normal(stream_key, shape, jnp.float32) * deviation
    if len(pieces) > 0:
        array = block_levels(stream_key, shape, pieces, -0.22, 0.18) * array
    return jnp.clip(array, min=-most, max=most).astype(kind)


def setup_inputs(seed: int = 0) -> dict:
    key_list = jax.random.split(jax.random.key(seed), 15)
    tokens = scatter_about(key_list[0], (TOKENS, D), 1.0, 6.0, ((0, 8),))
    att_gain = jnp.clip(1.0 + 0.1 * jax.random.normal(key_list[1], (D,), jnp.float32), 0.5, 1.5).astype(jnp.bfloat16)
    att_router = scatter_about(key_list[2], (D, EXPERTS), D ** -0.5, 0.125, ((0, 8),))
    kv_weight = scatter_about(key_list[3], (D, 2, HEADS * HEAD_DIM), D ** -0.5, 0.125, ((0, 8), (2, 4)))
    query_weight = scatter_about(key_list[4], (EXPERTS, D, HEADS * HEAD_DIM), D ** -0.5, 0.125, ((0, 2), (1, 4), (2, 4)))
    out_weight = scatter_about(key_list[5], (EXPERTS, D, HEADS * HEAD_DIM), (max(1, HEADS * HEAD_DIM * 16 // (TOK_DEV * N_EXPERT))) ** -0.5, 0.75, ((0, 2), (1, 4), (2, 4)))
    mlp_gain = jnp.clip(1.0 + 0.1 * jax.random.normal(key_list[6], (D,), jnp.float32), 0.5, 1.5).astype(jnp.bfloat16)
    mlp_router = scatter_about(key_list[7], (D, EXPERTS), D ** -0.5, 0.125, ((0, 8),))
    gate_weight = scatter_about(key_list[8], (EXPERTS, D, FF), D ** -0.5, 0.125, ((0, 2), (1, 4), (2, 4)))
    up_weight = scatter_about(key_list[9], (EXPERTS, D, FF), D ** -0.5, 0.125, ((0, 2), (1, 4), (2, 4)))
    down_weight = scatter_about(key_list[10], (EXPERTS, D, FF), FF ** -0.5, 0.078125, ((0, 2), (1, 4), (2, 4)))
    att_routes_keys = jax.random.split(jax.random.fold_in(key_list[11], 1), TOKENS // TOK_DEV)
    att_routes_turns = jax.random.permutation(jax.random.fold_in(key_list[11], 3), TOKENS // TOK_DEV)
    att_routes = jax.vmap(lambda own, number: assign_block(jax.random.fold_in(key_list[11], 2), own, number, TOK_DEV, EXPERTS, TOPK, CAP, 1))(att_routes_keys, att_routes_turns).reshape((TOKENS, TOPK))
    mlp_routes_keys = jax.random.split(jax.random.fold_in(key_list[12], 1), TOKENS // TOK_DEV)
    mlp_routes_turns = jax.random.permutation(jax.random.fold_in(key_list[12], 3), TOKENS // TOK_DEV)
    mlp_routes = jax.vmap(lambda own, number: assign_block(jax.random.fold_in(key_list[12], 2), own, number, TOK_DEV, EXPERTS, TOPK, CAP, 1))(mlp_routes_keys, mlp_routes_turns).reshape((TOKENS, TOPK))
    cotangent = scatter_about(key_list[13], (TOKENS, D), 1.0, 6.0, ((0, 8),))
    return {"tokens": tokens, "att_gain": att_gain, "att_router": att_router, "kv_weight": kv_weight, "query_weight": query_weight, "out_weight": out_weight, "mlp_gain": mlp_gain, "mlp_router": mlp_router, "gate_weight": gate_weight, "up_weight": up_weight, "down_weight": down_weight, "att_routes": att_routes, "mlp_routes": mlp_routes, "cotangent": cotangent}


EPSILON = 1e-06
AUX_WEIGHT = 0.01
MASKED = -1e+30
HIGHEST = lax.Precision.HIGHEST

@jax.custom_vjp
def low(v):
    return lax.optimization_barrier(v.astype(jnp.bfloat16)).astype(jnp.float32)

@jax.custom_vjp
def low_back(v):
    return v

def low_keep(v):
    return (low(v), None)

def low_pass(kept, grad):
    return (grad,)

def back_keep(v):
    return (v, None)

def back_low(kept, grad):
    return (low(grad),)
low.defvjp(low_keep, low_pass)
low_back.defvjp(back_keep, back_low)

def matmul(left, right):
    return jnp.dot(left, right, precision=HIGHEST, preferred_element_type=jnp.float32)

def attend(queries_in, key_rows, value_rows, w_query, w_out):
    queries = low(low_back(matmul(queries_in, w_query))).reshape(SEQ, HEADS, HEAD_DIM)
    block_rows = min(SEQ, 512)
    score_scale = HEAD_DIM ** (-0.5)
    key_pos = jnp.arange(SEQ, dtype=jnp.int32)

    def one_block(offset):
        block_q = lax.dynamic_slice_in_dim(queries, offset, block_rows, 0)
        scores = low_back(jnp.einsum('qhd,khd->hqk', block_q, key_rows, precision=HIGHEST) * score_scale)
        query_pos = offset + jnp.arange(block_rows, dtype=jnp.int32)
        scores = jnp.where(key_pos[None, None, :] <= query_pos[None, :, None], scores, MASKED)
        weights = low(jax.nn.softmax(scores, axis=-1))
        return jnp.einsum('hqk,khd->qhd', weights, value_rows, precision=HIGHEST)
    starts = jnp.arange(0, SEQ, block_rows, dtype=jnp.int32)
    mixture = lax.map(jax.checkpoint(one_block), starts).reshape(SEQ, HEADS * HEAD_DIM)
    mixture = low(low_back(mixture))
    return low(low_back(matmul(mixture, w_out.T)))

def feed(expert_in, w_gate, w_up, w_down):
    gating = low_back(matmul(expert_in, w_gate))
    upward = low_back(matmul(expert_in, w_up))
    active = low(jax.nn.silu(gating) * upward)
    return low(low_back(matmul(active, w_down.T)))

def combine(expert_out, logits, routes):
    choose = (routes[:, :, None] == jnp.arange(EXPERTS, dtype=jnp.int32)[None, None, :]).astype(jnp.float32)
    picked = jnp.einsum('tce,etd->tcd', choose, expert_out, precision=HIGHEST)
    route_gates = jax.nn.softmax(jnp.take_along_axis(logits, routes, axis=1), axis=1)
    return route_gates[:, 0:1] * picked[:, 0] + route_gates[:, 1:2] * picked[:, 1]

def rms_scale(values):
    return lax.rsqrt(lax.optimization_barrier(jnp.mean(values * values, axis=1, keepdims=True)) + EPSILON)

def layer(inputs, routes_a, routes_m, params):
    att_gain, att_router, kv_weight, query_weight, out_weight, mlp_gain, mlp_router, gate_weight, up_weight, down_weight = params
    normed = low(inputs * rms_scale(inputs) * att_gain)
    logits_a = matmul(normed, att_router)
    key_value = low(low_back(jnp.einsum('td,dcf->tcf', normed, kv_weight, precision=HIGHEST)))
    key_rows = key_value[:, 0].reshape(SEQ, HEADS, HEAD_DIM)
    value_rows = key_value[:, 1].reshape(SEQ, HEADS, HEAD_DIM)

    def attention_expert(weight_pair):
        return attend(low_back(normed), key_rows, value_rows, weight_pair[0], weight_pair[1])
    att_out = lax.map(jax.checkpoint(attention_expert), (query_weight, out_weight))
    middle = inputs + combine(att_out, logits_a, routes_a)
    normed_m = low(middle * rms_scale(middle) * mlp_gain)
    logits_m = matmul(normed_m, mlp_router)

    def feed_expert(weight_set):
        return feed(low_back(normed_m), weight_set[0], weight_set[1], weight_set[2])
    mlp_out = lax.map(jax.checkpoint(feed_expert), (gate_weight, up_weight, down_weight))
    result = middle + combine(mlp_out, logits_m, routes_m)
    return (result, lax.optimization_barrier(jnp.sum(jax.nn.softmax(logits_a, axis=1), axis=0)), lax.optimization_barrier(jnp.sum(jax.nn.softmax(logits_m, axis=1), axis=0)))

def route_count(routes):
    return lax.optimization_barrier(jnp.sum((routes[:, :, None] == jnp.arange(EXPERTS, dtype=jnp.int32)[None, None, :]).astype(jnp.float32), axis=(0, 1)))

def forward(tokens, att_gain, att_router, kv_weight, query_weight, out_weight, mlp_gain, mlp_router, gate_weight, up_weight, down_weight, att_routes, mlp_routes):
    params = (att_gain, att_router, kv_weight, query_weight, out_weight, mlp_gain, mlp_router, gate_weight, up_weight, down_weight)

    def per_sequence(members):
        return layer(members[0], members[1], members[2], params)
    result, probs_a, probs_m = lax.map(jax.checkpoint(per_sequence), (tokens.reshape(N_DP, SEQ, D), att_routes.reshape(N_DP, SEQ, TOPK), mlp_routes.reshape(N_DP, SEQ, TOPK)))
    term_a = EXPERTS * EXPERTS * (route_count(att_routes) / (TOKENS * TOPK)) * (lax.optimization_barrier(jnp.sum(probs_a, axis=0)) / TOKENS)
    term_m = EXPERTS * EXPERTS * (route_count(mlp_routes) / (TOKENS * TOPK)) * (lax.optimization_barrier(jnp.sum(probs_m, axis=0)) / TOKENS)
    terms = jnp.stack([term_a, term_m])
    aux_loss = (jnp.sum(terms) / EXPERTS).reshape(1)
    return (result.reshape(TOKENS, D), aux_loss, terms)

def reference(tokens, att_gain, att_router, kv_weight, query_weight, out_weight, mlp_gain, mlp_router, gate_weight, up_weight, down_weight, att_routes, mlp_routes, cotangent):
    floats = tuple((member.astype(jnp.float32) for member in (tokens, att_gain, att_router, kv_weight, query_weight, out_weight, mlp_gain, mlp_router, gate_weight, up_weight, down_weight)))

    def closed(*inputs):
        return forward(*inputs, att_routes, mlp_routes)
    (result, aux_loss, terms), pullback = jax.vjp(closed, *floats)
    gradients = pullback((cotangent.astype(jnp.float32), jnp.full((1,), AUX_WEIGHT, jnp.float32), jnp.zeros((2, EXPERTS), jnp.float32)))
    return (result, aux_loss, gradients[0], gradients[1], gradients[2], gradients[3], gradients[4], gradients[5], gradients[6], gradients[7], gradients[8], gradients[9], gradients[10], terms)
```

```python
import jax
import jax.numpy as jnp
from jax import lax
from jax.sharding import PartitionSpec as P

HEAD_DIM = 128
EXPERTS = 8
TOPK = 2
EPSILON = 1e-06
AUX_WEIGHT = 0.01
MASKED = -1e30
HIGHEST = lax.Precision.HIGHEST
BF16 = jnp.bfloat16
F32 = jnp.float32


def dot32(spec, left, right):
    return jnp.einsum(spec, left, right, preferred_element_type=F32)


def swap(value, axis, flip):
    size = lax.axis_size(axis)
    return lax.ppermute(value, axis, [(i, i ^ flip) for i in range(size)])


def bits_in(size):
    count = 0
    while (1 << count) < size:
        count += 1
    return count


def split_bits(value, axis, bits):
    shape = value.shape
    return value.reshape(shape[:axis] + (2,) * bits + shape[axis + 1 :])


def join_bits(value, axis, bits):
    shape = value.shape
    return value.reshape(shape[:axis] + (1 << bits,) + shape[axis + bits :])


def gather_rows(own, axis, order):
    value, held = own, []
    for bit in reversed(order):
        received = swap(value, "dp", 1 << bit)
        place = sum(1 for other in held if other > bit)
        value = jnp.stack([value, received], axis=axis + place)
        held.append(bit)
    return join_bits(value, axis, len(order))


def scatter_product(spec, rows, weights, axis, order):
    bits = len(order)
    rows = split_bits(rows, axis, bits)
    held = list(range(bits - 1, -1, -1))
    place = axis + held.index(order[0])
    send = dot32(spec, join_bits(lax.index_in_dim(rows, 1, place, False), axis, bits - 1), weights)
    received = swap(send.astype(BF16), "dp", 1 << order[0])
    keep = dot32(spec, join_bits(lax.index_in_dim(rows, 0, place, False), axis, bits - 1), weights)
    value = (keep + received.astype(F32)).astype(BF16)
    value = split_bits(value, axis, bits - 1)
    held.remove(order[0])
    for bit in order[1:]:
        place = axis + held.index(bit)
        received = swap(lax.index_in_dim(value, 1, place, False), "dp", 1 << bit)
        value = lax.index_in_dim(value, 0, place, False) + received
        held.remove(bit)
    return value


def total_dp(value, bits):
    value = split_bits(value, 0, bits)
    for bit in range(bits):
        received = swap(value, "dp", 1 << bit)
        value = value + jnp.flip(received, axis=bits - 1 - bit)
    return join_bits(value, 0, bits)


def total_shard(value, bits):
    index = lax.axis_index("shard")
    for bit in range(bits):
        mine = (index >> bit) & 1
        half = value.shape[0] // 2
        send = lax.dynamic_slice_in_dim(value, (1 - mine) * half, half, 0)
        keep = lax.dynamic_slice_in_dim(value, mine * half, half, 0)
        value = keep + swap(send, "shard", 1 << bit)
    for bit in reversed(range(bits)):
        mine = (index >> bit) & 1
        received = swap(value, "shard", 1 << bit)
        value = jnp.where(
            mine == 0,
            jnp.concatenate([value, received], axis=0),
            jnp.concatenate([received, value], axis=0),
        )
    return value


def total_block(partial_value, bits):
    own = partial_value[:, 0] + swap(partial_value[:, 1], "expert", 1)
    count, rows, width = own.shape
    return total_shard(own.reshape(count * rows, width), bits).reshape(count, rows, width)


def both_blocks(own, axis):
    return jnp.stack([own, swap(own, "expert", 1)], axis=axis)


def spread_columns(pieces):
    return [pieces[0]] + [swap(pieces[d], "dp", d) for d in range(1, len(pieces))]


def place_columns(pieces):
    index = lax.axis_index("dp")
    rows, width = pieces[0].shape
    out = jnp.zeros((rows, width * len(pieces)), F32)
    for d, piece in enumerate(pieces):
        out = lax.dynamic_update_slice(out, piece.astype(F32), (0, (index ^ d) * width))
    return out


def route_tables(routes, first, local_count, capacity):
    experts = jnp.arange(EXPERTS, dtype=jnp.int32)[:, None]
    member = routes[:, :, 0:1] == experts
    for choice in range(1, TOPK):
        member = member | (routes[:, :, choice : choice + 1] == experts)
    count = routes.shape[-1]
    before = (
        jnp.arange(count, dtype=jnp.int32)[:, None] < jnp.arange(count, dtype=jnp.int32)[None, :]
    ).astype(BF16)
    ranks = dot32("dbet,tu->dbeu", member.astype(BF16), before)
    ranks = jnp.where(member, ranks, -1.0)
    mine = lax.dynamic_slice_in_dim(ranks, first, local_count, 2)
    slots = jnp.arange(capacity, dtype=jnp.int32).astype(F32)[:, None]
    table = (mine[:, :, :, None, :] == slots).astype(BF16)
    return (member, table)


def expert_gates(logits, member):
    peak = jnp.max(jnp.where(member, logits, MASKED), axis=2, keepdims=True)
    weights = jnp.where(member, jnp.exp(jnp.minimum(logits - peak, 0.0)), 0.0)
    return weights / jnp.sum(weights, axis=2, keepdims=True)


def to_rows(table, token_values):
    return jnp.sum(table.astype(F32) * token_values[..., None, :], axis=-1)


def per_device(
    tokens,
    att_gain,
    att_router,
    kv_weight,
    query_weight,
    out_weight,
    mlp_gain,
    mlp_router,
    gate_weight,
    up_weight,
    down_weight,
    att_routes,
    mlp_routes,
    cotangent,
):
    owners = lax.axis_size("expert")
    groups = lax.axis_size("dp")
    shards = lax.axis_size("shard")
    bits = bits_in(groups)
    shard_bits = bits_in(shards)
    local_count = EXPERTS // owners
    count, model_width = tokens.shape
    width = model_width // groups
    part = width // owners
    capacity = 5 * count * TOPK // (4 * EXPERTS)
    all_tokens = count * owners * groups
    features = query_weight.shape[2]
    heads = features // HEAD_DIM
    score_scale = HEAD_DIM ** (-0.5)
    me = lax.axis_index("dp")
    core = lax.axis_index("expert")
    first = core * local_count
    order_a = list(range(bits))
    order_b = order_a[bits // 2 :] + order_a[: bits // 2]

    both = jnp.stack([tokens, cotangent])
    pieces = [
        lax.dynamic_slice_in_dim(both, (me ^ d) * width, width, 2) for d in range(groups)
    ]
    spread = both_blocks(jnp.stack(spread_columns(pieces)), 2)
    inputs, grad_out = spread[:, 0], spread[:, 1]
    routes = jnp.stack(
        [att_routes[:, 0], att_routes[:, 1], mlp_routes[:, 0], mlp_routes[:, 1]]
    )
    routes = gather_rows(both_blocks(routes, 0), 0, order_a)
    small = jnp.concatenate(
        [att_gain[:, None], mlp_gain[:, None], att_router, mlp_router], axis=1
    )
    small_other = swap(small, "expert", 1)
    small = jnp.where(
        core == 0,
        jnp.concatenate([small, small_other]),
        jnp.concatenate([small_other, small]),
    ).astype(F32)
    gain_a, gain_m = small[:, 0], small[:, 1]
    router_a, router_m = small[:, 2 : 2 + EXPERTS], small[:, 2 + EXPERTS :]

    member_a, table_a = route_tables(routes[:, :, :TOPK], first, local_count, capacity)
    member_m, table_m = route_tables(routes[:, :, TOPK:], first, local_count, capacity)
    rows_shape = (local_count, groups, owners * capacity)

    def dispatch(table, values):
        picked = dot32("dbest,dbtk->edbsk", table, values).astype(BF16)
        return picked.reshape(rows_shape + (picked.shape[-1],))

    def combine(table, rows):
        parts = rows.reshape(rows_shape[:2] + (owners, capacity, rows.shape[-1]))
        return dot32("dbest,edbsk->dbtk", table, parts)

    def row_order(values):
        return jnp.transpose(values, (2, 0, 1, 3)).reshape(rows_shape)

    def local_experts(values):
        return lax.dynamic_slice_in_dim(values, first, local_count, 2)

    def in_halves(function, value, axis=0):
        half = value.shape[axis] // 2
        return jnp.concatenate(
            [
                function(lax.slice_in_dim(value, 0, half, axis=axis), order_a),
                function(lax.slice_in_dim(value, half, 2 * half, axis=axis), order_b),
            ],
            axis=axis,
        )

    def scatter_halves(spec, rows, weights):
        half = local_count // 2
        return jnp.concatenate(
            [
                scatter_product(spec, rows[:half], weights[:half], 1, order_a),
                scatter_product(spec, rows[half:], weights[half:], 1, order_b),
            ]
        )

    def gather_halves(rows):
        return in_halves(lambda value, order: gather_rows(value, 1, order), rows)

    grad_rows_m = dispatch(table_m, grad_out)
    grad_act = scatter_halves("edrk,ekf->edrf", grad_rows_m, down_weight)

    scaled_kv = (kv_weight.astype(F32) * lax.dynamic_slice_in_dim(gain_a, core * part, part)[:, None, None]).astype(BF16)
    kv_parts = jnp.stack(
        [
            gather_rows(scaled_kv[:, 0], 0, order_a),
            gather_rows(scaled_kv[:, 1], 0, order_b),
        ],
        axis=2,
    )
    kv_all = both_blocks(kv_parts, 1)
    own_tokens = jnp.stack(
        [
            jnp.stack(
                [
                    lax.dynamic_slice_in_dim(
                        tokens, ((me ^ d) * owners + (core ^ b)) * part, part, 1
                    )
                    for b in range(owners)
                ],
                axis=1,
            )
            for d in range(groups)
        ],
        axis=1,
    )
    own_float = tokens.astype(F32)
    own_rms = lax.rsqrt(jnp.mean(own_float * own_float, axis=1) + EPSILON)
    key_value = dot32(
        "tk,kcf->ctf",
        own_tokens.reshape(count, model_width),
        kv_all.reshape(model_width, 2, features),
    )
    key_value = (key_value * own_rms[None, :, None]).astype(BF16)
    key_value = both_blocks(key_value, 1).reshape(2, owners * count, heads, HEAD_DIM)
    keys, values = key_value[0], key_value[1]
    seq_rms = both_blocks(own_rms, 0)

    inputs_f = inputs.astype(F32)
    scaled_a = (inputs_f * gain_a).astype(BF16)
    rows_a = dispatch(table_a, scaled_a)
    row_rms_a = jnp.transpose(to_rows(table_a[0], seq_rms[:, None, :]), (1, 0, 2)).reshape(
        local_count, owners * capacity
    )
    token_pos = (
        jnp.arange(count, dtype=jnp.int32)[None, :]
        + ((core ^ jnp.arange(owners, dtype=jnp.int32)) * count)[:, None]
    ).astype(F32)
    row_pos = jnp.transpose(to_rows(table_a[0], token_pos[:, None, :]), (1, 0, 2)).reshape(-1)
    queries = scatter_halves("edrk,ekf->edrf", rows_a, query_weight)
    queries = (queries.astype(F32) * row_rms_a[..., None]).astype(BF16)
    flat_queries = queries.reshape(-1, heads, HEAD_DIM)
    allowed = token_pos.reshape(1, 1, -1) <= row_pos[None, :, None]

    def scores_of(query_rows):
        scores = dot32("qhd,khd->hqk", query_rows, keys) * score_scale
        return jnp.where(allowed, scores, MASKED)

    scores = scores_of(flat_queries)
    peak = jnp.max(scores, axis=-1, keepdims=True)
    expo = jnp.exp(scores - peak)
    denom = jnp.sum(expo, axis=-1, keepdims=True)
    probs = (expo / denom).astype(BF16)
    log_total = peak + jnp.log(denom)
    mixture = dot32("hqk,khd->qhd", probs, values).astype(BF16)
    mixture = mixture.reshape(local_count, owners * capacity, features)
    mixture_all = gather_halves(mixture)

    def statistics(values, scaled, router):
        squares = jnp.sum(values * values, axis=-1)[:, :, None]
        logits = dot32("dbtk,ke->dbet", scaled, router.astype(BF16))
        sums = total_dp(jnp.concatenate([squares, logits], axis=2), bits)
        rms = lax.rsqrt(sums[:, :, 0] / model_width + EPSILON)
        return (rms, sums[:, :, 1:] * rms[:, :, None])

    rms_a, logits_a = statistics(inputs_f, scaled_a, router_a)
    gates_a = expert_gates(logits_a, member_a)
    row_gates_a = row_order(to_rows(table_a, local_experts(gates_a)))
    out_rows = dot32("edrf,ekf->edrk", mixture_all, out_weight)
    att_part = combine(table_a, (out_rows * row_gates_a[..., None]).astype(BF16)).astype(BF16)
    middle = inputs_f + both_blocks(total_block(att_part, shard_bits), 1).astype(F32)

    scaled_m = (middle * gain_m).astype(BF16)
    rms_m, logits_m = statistics(middle, scaled_m, router_m)
    gates_m = expert_gates(logits_m, member_m)
    rows_m = dispatch(table_m, scaled_m)
    row_gates_m = row_order(to_rows(table_m, local_experts(gates_m)))
    row_rms_m = row_order(to_rows(table_m, rms_m[:, :, None]))[:, 0]
    gating = scatter_product("edrk,ekf->edrf", rows_m, gate_weight, 1, order_a)
    upward = scatter_product("edrk,ekf->edrf", rows_m, up_weight, 1, order_b)
    gating = gating.astype(F32) * row_rms_m[..., None]
    upward = upward.astype(F32) * row_rms_m[..., None]
    sigma = jax.nn.sigmoid(gating)
    silu = gating * sigma
    active = (silu * upward).astype(BF16)
    grad_act = grad_act.astype(F32)
    grad_row_gates_m = jnp.sum(grad_act * active.astype(F32), axis=-1)
    grad_act = grad_act * (row_gates_m[:, 0] * row_rms_m)[..., None]
    grad_gating = (grad_act * upward * sigma * (1.0 + gating * (1.0 - sigma))).astype(BF16)
    grad_upward = (grad_act * silu).astype(BF16)
    grad_gating_all = gather_rows(grad_gating, 1, order_a)
    grad_upward_all = gather_rows(grad_upward, 1, order_b)
    active_all = gather_halves(active)

    def router_part(grad_row_gates, table, gates, member, logits, rms):
        by_row = grad_row_gates.reshape(local_count, owners, capacity)
        by_token = jnp.einsum("best,ebs->bet", table[0].astype(F32), by_row, precision=HIGHEST)
        wide = jnp.zeros((owners, EXPERTS, count), F32)
        wide = lax.dynamic_update_slice_in_dim(wide, by_token, first, 1)
        wide = gather_rows(wide, 0, order_a)
        picked = gates * (wide - jnp.sum(gates * wide, axis=2, keepdims=True))
        fraction = jnp.sum(member.astype(F32), axis=(0, 1, 3)) / (all_tokens * TOPK)
        weighting = (AUX_WEIGHT * EXPERTS / all_tokens) * fraction[:, None]
        probs = jax.nn.softmax(logits, axis=2)
        aux = probs * (weighting - jnp.sum(probs * weighting, axis=2, keepdims=True))
        balance = EXPERTS * EXPERTS * fraction * (jnp.sum(probs, axis=(0, 1, 3)) / all_tokens)
        return ((picked + aux / (owners * shards)) * rms[:, :, None], balance)

    router_rows_m, balance_m = router_part(
        grad_row_gates_m, table_m, gates_m, member_m, logits_m, rms_m
    )
    grad_in_rows = dot32("edrf,ekf->edrk", grad_gating_all, gate_weight) + dot32(
        "edrf,ekf->edrk", grad_upward_all, up_weight
    )
    back_m = combine(table_m, grad_in_rows.astype(BF16)) + jnp.einsum(
        "dbet,ke->dbtk", router_rows_m, router_m, precision=HIGHEST
    )
    back_m = both_blocks(total_block(back_m.astype(BF16), shard_bits), 1).astype(F32)
    grad_gate_weight = dot32("edrk,edrf->ekf", rows_m, grad_gating_all)
    grad_up_weight = dot32("edrk,edrf->ekf", rows_m, grad_upward_all)
    gated_rows_m = (grad_rows_m.astype(F32) * row_gates_m[..., None]).astype(BF16)
    grad_down_weight = dot32("edrk,edrf->ekf", gated_rows_m, active_all)
    mlp_rows = dot32("edrf,ekf->edrk", active_all, down_weight)
    mlp_part = combine(table_m, (mlp_rows * row_gates_m[..., None]).astype(BF16)).astype(BF16)
    layer_block = middle[:, 0] + total_block(mlp_part, shard_bits).astype(F32)
    layer_out = place_columns(spread_columns([layer_block[d].astype(BF16) for d in range(groups)]))

    def router_grad(scaled, rows):
        partial_value = jnp.einsum("dbtk,dbet->ke", scaled.astype(F32), rows, precision=HIGHEST)
        partial_value = lax.psum(partial_value, ("expert", "shard"))
        return lax.dynamic_slice_in_dim(partial_value, core * part, part, 0)

    def norm_backward(back, gain, values, rms):
        scaled = back * gain
        inner = total_dp(jnp.sum(scaled * values, axis=-1), bits) / model_width
        return scaled - values * (rms * rms * inner)[..., None]

    grad_mlp_gain = lax.dynamic_slice_in_dim(
        jnp.sum(back_m * middle, axis=(0, 1, 2)), core * part, part, 0
    )
    grad_mlp_router = router_grad(scaled_m, router_rows_m)
    grad_middle = grad_out.astype(F32) + norm_backward(back_m, gain_m, middle, rms_m)

    grad_rows_a = dispatch(table_a, grad_middle.astype(BF16))
    grad_mix = scatter_halves("edrk,ekf->edrf", grad_rows_a, out_weight).astype(F32)
    grad_row_gates_a = jnp.sum(grad_mix * mixture.astype(F32), axis=-1)
    grad_mix = (grad_mix * row_gates_a[:, 0][..., None]).astype(BF16)
    grad_mix = grad_mix.reshape(-1, heads, HEAD_DIM)
    probs = jnp.exp(scores_of(flat_queries) - log_total)
    grad_values = dot32("hqk,qhd->khd", probs.astype(BF16), grad_mix)
    grad_probs = dot32("qhd,khd->hqk", grad_mix, values)
    grad_scores = probs * (grad_probs - jnp.sum(probs * grad_probs, axis=-1, keepdims=True))
    grad_scores = grad_scores.astype(BF16)
    grad_queries = dot32("hqk,khd->qhd", grad_scores, keys) * score_scale
    grad_keys = dot32("hqk,qhd->khd", grad_scores, flat_queries) * score_scale
    grad_queries = grad_queries.reshape(local_count, owners * capacity, features)
    grad_queries = (grad_queries * row_rms_a[..., None]).astype(BF16)
    grad_queries_all = gather_halves(grad_queries)

    grad_keys = grad_keys.reshape(owners, count, features)
    grad_values = grad_values.reshape(owners, count, features)
    keep = jnp.where(core == 0, grad_keys, grad_values)
    send = jnp.where(core == 0, grad_values, grad_keys).astype(BF16)
    grad_kv = keep + jnp.flip(swap(send, "expert", 1), axis=0).astype(F32)
    grad_kv = (grad_kv * seq_rms[..., None]).astype(BF16)
    grad_kv = jnp.stack(
        [gather_rows(grad_kv[0], 0, order_a), gather_rows(grad_kv[1], 0, order_b)], axis=1
    )
    other_kv = jnp.flip(swap(grad_kv, "expert", 1), axis=1)
    grad_kv = jnp.where(
        core == 0, jnp.stack([grad_kv, other_kv], 3), jnp.stack([other_kv, grad_kv], 3)
    )
    own_scaled = lax.dynamic_slice_in_dim(scaled_a, core * part, part, 3)
    grad_kv_weight = dot32("dbtk,dbtcf->kcf", own_scaled, grad_kv)
    kv_back = dot32("dbtcf,kcf->dbtk", grad_kv, kv_weight)

    router_rows_a, balance_a = router_part(
        grad_row_gates_a, table_a, gates_a, member_a, logits_a, rms_a
    )
    grad_in_rows = dot32("edrf,ekf->edrk", grad_queries_all, query_weight)
    back_a = combine(table_a, grad_in_rows.astype(BF16)) + jnp.einsum(
        "dbet,ke->dbtk", router_rows_a, router_a, precision=HIGHEST
    )
    nothing = jnp.zeros_like(kv_back)
    back_a = back_a + jnp.where(
        core == 0,
        jnp.concatenate([kv_back, nothing], axis=3),
        jnp.concatenate([nothing, kv_back], axis=3),
    )
    back_a = total_block(back_a.astype(BF16), shard_bits).astype(F32)
    grad_query_weight = dot32("edrk,edrf->ekf", rows_a, grad_queries_all)
    gated_rows_a = (grad_rows_a.astype(F32) * row_gates_a[..., None]).astype(BF16)
    grad_out_weight = dot32("edrk,edrf->ekf", gated_rows_a, mixture_all)
    own_inputs = inputs_f[:, 0]
    grad_att_gain = jnp.sum(back_a * own_inputs, axis=(0, 1))
    grad_att_gain = grad_att_gain + swap(grad_att_gain, "expert", 1)
    grad_att_gain = lax.dynamic_slice_in_dim(grad_att_gain, core * part, part, 0)
    grad_att_router = router_grad(scaled_a, router_rows_a)
    grad_block = grad_middle[:, 0] + norm_backward(back_a, gain_a, own_inputs, rms_a[:, 0])
    grad_tokens = place_columns(spread_columns([grad_block[d].astype(BF16) for d in range(groups)]))

    balance_terms = jnp.stack([balance_a, balance_m])
    aux_loss = (jnp.sum(balance_terms) / EXPERTS).reshape(1)
    return (
        layer_out,
        aux_loss,
        grad_tokens,
        grad_att_gain,
        grad_att_router,
        grad_kv_weight,
        grad_query_weight,
        grad_out_weight,
        grad_mlp_gain,
        grad_mlp_router,
        grad_gate_weight,
        grad_up_weight,
        grad_down_weight,
        balance_terms,
    )


def solution(mesh):
    rows = P(("dp", "expert"), None)
    vector = P(("dp", "expert"))
    shared = P(("dp", "expert"), None, "shard")
    weight = P("expert", "dp", "shard")
    return jax.shard_map(
        per_device,
        mesh=mesh,
        in_specs=(
            rows, vector, rows, shared, weight, weight, vector, rows,
            weight, weight, weight, rows, rows, rows,
        ),
        out_specs=(
            rows, P(), rows, vector, rows, shared, weight, weight,
            vector, rows, weight, weight, weight, P(),
        ),
        check_vma=False,
    )
```

```python
import jax
import jax.numpy as jnp
from jax import lax
from jax.experimental import pallas as pl
from jax.experimental.pallas import tpu as pltpu
from jax.sharding import PartitionSpec as P

HEAD_DIM = 128
EXPERTS = 8
TOPK = 2
EPSILON = 1e-06
AUX_WEIGHT = 0.01
MASKED = -1e30
HIGHEST = lax.Precision.HIGHEST
BF16 = jnp.bfloat16
F32 = jnp.float32
TOGETHER = 4


def dot32(spec, left, right):
    return jnp.einsum(spec, left, right, preferred_element_type=F32)


def swap(value, axis, flip):
    size = lax.axis_size(axis)
    return lax.ppermute(value, axis, [(i, i ^ flip) for i in range(size)])


def marker(*earlier):
    firsts = [value[(0,) * value.ndim].astype(F32) for value in earlier]
    return sum((first == jnp.inf).astype(jnp.int32) for first in firsts)


def late(value, *earlier):
    return value + marker(*earlier).astype(value.dtype)


def bits_in(size):
    count = 0
    while (1 << count) < size:
        count += 1
    return count


def split_bits(value, axis, bits):
    shape = value.shape
    return value.reshape(shape[:axis] + (2,) * bits + shape[axis + 1 :])


def join_bits(value, axis, bits):
    shape = value.shape
    return value.reshape(shape[:axis] + (1 << bits,) + shape[axis + bits :])


def gather_pieces(own, order):
    value, places = own[None], [0]
    for step, bit in enumerate(reversed(order)):
        received = swap(value, "dp", 1 << bit)
        others = [place | (1 << bit) for place in places]
        if step == len(order) - 1:
            return [(value, places), (received, others)]
        value, places = jnp.concatenate([value, received]), places + others
    return [(value, places)]


def gather_directly(own):
    groups = lax.axis_size("dp")
    return [(own[None], [0])] + [(swap(own, "dp", d)[None], [d]) for d in range(1, groups)]


def in_order(pieces):
    found = {}
    for array, places in pieces:
        for number, place in enumerate(places):
            found[place] = array[number]
    return jnp.stack([found[d] for d in range(len(found))])


def gather_rows(own, order):
    return in_order(gather_pieces(own, order))


def scatter_groups(order):
    places = range(1 << len(order))
    first = 1 << order[0]
    return [
        tuple(d for d in places if d & first),
        tuple(d for d in places if not d & first),
    ]


def scatter_terms(sent, kept, order, earlier=(), passed=None):
    bits = len(order)
    received = swap(sent, "dp", 1 << order[0])
    held = [bit for bit in range(bits - 1, -1, -1) if bit != order[0]]
    terms = [kept, received]
    for bit in order[1:]:
        parts = [split_bits(term, 0, len(held)) for term in terms]
        place = held.index(bit)
        parts = [jnp.moveaxis(term, place, 0) for term in parts]
        send = sum(term[1].astype(F32) for term in parts).astype(BF16)
        send = send.reshape((-1,) + kept.shape[1:])
        if passed is not None:
            passed.append(send)
        terms = [term[0].reshape(send.shape) for term in parts] if len(held) > 1 else terms
        terms = terms + [swap(send, "dp", 1 << bit)]
        held = [other for other in held if other != bit]
    return terms


def term_sum(terms):
    return sum(term[0].astype(F32) for term in terms)


def shard_part(value, axis):
    size = value.shape[axis] // lax.axis_size("shard")
    return lax.dynamic_slice_in_dim(value, lax.axis_index("shard") * size, size, axis)


def added(terms, earlier=()):
    shape = terms[0].shape
    if len(shape) == 3:
        steps, block = shape[0], (1,) + shape[1:]
    else:
        steps, block = max(1, shape[0] // 256), (min(256, shape[0]), shape[1])
    spec = pl.BlockSpec(block, lambda i: (i,) + (0,) * (len(shape) - 1))

    def kernel(*refs):
        total = refs[0][...].astype(F32)
        for more in refs[1 : len(terms)]:
            total = total + more[...].astype(F32)
        refs[-1][...] = total.astype(BF16)

    return pl.pallas_call(
        kernel,
        grid=(steps,),
        in_specs=[spec] * len(terms) + anywhere(earlier),
        out_specs=spec,
        out_shape=jax.ShapeDtypeStruct(shape, BF16),
        **params(terms[0].size * len(terms), 2 * terms[0].size * (len(terms) + 1), memory=8),
    )(*terms, *earlier)


def split_sum(one, two, shards, earlier=()):
    groups, count, width = one.shape
    size = count // shards
    whole = pl.BlockSpec((1, count, width), lambda i, _: (i, 0, 0))

    def kernel(index_ref, one_ref, two_ref, *refs):
        for number, out in enumerate(refs[len(earlier) :]):
            place = pl.ds(pl.multiple_of((index_ref[0] ^ number) * size, size), size)
            total = one_ref[0, place, :].astype(F32) + two_ref[0, place, :].astype(F32)
            out[0] = total.astype(BF16)

    return pl.pallas_call(
        kernel,
        grid_spec=pltpu.PrefetchScalarGridSpec(
            num_scalar_prefetch=1,
            grid=(groups,),
            in_specs=[whole] * 2 + anywhere(earlier),
            out_specs=[pl.BlockSpec((1, size, width), lambda i, _: (i, 0, 0))] * shards,
        ),
        out_shape=[jax.ShapeDtypeStruct((groups, size, width), BF16)] * shards,
        **params(one.size, 6 * one.size, memory=8),
    )(lax.axis_index("shard").reshape(1), one, two, *earlier)


def joined(parts, kind, earlier=()):
    groups, size, width = parts[0].shape
    shards = len(parts)

    def kernel(index_ref, *refs):
        out = refs[-1]
        for number in range(shards):
            place = pl.ds(pl.multiple_of((index_ref[0] ^ number) * size, size), size)
            out[0, place, :] = refs[number][0].astype(kind)

    return pl.pallas_call(
        kernel,
        grid_spec=pltpu.PrefetchScalarGridSpec(
            num_scalar_prefetch=1,
            grid=(groups,),
            in_specs=[pl.BlockSpec((1, size, width), lambda i, _: (i, 0, 0))] * shards + anywhere(earlier),
            out_specs=pl.BlockSpec((1, size * shards, width), lambda i, _: (i, 0, 0)),
        ),
        out_shape=jax.ShapeDtypeStruct((groups, size * shards, width), kind),
        **params(0, 8 * parts[0].size * shards, memory=16),
    )(lax.axis_index("shard").reshape(1), *parts, *earlier)


def stacked(arrays, earlier=()):
    rows, width = arrays[0].shape

    def kernel(*refs):
        for number in range(len(arrays)):
            refs[-1][number * rows : (number + 1) * rows] = refs[number][...]

    return pl.pallas_call(
        kernel,
        in_specs=[pl.BlockSpec(memory_space=pltpu.VMEM)] * len(arrays) + anywhere(earlier),
        out_specs=pl.BlockSpec(memory_space=pltpu.VMEM),
        out_shape=jax.ShapeDtypeStruct((rows * len(arrays), width), arrays[0].dtype),
        **params(0, 4 * arrays[0].size * len(arrays), memory=16),
    )(*arrays, *earlier)


def shard_scatter(parts, pin=None):
    far = swap(parts[3], "shard", 1)
    near = swap(parts[1], "shard", 1)
    side = swap(parts[2] + far, "shard", 2)
    return added([parts[0], near, side], [] if pin is None else pin(parts[0]))


def shard_gather(own, kind=BF16, pin=None):
    count = own.shape[0]
    both = jnp.concatenate([own, swap(own, "shard", 2)])
    more = swap(both, "shard", 1)
    parts = [both[:count], more[:count], both[count:], more[count:]]
    return joined(parts, kind, [] if pin is None else pin(own))


def core_sum(pair, shards, earlier=()):
    return split_sum(pair[0], swap(pair[1], "expert", 1), shards, earlier)


def total_pair(partial_pair, shards, scatter_pin=None, gather_pin=None, earlier=()):
    own = shard_scatter(core_sum(partial_pair, shards, earlier), scatter_pin)
    whole = shard_gather(own, BF16, gather_pin)
    return (whole, swap(whole, "expert", 1))


def total_small(value, block_axis, bits):
    received = swap(value, "expert", 1)
    if block_axis is not None:
        received = jnp.flip(received, axis=block_axis)
    value = value + received
    for bit in range(bits):
        value = value + swap(value, "shard", 1 << bit)
    return value


def both_blocks(own, axis):
    return jnp.stack([own, swap(own, "expert", 1)], axis=axis)


def spread_columns(pieces):
    return [pieces[0]] + [swap(pieces[d], "dp", d) for d in range(1, len(pieces))]


def place_columns(pieces):
    rows, width = pieces[0].shape

    def kernel(index_ref, *refs):
        for number in range(len(pieces)):
            place = pl.ds(pl.multiple_of((index_ref[0] ^ number) * width, 128), width)
            refs[-1][0, :, place] = refs[number][...]

    shape = (1, rows, width * len(pieces))
    return pl.pallas_call(
        kernel,
        grid_spec=pltpu.PrefetchScalarGridSpec(
            num_scalar_prefetch=1,
            grid=(1,),
            in_specs=[pl.BlockSpec((rows, width), lambda *_: (0, 0))] * len(pieces),
            out_specs=pl.BlockSpec(shape, lambda *_: (0, 0, 0)),
        ),
        out_shape=jax.ShapeDtypeStruct(shape, BF16),
        **params(0, 4 * rows * width * len(pieces), memory=8),
    )(lax.axis_index("dp").reshape(1), *pieces)


def product(left, right, dims=((1,), (0,))):
    return lax.dot_general(left, right, (dims, ((), ())), preferred_element_type=F32)


def window_of(bounds_ref, sequence, group, rows, window):
    low = bounds_ref[sequence, 2 * group]
    high = bounds_ref[sequence, 2 * group + 1]
    base = pl.multiple_of(jnp.minimum(jnp.bitwise_and(low, -16), rows - window), 16)
    at = base + lax.broadcasted_iota(jnp.int32, (window, 1), 0)
    return (base, (at >= low) & (at < high))


def whole_block(array):
    zeros = (0,) * len(array.shape)
    return pl.BlockSpec(array.shape, lambda *_: zeros, pipeline_mode=pl.Buffered(1))


def anywhere(arrays):
    return [pl.BlockSpec(memory_space=pl.ANY) for _ in arrays]


def params(flops, moved, exps=0, memory=24):
    return dict(
        compiler_params=pltpu.CompilerParams(vmem_limit_bytes=memory << 20),
        cost_estimate=pl.CostEstimate(flops=flops, bytes_accessed=moved, transcendentals=exps),
    )


def group_specs(pair):
    own, other = pair
    last = own.shape[0] - 1
    return [
        pl.BlockSpec((1,) + own.shape[1:], lambda g, *_: (jnp.minimum(g, last), 0, 0)),
        whole_block(other),
    ]


def each_group(groups, windows, step):
    group = pl.program_id(0)

    @pl.when(group < groups - 1)
    def _():
        step(group, windows[0], 0)

    @pl.when(group == groups - 1)
    def _():
        step(group, windows[1], 1)


def chosen_rows(ref, index, base, window, mine, scale=None):
    rows = ref[index, pl.ds(base, window), :]
    keep = jnp.where(mine, 1.0, 0.0)
    if scale is None:
        return rows * keep.astype(BF16)
    return (rows.astype(F32) * (scale[index, pl.ds(base, window), :] * keep)).astype(BF16)


def expert_product(rows, pair, bounds, cuts, windows, earlier=(), first=0):
    sequences = sorted(d for group in cuts[0][1] for d in group)
    if len(sequences) > TOGETHER:
        found = [{} for _ in cuts]
        for at in range(0, len(sequences), TOGETHER):
            some = sequences[at : at + TOGETHER]
            split = [(size, [(d,) for d in some]) for size, _ in cuts]
            parts = expert_product(rows, pair, bounds, split, windows, earlier, first)
            for place, part in zip(found, parts):
                place.update({d: one[0] for d, one in zip(some, part)})
        return [
            [jnp.stack([place[d] for d in group]) for group in wanted]
            for place, (_, wanted) in zip(found, cuts)
        ]
    count, depth = rows.shape[1:]
    groups, width = pair[0].shape[0] + 1, sum(size for size, _ in cuts)
    amount = len(sequences)

    def kernel(bounds_ref, rows_ref, *refs):
        weights, outs = refs[:2], refs[2 + len(earlier) :]

        @pl.when(pl.program_id(0) == 0)
        def _():
            for out in outs:
                out[...] = jnp.zeros_like(out)

        def step(group, window, which):
            bases, picked = [], []
            for sequence in sequences:
                base, mine = window_of(bounds_ref, sequence, group, count, window)
                bases.append(base)
                picked.append(chosen_rows(rows_ref, sequence, base, window, mine))
            left = jnp.concatenate(picked, axis=0)
            start = first
            number = 0
            for size, wanted in cuts:
                part = product(left, weights[which][0, :, start : start + size]).astype(BF16)
                for some in wanted:
                    for index, sequence in enumerate(some):
                        place = sequences.index(sequence)
                        at = (index, pl.ds(bases[place], window), slice(None))
                        outs[number][at] = (
                            outs[number][at] + part[place * window : (place + 1) * window]
                        )
                    number += 1
                start += size

        each_group(groups, windows, step)

    shapes = [
        jax.ShapeDtypeStruct((len(some), count, size), BF16) for size, wanted in cuts for some in wanted
    ]
    outs = pl.pallas_call(
        kernel,
        grid_spec=pltpu.PrefetchScalarGridSpec(
            num_scalar_prefetch=1,
            grid=(groups,),
            in_specs=[whole_block(rows)] + group_specs(pair) + anywhere(earlier),
            out_specs=[whole_block(shape) for shape in shapes],
        ),
        out_shape=shapes,
        **params(
            2 * amount * groups * windows[0] * depth * width,
            2 * (pair[0].size + pair[1].size + amount * count * (depth + width)),
        ),
    )(bounds, rows, *pair, *earlier)
    outs = list(outs)
    return [[outs.pop(0) for _ in wanted] for _, wanted in cuts]


def pieces_at(pieces, sequences):
    if len(sequences) == sum(len(places) for _, places in pieces):
        return pieces
    whole = in_order(pieces)
    return [(whole[sequences[0] : sequences[-1] + 1], sequences)]


def flat_pieces(pieces, arrays, specs):
    found = {}
    for array, places in pieces:
        for number, place in enumerate(places):
            found[place] = (len(arrays), number)
        arrays.append(array)
        specs.append(whole_block(array))
    return found


def expert_product_back(parts, bounds, sequences, windows, carry=None, ending=None, earlier=()):
    total_count = len(sequences)
    if total_count > TOGETHER:
        done = []
        for at in range(0, total_count, TOGETHER):
            some = sequences[at : at + TOGETHER]
            cut = slice(at, at + TOGETHER)
            some_parts = [(pieces_at(pieces, some), pair, start) for pieces, pair, start in parts]
            some_ending = None
            if ending is not None:
                slots, gates, router, extra = ending
                some_ending = (
                    slots[cut],
                    None if gates is None else gates[cut],
                    None if router is None else (router[0][cut], router[1]),
                    None if extra is None else tuple(one[cut] for one in extra),
                )
            renamed = [
                ([(array, list(range(len(places)))) for array, places in pieces], pair, start)
                for pieces, pair, start in some_parts
            ]
            done.append(
                expert_product_back(
                    renamed,
                    bounds[cut],
                    list(range(len(some))),
                    windows,
                    None if carry is None else carry[cut],
                    some_ending,
                    earlier,
                )
            )
        if ending is None:
            return jnp.concatenate(done)
        return tuple(jnp.concatenate(one) for one in zip(*done))

    own = parts[0][1][0]
    groups, depth = own.shape[0] + 1, own.shape[1]
    count = parts[0][0][0][0].shape[1]
    arrays, specs, plan, held = [], [], [], {}
    flops, moved = 0, 4 * total_count * count * depth
    for pieces, pair, start in parts:
        if id(pair) not in held:
            held[id(pair)] = len(arrays)
            arrays += list(pair)
            specs += group_specs(pair)
            moved += 2 * (pair[0].size + pair[1].size)
        size = pieces[0][0].shape[2]
        plan.append((flat_pieces(pieces, arrays, specs), held[id(pair)], start, size))
        flops += 2 * total_count * groups * windows[0] * size * depth
        moved += 2 * total_count * count * size
    places = {}

    def operand(name, array):
        places[name] = len(arrays)
        arrays.append(array)
        specs.append(whole_block(array))

    if carry is not None:
        operand("carry", carry)
    if ending is not None:
        slots, gates, router, extra = ending
        operand("slots", slots)
        if gates is not None:
            operand("gates", gates)
        if router is not None:
            operand("router_rows", router[0])
            operand("router", router[1])
        if extra is not None:
            operand("extra0", extra[0])
            operand("extra1", extra[1])
    arrays += list(earlier)
    specs += anywhere(earlier)

    def kernel(bounds_ref, *refs):
        ins, outs = refs[: len(arrays)], refs[len(arrays) :]
        total = outs[-1]

        def step(group, window, which):
            bases, masks, sums = [], [], None
            for sequence in sequences:
                base, mine = window_of(bounds_ref, sequence, group, count, window)
                bases.append(base)
                masks.append(mine)
            for found, weight_at, start, size in plan:
                left = jnp.concatenate(
                    [
                        ins[found[sequence][0]][found[sequence][1], pl.ds(base, window), :]
                        for sequence, base in zip(sequences, bases)
                    ],
                    axis=0,
                )
                weight = ins[weight_at + which][0, :, start : start + size]
                part = product(left, weight, ((1,), (1,)))
                sums = part if sums is None else sums + part
            for number, (base, mine) in enumerate(zip(bases, masks)):
                place = (number, pl.ds(base, window), slice(None))
                part = sums[number * window : (number + 1) * window]
                total[place] = jnp.where(mine, part, total[place])

        each_group(groups, windows, step)

        @pl.when(pl.program_id(0) == groups - 1)
        def _():
            if ending is None:
                if carry is not None:
                    total[...] += ins[places["carry"]][...]
                return
            tokens = outs[0].shape[1]
            for number in range(total_count):
                rows = total[number]
                if carry is not None:
                    rows = rows + ins[places["carry"]][number]
                if gates is not None:
                    rows = rows * ins[places["gates"]][number]
                rows = rows.astype(BF16)
                for block in range(2):
                    numbers = lax.broadcasted_iota(jnp.int32, (tokens, count), 1)
                    hit = None
                    for choice in range(TOPK):
                        column = ins[places["slots"]][
                            number, block * tokens : (block + 1) * tokens, choice : choice + 1
                        ]
                        one = column == numbers
                        hit = one if hit is None else hit | one
                    value = product(jnp.where(hit, 1.0, 0.0).astype(BF16), rows)
                    if router is not None:
                        value = value + product(
                            ins[places["router_rows"]][number, block].astype(BF16),
                            ins[places["router"]][...].astype(BF16),
                            ((0,), (0,)),
                        )
                    if extra is not None:
                        value = value + ins[places["extra%d" % block]][number].astype(F32)
                    outs[block][number] = value.astype(BF16)

    if ending is None:
        out_specs = [whole_block(jax.ShapeDtypeStruct((total_count, count, depth), F32))]
        out_shape = [jax.ShapeDtypeStruct((total_count, count, depth), F32)]
        scratch = []
    else:
        tokens = ending[0].shape[1] // 2
        out_shape = [jax.ShapeDtypeStruct((total_count, tokens, depth), BF16)] * 2
        out_specs = [whole_block(one) for one in out_shape]
        scratch = [pltpu.VMEM((total_count, count, depth), F32)]
    result = pl.pallas_call(
        kernel,
        grid_spec=pltpu.PrefetchScalarGridSpec(
            num_scalar_prefetch=1,
            grid=(groups,),
            in_specs=specs,
            out_specs=out_specs,
            scratch_shapes=scratch,
        ),
        out_shape=out_shape,
        **params(flops, moved, memory=36),
    )(bounds, *arrays)
    return result[0] if ending is None else tuple(result)


def expert_grads(rows, parts, bounds, sequences, local_count, windows, scale=None, earlier=()):
    if len(sequences) > TOGETHER:
        done = []
        for at in range(0, len(sequences), TOGETHER):
            some = sequences[at : at + TOGETHER]
            cut = slice(at, at + TOGETHER)
            renamed = [
                [(array, list(range(len(some)))) for array, _ in pieces_at(pieces, some)]
                for pieces in parts
            ]
            done.append(
                expert_grads(
                    rows[cut], renamed, bounds[cut], list(range(len(some))), local_count, windows,
                    None if scale is None else scale[cut], earlier,
                )
            )
        return tuple(sum(one[1:], one[0]) for one in zip(*done))
    amount = len(sequences)
    count, depth = rows.shape[1:]
    sizes = [pieces[0][0].shape[2] for pieces in parts]
    width = sum(sizes)
    groups = local_count + 1
    arrays, specs = [rows], [whole_block(rows)]
    if scale is not None:
        arrays.append(scale)
        specs.append(whole_block(scale))
    plan = [flat_pieces(pieces, arrays, specs) for pieces in parts]
    arrays += list(earlier)
    specs += anywhere(earlier)

    def kernel(bounds_ref, *refs):
        ins, outs = refs[: len(arrays)], refs[len(arrays) :]

        def step(group, window, which):
            bases, picked = [], []
            for sequence in sequences:
                base, mine = window_of(bounds_ref, sequence, group, count, window)
                bases.append(base)
                picked.append(
                    chosen_rows(ins[0], sequence, base, window, mine, None if scale is None else ins[1])
                )
            left = jnp.concatenate(picked, axis=0)
            start = 0
            for found, size in zip(plan, sizes):
                right = jnp.concatenate(
                    [
                        ins[found[sequence][0]][found[sequence][1], pl.ds(base, window), :]
                        for sequence, base in zip(sequences, bases)
                    ],
                    axis=0,
                )
                part = product(left, right, ((0,), (0,)))
                outs[which][0, :, start : start + size] = part.astype(outs[which].dtype)
                start += size

        each_group(groups, windows, step)

    return pl.pallas_call(
        kernel,
        grid_spec=pltpu.PrefetchScalarGridSpec(
            num_scalar_prefetch=1,
            grid=(groups,),
            in_specs=specs,
            out_specs=[
                pl.BlockSpec((1, depth, width), lambda g, *_: (jnp.minimum(g, local_count - 1), 0, 0)),
                whole_block(jax.ShapeDtypeStruct((1, depth, width), BF16)),
            ],
        ),
        out_shape=[
            jax.ShapeDtypeStruct((local_count, depth, width), F32),
            jax.ShapeDtypeStruct((1, depth, width), BF16),
        ],
        **params(
            2 * amount * groups * windows[0] * depth * width,
            2 * amount * count * (depth + width) + 4 * groups * depth * width,
            memory=32,
        ),
    )(bounds, *arrays)


def add_at(array, more, index, earlier=()):
    _, depth, width = array.shape
    step = depth // 4 if depth % 64 == 0 else depth
    spec = pl.BlockSpec((1, step, width), lambda i, at: (at[0], i, 0))

    def kernel(index_ref, array_ref, more_ref, *refs):
        refs[-1][...] = array_ref[...] + more_ref[...].astype(F32)

    return pl.pallas_call(
        kernel,
        grid_spec=pltpu.PrefetchScalarGridSpec(
            num_scalar_prefetch=1,
            grid=(depth // step,),
            in_specs=[spec, pl.BlockSpec((1, step, width), lambda i, _: (0, i, 0))] + anywhere(earlier),
            out_specs=spec,
        ),
        out_shape=jax.ShapeDtypeStruct(array.shape, F32),
        input_output_aliases={1: 0},
        **params(depth * width, 10 * depth * width, memory=12),
    )(index.reshape(1), array, more, *earlier)


def slot_hits(slots_ref, number, block, tokens, rows):
    numbers = lax.broadcasted_iota(jnp.int32, (rows, tokens), 0)
    hit = None
    for choice in range(TOPK):
        line = slots_ref[number, choice : choice + 1, block * tokens : (block + 1) * tokens]
        one = line == numbers
        hit = one if hit is None else hit | one
    return jnp.where(hit, 1.0, 0.0).astype(BF16)


def dispatch(slots, rows, pairs, vectors, columns, function, earlier=()):
    groups, tokens, width = pairs[0][0].shape
    arrays = [slots]
    specs = [pl.BlockSpec((1,) + slots.shape[1:], lambda i: (i, 0, 0))]
    for pair in pairs:
        arrays += list(pair)
        specs += [pl.BlockSpec((1, tokens, width), lambda i: (i, 0, 0))] * 2
    for pair in columns:
        arrays += list(pair)
        specs += [pl.BlockSpec((1, tokens, 1), lambda i: (i, 0, 0))] * 2
    arrays += list(vectors)
    specs += [whole_block(vector) for vector in vectors]
    arrays += list(earlier)
    specs += anywhere(earlier)

    def kernel(slots_ref, *refs):
        out = refs[-1]
        total = None
        for block in range(2):
            at = 0
            values, sides = [], []
            for _ in pairs:
                values.append(refs[at + block][0].astype(F32))
                at += 2
            for _ in columns:
                sides.append(refs[at + block][0])
                at += 2
            lines = [refs[at + number][...] for number in range(len(vectors))]
            value = function(values, lines, sides).astype(BF16)
            part = product(slot_hits(slots_ref, 0, block, tokens, rows), value)
            total = part if total is None else total + part
        out[0] = total.astype(BF16)

    return pl.pallas_call(
        kernel,
        grid=(groups,),
        in_specs=specs,
        out_specs=pl.BlockSpec((1, rows, width), lambda i: (i, 0, 0)),
        out_shape=jax.ShapeDtypeStruct((groups, rows, width), BF16),
        **params(4 * groups * rows * tokens * width, 2 * groups * width * (rows + 2 * tokens * len(pairs))),
    )(*arrays)


def unit_rows(gate_terms, up_terms, grad_terms, scale, gates, earlier=()):
    count, width = gate_terms[0].shape[1:]
    step = min(count, 128)
    tile = pl.BlockSpec((step, width), lambda i: (i, 0))
    term = pl.BlockSpec((None, step, width), lambda i: (0, i, 0))
    column = pl.BlockSpec((step, 1), lambda i: (i, 0))
    lists = (gate_terms, up_terms, grad_terms)
    amount = sum(len(terms) for terms in lists)

    def kernel(*refs):
        scale_ref, gates_ref = refs[amount : amount + 2]
        active_out, gating_out, upward_out, dots_out, norms_out = refs[-5:]
        sums, at = [], 0
        for terms in lists:
            total = refs[at][...].astype(F32)
            for more in refs[at + 1 : at + len(terms)]:
                total = total + more[...].astype(F32)
            sums.append(total)
            at += len(terms)
        scale_rows = scale_ref[...]
        gating, upward, grad = sums[0] * scale_rows, sums[1] * scale_rows, sums[2]
        sigma = 1.0 / (1.0 + jnp.exp(-gating))
        silu = gating * sigma
        active = silu * upward
        active_out[...] = active.astype(BF16)
        dots_out[...] = jnp.sum(grad * active, axis=1, keepdims=True)
        grad = grad * gates_ref[...]
        grad_gating = grad * upward * sigma * (1.0 + gating * (1.0 - sigma))
        grad_upward = grad * silu
        norms_out[...] = jnp.sum(grad_gating * gating + grad_upward * upward, axis=1, keepdims=True)
        gating_out[...] = (grad_gating * scale_rows).astype(BF16)
        upward_out[...] = (grad_upward * scale_rows).astype(BF16)

    return pl.pallas_call(
        kernel,
        grid=(count // step,),
        in_specs=[term] * amount + [column] * 2 + anywhere(earlier),
        out_specs=[tile] * 3 + [column] * 2,
        out_shape=[jax.ShapeDtypeStruct((count, width), BF16)] * 3
        + [jax.ShapeDtypeStruct((count, 1), F32)] * 2,
        **params(20 * count * width, 18 * count * width, count * width),
    )(*gate_terms, *up_terms, *grad_terms, scale, gates, *earlier)


def router_statistics(pairs, gain, router, earlier=()):
    groups, tokens, width = pairs[0][0].shape
    rows = 2 * EXPERTS
    block = pl.BlockSpec((1, tokens, width), lambda i: (i, 0, 0))
    amount = 2 * len(pairs)

    def kernel(*refs):
        gain_ref, router_ref, out = refs[amount], refs[amount + 1], refs[-1]
        for number in range(2):
            value = refs[number][0].astype(F32)
            for more in range(1, len(pairs)):
                value = value + refs[2 * more + number][0].astype(F32)
            scaled = (value * gain_ref[...]).astype(BF16)
            out[0, number, :EXPERTS] = product(router_ref[...].astype(BF16), scaled, ((1,), (1,)))
            out[0, number, EXPERTS:] = lax.dot_general(
                jnp.ones((EXPERTS, width), F32),
                value * value,
                (((1,), (1,)), ((), ())),
                precision=HIGHEST,
                preferred_element_type=F32,
            )

    return pl.pallas_call(
        kernel,
        grid=(groups,),
        in_specs=[block] * amount + [whole_block(gain), whole_block(router)] + anywhere(earlier),
        out_specs=pl.BlockSpec((1, 2, rows, tokens), lambda i: (i, 0, 0, 0)),
        out_shape=jax.ShapeDtypeStruct((groups, 2, rows, tokens), F32),
        **params(8 * rows * groups * tokens * width, 2 * amount * groups * tokens * width, memory=12),
    )(*(one for pair in pairs for one in pair), gain, router, *earlier)


def softmax_rows(queries, keys, row_pos, key_pos):
    scores = product(queries, keys, ((1,), (1,))) * HEAD_DIM ** (-0.5)
    scores = jnp.where(key_pos <= row_pos, scores, MASKED)
    expo = jnp.exp(scores - jnp.max(scores, axis=1, keepdims=True))
    return expo / jnp.sum(expo, axis=1, keepdims=True)


def attention_calls(count, length, features):
    heads = features // HEAD_DIM
    rows = pl.BlockSpec((count, HEAD_DIM), lambda h: (0, h))
    places = pl.BlockSpec((length, HEAD_DIM), lambda h: (0, h))
    column = pl.BlockSpec((count, 1), lambda h: (0, 0))
    line = pl.BlockSpec((1, length), lambda h: (0, 0))

    def forward_kernel(queries, keys, values, row_pos, key_pos, *refs):
        probs = softmax_rows(queries[...], keys[...], row_pos[...], key_pos[...])
        refs[-1][...] = product(probs.astype(BF16), values[...]).astype(BF16)

    def forward(*arrays, earlier=()):
        return pl.pallas_call(
            forward_kernel,
            grid=(heads,),
            in_specs=[rows, places, places, column, line] + anywhere(earlier),
            out_specs=rows,
            out_shape=jax.ShapeDtypeStruct((count, features), BF16),
            **params(4 * count * length * features, 8 * count * features, heads * count * length),
        )(*arrays, *earlier)

    def backward_kernel(
        queries, keys, values, row_pos, key_pos, mixture, grad_mix, gates, scale, *refs
    ):
        grad_queries, grad_keys, grad_values, grad_gates, norms = refs[-5:]
        probs = softmax_rows(queries[...], keys[...], row_pos[...], key_pos[...])
        grad_raw = grad_mix[...].astype(F32)
        gate_part = jnp.sum(grad_raw * mixture[...].astype(F32), axis=1, keepdims=True)
        grad_out = (grad_raw * gates[...]).astype(BF16)
        grad_values[...] = product(probs.astype(BF16), grad_out, ((0,), (0,)))
        grad_probs = product(grad_out, values[...], ((1,), (1,)))
        inner = jnp.sum(probs * grad_probs, axis=1, keepdims=True)
        grad_scores = (probs * (grad_probs - inner)).astype(BF16)
        grad_keys[...] = product(grad_scores, queries[...], ((0,), (0,))) * HEAD_DIM ** (-0.5)
        grad = product(grad_scores, keys[...]) * HEAD_DIM ** (-0.5)
        norm_part = jnp.sum(grad * queries[...].astype(F32), axis=1, keepdims=True)
        grad_queries[...] = (grad * scale[...]).astype(BF16)

        @pl.when(pl.program_id(0) == 0)
        def _():
            grad_gates[...] = gate_part
            norms[...] = norm_part

        @pl.when(pl.program_id(0) > 0)
        def _():
            grad_gates[...] += gate_part
            norms[...] += norm_part

    def backward(*arrays, earlier=()):
        return pl.pallas_call(
            backward_kernel,
            grid=(heads,),
            in_specs=[rows, places, places, column, line, rows, rows, column, column]
            + anywhere(earlier),
            out_specs=[rows, places, places, column, column],
            out_shape=[
                jax.ShapeDtypeStruct((count, features), BF16),
                jax.ShapeDtypeStruct((length, features), F32),
                jax.ShapeDtypeStruct((length, features), F32),
                jax.ShapeDtypeStruct((count, 1), F32),
                jax.ShapeDtypeStruct((count, 1), F32),
            ],
            **params(10 * count * length * features, 20 * count * features, heads * count * length),
        )(*arrays, *earlier)

    return forward, backward


def route_tables(routes, core, local_count, half):
    sequences, blocks, _, count = routes.shape
    experts = jnp.arange(EXPERTS, dtype=jnp.int32)[:, None]
    named = [routes[:, :, choice : choice + 1] == experts for choice in range(TOPK)]
    member = named[0]
    for more in named[1:]:
        member = member | more
    steps = jnp.arange(count, dtype=jnp.int32)
    before = (steps[:, None] < steps[None, :]).astype(BF16)
    ranks = dot32("dbet,tu->dbeu", member.astype(BF16), before)
    counts = jnp.sum(member.astype(F32), axis=3)
    first_counts = jnp.where(core == 0, counts[:, 0], counts[:, 1])[:, None, :]
    second = ((core ^ jnp.arange(blocks, dtype=jnp.int32)) == 1).astype(F32)[None, :, None]
    totals = counts[:, 0] + counts[:, 1]
    smaller = (experts > experts[:, 0][None, :]).astype(F32)
    starts = jnp.sum(totals[:, None, :] * smaller, axis=2) - (core * half).astype(F32)
    places = ranks + (starts[:, None, :] + second * first_counts)[..., None]
    slots = [jnp.sum(jnp.where(one, places, 0.0), axis=2) for one in named]
    slots = jnp.stack(slots, axis=1).astype(jnp.int32).reshape(sequences, TOPK, blocks * count)
    low = jnp.clip(starts, 0, half)
    high = jnp.clip(starts + totals, 0, half)
    limits = jnp.stack([low, high], axis=2).astype(jnp.int32)
    own = lax.dynamic_slice_in_dim(limits, core * local_count, local_count, 1)
    other = lax.dynamic_slice_in_dim(
        limits, jnp.where(core == 0, local_count, local_count - 1), 1, 1
    )
    bounds = jnp.concatenate([own, other], axis=1).reshape(sequences, 2 * (local_count + 1))
    return (slots, bounds, named, jnp.sum(totals, axis=0))


def hits(slots, half):
    numbers = jnp.arange(half, dtype=jnp.int32)[:, None]
    return [slots[:, choice : choice + 1] == numbers for choice in range(TOPK)]


def choice_rows(slots, half, values):
    total = 0.0
    for choice, hit in enumerate(hits(slots, half)):
        total = total + jnp.sum(jnp.where(hit, values[:, choice : choice + 1], 0.0), axis=2)
    return total


def choice_gates(logits, named):
    picked = [jnp.sum(jnp.where(one, logits, 0.0), axis=2) for one in named]
    return jax.nn.softmax(jnp.stack(picked, axis=1), axis=1)


def per_device(
    tokens,
    att_gain,
    att_router,
    kv_weight,
    query_weight,
    out_weight,
    mlp_gain,
    mlp_router,
    gate_weight,
    up_weight,
    down_weight,
    att_routes,
    mlp_routes,
    cotangent,
):
    owners = lax.axis_size("expert")
    groups = lax.axis_size("dp")
    shards = lax.axis_size("shard")
    bits = bits_in(groups)
    shard_bits = bits_in(shards)
    local_count = EXPERTS // owners
    count, model_width = tokens.shape
    width = model_width // groups
    part = width // owners
    capacity = 5 * count * TOPK // (4 * EXPERTS)
    half = count * TOPK
    length = owners * count
    windows = [
        min(half, (most + 30) // 16 * 16)
        for most in (owners * capacity, owners * local_count * capacity - half)
    ]
    all_tokens = count * owners * groups
    features = query_weight.shape[2]
    units = gate_weight.shape[2]
    me = lax.axis_index("dp")
    core = lax.axis_index("expert")
    order_a = list(range(bits))
    order_b = order_a[bits // 2 :] + order_a[: bits // 2]
    orders = (order_a, order_b)
    everything = list(range(groups))

    def halves_of(size):
        first = (size // 128 + 1) // 2 * 128 if size >= 256 else size // 2
        return [first, size - first]

    feature_cuts, unit_cuts = halves_of(features), halves_of(units)

    def columns(value, shift=0):
        return [
            lax.dynamic_slice_in_dim(value, (me ^ d) * width + shift, width, 1) for d in range(groups)
        ]

    def core_order(own, other, axis=0):
        return jnp.where(
            core == 0,
            jnp.concatenate([own, other], axis=axis),
            jnp.concatenate([other, own], axis=axis),
        )

    routes = jnp.stack(
        [att_routes[:, 0], att_routes[:, 1], mlp_routes[:, 0], mlp_routes[:, 1]]
    )
    routes = gather_rows(both_blocks(routes, 0), order_a)
    inputs = jnp.stack(spread_columns(columns(tokens)))
    inputs = (inputs, swap(inputs, "expert", 1))
    small = jnp.concatenate(
        [att_gain[:, None], mlp_gain[:, None], att_router, mlp_router], axis=1
    )
    small = core_order(small, swap(small, "expert", 1)).astype(F32)
    gain_a, gain_m = small[:, 0][None, :], small[:, 1][None, :]
    router_a, router_m = small[:, 2 : 2 + EXPERTS].T, small[:, 2 + EXPERTS :].T
    slots_a, bounds_a, named_a, totals_a = route_tables(
        routes[:, :, :TOPK], core, local_count, half
    )
    slots_m, bounds_m, named_m, totals_m = route_tables(
        routes[:, :, TOPK:], core, local_count, half
    )

    columns_a, columns_m = jnp.swapaxes(slots_a, 1, 2), jnp.swapaxes(slots_m, 1, 2)

    def with_other(weight, shift=0):
        mine = lax.dynamic_slice_in_dim(weight, (1 - core) * (local_count - 1) + shift, 1, 0)
        return (weight, swap(mine, "expert", 1))

    grad_out = jnp.stack(spread_columns(columns(cotangent, marker(inputs[0]))))
    grad_out = (grad_out, swap(grad_out, "expert", 1))
    plain_values = lambda values, lines, sides: values[0]
    query_pair = with_other(query_weight)
    scaled_values = lambda values, lines, sides: values[0] * lines[0]
    rows_a = dispatch(slots_a, half, [inputs], [gain_a], [], scaled_values)
    group_lists = [scatter_groups(order) for order in orders]
    feature_plan = list(zip(feature_cuts, group_lists))
    unit_plan = list(zip(unit_cuts, group_lists))
    query_parts = expert_product(rows_a, query_pair, bounds_a, feature_plan, windows)
    query_there = query_parts[0][0]

    scaled_kv = kv_weight.astype(F32) * lax.dynamic_slice_in_dim(gain_a[0], core * part, part)[:, None, None]
    scaled_kv = scaled_kv.astype(BF16)
    own_float = tokens.astype(F32)
    own_rms = lax.rsqrt(jnp.mean(own_float * own_float, axis=1) + EPSILON)
    block_tokens = [
        jnp.concatenate(
            [
                lax.dynamic_slice_in_dim(tokens, ((me ^ d) * owners + (core ^ b)) * part, part, 1)
                for d in everything
            ],
            axis=1,
        )
        for b in range(owners)
    ]
    key_value, kv_all = [], []
    for c, order in enumerate(orders):
        found = {}
        for array, places in gather_pieces(scaled_kv[:, c], order):
            for number, place in enumerate(places):
                found[place] = array[number]
        own = stacked([found[d] for d in everything], [query_there])
        kv_all.append((own, swap(own, "expert", 1)))
        total = sum(
            dot32("tk,kf->tf", some, weight) for some, weight in zip(block_tokens, kv_all[-1])
        )
        total = (total * own_rms[:, None]).astype(BF16)
        key_value.append(jnp.concatenate([total, swap(total, "expert", 1)]))
    keys, values = key_value
    seq_rms = both_blocks(own_rms, 0)

    def own_rows(slots, token_values):
        wide = jnp.broadcast_to(token_values.reshape(1, 1, length), (1, TOPK, length))
        return choice_rows(slots[:1], half, wide)[0][:, None]

    row_rms_a = own_rows(slots_a, seq_rms)
    token_pos = (
        jnp.arange(count, dtype=jnp.int32)[None, :]
        + ((core ^ jnp.arange(owners, dtype=jnp.int32)) * count)[:, None]
    ).astype(F32)
    row_pos = own_rows(slots_a, token_pos)
    key_pos = token_pos.reshape(1, length)

    def gather_cuts(value, cuts):
        return [
            gather_pieces(value[:, : cuts[0]], order_a),
            gather_pieces(value[:, cuts[0] :], order_b),
        ]

    queries = jnp.concatenate(
        [
            term_sum(scatter_terms(*parts, order)) for parts, order in zip(query_parts, orders)
        ],
        axis=1,
    )
    queries = (queries * row_rms_a).astype(BF16)
    attention_forward, attention_backward = attention_calls(half, length, features)
    sums_a = router_statistics([inputs], gain_a, router_a, [query_there])
    mixture = attention_forward(queries, keys, values, row_pos, key_pos, earlier=[sums_a])
    mixture_all = gather_cuts(mixture, feature_cuts)

    down_pair = with_other(down_weight, marker(query_there))
    grad_rows_m = dispatch(slots_m, half, [grad_out], [], [], plain_values, earlier=[mixture])
    grad_act_parts = expert_product(grad_rows_m, down_pair, bounds_m, unit_plan, windows)
    grad_act = [scatter_terms(*parts, order) for parts, order in zip(grad_act_parts, orders)]

    shift = marker(query_there)
    out_pair = with_other(out_weight, shift)
    shift = marker(mixture)
    gate_pair, up_pair = [with_other(weight, shift) for weight in (gate_weight, up_weight)]

    def statistics(sums):
        total = split_bits(sums, 0, bits)
        for d in range(1, groups):
            received = split_bits(swap(sums, "dp", d), 0, bits)
            turned = [bits - 1 - bit for bit in range(bits) if (d >> bit) & 1]
            total = total + jnp.flip(received, axis=turned)
        sums = join_bits(total, 0, bits)
        rms = lax.rsqrt(sums[:, :, EXPERTS] / model_width + EPSILON)
        return (rms, sums[:, :, :EXPERTS] * rms[:, :, None])

    inputs_f = [value.astype(F32) for value in inputs]
    rms_a, logits_a = statistics(sums_a)
    gates_a = choice_gates(logits_a, named_a)
    row_gates_a = choice_rows(slots_a, half, gates_a.reshape(groups, TOPK, length))[..., None]
    att_part = expert_product_back(
        [(mixture_all[0], out_pair, 0), (mixture_all[1], out_pair, feature_cuts[0])],
        bounds_a,
        everything,
        windows,
        ending=(columns_a, row_gates_a, None, None),
        earlier=[grad_act_parts[0][0]],
    )
    made = {}
    att_total = total_pair(att_part, shards, None, lambda own: [terms[1] for terms in grad_act])

    middle = [one + more.astype(F32) for one, more in zip(inputs_f, att_total)]
    rows_m = dispatch(
        slots_m,
        half,
        [inputs, att_total],
        [gain_m],
        [],
        lambda values, lines, sides: (values[0] + values[1]) * lines[0],
    )

    there = ()
    gate_parts, up_parts = [[], []], [[], []]
    for which in range(2):
        for number, size in enumerate(unit_cuts):
            for parts, pair, order in (
                (gate_parts, gate_pair, order_a), (up_parts, up_pair, order_b)
            ):
                there = expert_product(
                    rows_m,
                    pair,
                    bounds_m,
                    [(size, [scatter_groups(order)[which]])],
                    windows,
                    there,
                    sum(unit_cuts[:number]),
                )[0]
                parts[number] += there
    passed = []
    gate_terms = [scatter_terms(*parts, order_a, passed=passed) for parts in gate_parts]
    up_terms = [scatter_terms(*parts, order_b, passed=passed) for parts in up_parts]
    rms_m, logits_m = statistics(
        router_statistics([inputs, att_total], gain_m, router_m, passed)
    )
    gates_m = choice_gates(logits_m, named_m)
    row_gates_m = choice_rows(slots_m, half, gates_m.reshape(groups, TOPK, length))[..., None]
    row_rms_m = own_rows(slots_m, rms_m[0])
    active_parts, gating_all, upward_all, there = [], [], [], ()
    row_gates_grad, row_norms = 0.0, 0.0
    for number in range(len(unit_cuts)):
        active, grad_gating, grad_upward, dots, norms = unit_rows(
            gate_terms[number], up_terms[number], grad_act[number], row_rms_m, row_gates_m[0], there
        )
        there = [active]
        active_parts.append(active)
        row_gates_grad = row_gates_grad + dots[:, 0]
        row_norms = row_norms + norms[:, 0]
        gating_all.append(gather_pieces(grad_gating, order_a))
        upward_all.append(gather_pieces(grad_upward, order_b))
    side_there = [pieces[0][0] for pieces in gating_all + upward_all]
    active_all = [
        gather_pieces(late(value, *side_there), order)
        for value, order in zip(active_parts, orders)
    ]

    def router_part(
        row_gates_grad, row_norms, more, slots, gates, named, totals, logits, rms, earlier
    ):
        by_choice = [jnp.where(hit[0], row_gates_grad[:, None], 0.0) for hit in hits(slots[:1], half)]
        by_choice = [jnp.sum(one, axis=0) for one in by_choice]
        norms = [jnp.where(hit[0], row_norms[:, None], 0.0) for hit in hits(slots[:1], half)]
        norms = sum(jnp.sum(one, axis=0) for one in norms)
        packed = jnp.stack(by_choice + [norms]).reshape(TOPK + 1, owners, count)
        packed = jnp.transpose(packed, (1, 0, 2))
        packed = jnp.concatenate([packed[:, :TOPK], packed[:, TOPK:] + more], axis=1)
        packed = in_order(gather_directly(late(packed, *earlier)))
        by_choice = jnp.transpose(packed[:, :, :TOPK], (0, 2, 1, 3))
        norms = packed[:, :, TOPK]
        picked = gates * (by_choice - jnp.sum(gates * by_choice, axis=1, keepdims=True))
        picked = sum(
            jnp.where(one, picked[:, choice][:, :, None], 0.0) for choice, one in enumerate(named)
        )
        fraction = totals / (all_tokens * TOPK)
        weighting = (AUX_WEIGHT * EXPERTS / all_tokens) * fraction[:, None]
        probs = jax.nn.softmax(logits, axis=2)
        aux = probs * (weighting - jnp.sum(probs * weighting, axis=2, keepdims=True))
        balance = EXPERTS * EXPERTS * fraction * (jnp.sum(probs, axis=(0, 1, 3)) / all_tokens)
        picked = picked + aux / (owners * shards)
        norms = norms + jnp.sum(picked * logits, axis=2)
        return (picked * rms[:, :, None], total_small(norms, 1, shard_bits), balance)

    router_rows_m, inner_m, balance_m = router_part(
        row_gates_grad, row_norms, 0.0, slots_m, gates_m, named_m, totals_m, logits_m, rms_m,
        side_there,
    )
    carry = expert_product_back(
        [(gating_all[0], gate_pair, 0), (upward_all[0], up_pair, 0)], bounds_m, everything, windows
    )
    back_part = expert_product_back(
        [(gating_all[1], gate_pair, unit_cuts[0]), (upward_all[1], up_pair, unit_cuts[0])],
        bounds_m,
        everything,
        windows,
        carry=carry,
        ending=(columns_m, None, (router_rows_m, router_m), None),
    )
    active_first = [pieces[0][0] for pieces in active_all]

    def weight_grad(rows, parts, bounds, scale=None, earlier=()):
        own, other = expert_grads(rows, parts, bounds, everything, local_count, windows, scale, earlier)
        index = (1 - core) * (local_count - 1)

        def finish(earlier):
            return add_at(own, swap(other, "expert", 1), index, earlier)

        return other, finish

    def gate_grads(own):
        made["gate"] = weight_grad(rows_m, gating_all, bounds_m, earlier=[own])
        return [made["gate"][0]]

    def up_grads(own):
        made["up"] = weight_grad(rows_m, upward_all, bounds_m, earlier=[own])
        return [made["up"][0]] + active_first

    back_total = total_pair(back_part, shards, gate_grads, up_grads)
    back_m = [value.astype(F32) for value in back_total]

    shrink = rms_m * rms_m * inner_m / model_width
    shrink_pair = (shrink[:, 0, :, None], shrink[:, 1, :, None])
    grad_rows_a = dispatch(
        slots_a,
        half,
        [grad_out, back_total, inputs, att_total],
        [gain_m],
        [shrink_pair],
        lambda values, lines, sides: values[0]
        + values[1] * lines[0]
        - (values[2] + values[3]) * sides[0],
    )
    mix_parts = expert_product(grad_rows_a, out_pair, bounds_a, feature_plan, windows)
    mlp_part = expert_product_back(
        [(active_all[0], down_pair, 0), (active_all[1], down_pair, unit_cuts[0])],
        bounds_m,
        everything,
        windows,
        ending=(columns_m, row_gates_m, None, None),
        earlier=[mix_parts[0][0]],
    )
    grad_mix = jnp.concatenate(
        [term_sum(scatter_terms(*parts, order)) for parts, order in zip(mix_parts, orders)], axis=1
    ).astype(BF16)
    layer_parts = core_sum(mlp_part, shards)
    layer_block = shard_part(middle[0], 1) + shard_scatter(layer_parts).astype(F32)

    def to_tokens(blocks):
        return place_columns(spread_columns([blocks[d].astype(BF16) for d in range(groups)]))

    layer_rows = to_tokens(layer_block)
    layer_out = shard_gather(layer_rows, F32)[0]
    grad_mlp_gain = sum(
        jnp.sum(one * two, axis=(0, 1)) for one, two in zip(back_m, middle)
    )
    grad_mlp_gain = lax.dynamic_slice_in_dim(grad_mlp_gain, core * part, part, 0)
    grad_queries, grad_keys, grad_values, row_gates_grad, row_norms = attention_backward(
        queries, keys, values, row_pos, key_pos, mixture, grad_mix, row_gates_a[0], row_rms_a,
        earlier=[layer_parts[0]],
    )
    grad_queries_all = gather_cuts(grad_queries, feature_cuts)

    sent_kv = jnp.stack([grad_keys[count:], grad_values[count:]]).astype(BF16)
    received_kv = swap(sent_kv, "expert", 1).astype(F32)
    own_kv, kv_norms = [], 0.0
    for c, (grad, held) in enumerate(zip((grad_keys, grad_values), key_value)):
        total = grad[:count] + received_kv[c]
        kv_norms = kv_norms + jnp.sum(total * held[:count].astype(F32), axis=-1)
        own_kv.append((total * own_rms[:, None]).astype(BF16))
    kv_norms = jnp.stack([kv_norms, jnp.zeros_like(kv_norms)])
    kv_terms = [
        sum(dot32("tf,kf->tk", own_kv[c], kv_all[c][b]) for c in range(2)) for b in range(owners)
    ]
    kv_terms = [
        core_order(*[term[:, d * part : (d + 1) * part] for term in kv_terms], axis=1).astype(BF16)
        for d in everything
    ]
    kv_back = jnp.stack(spread_columns(kv_terms))
    grad_kv = [gather_rows(value, order) for value, order in zip(own_kv, orders)]
    router_rows_a, inner_a, balance_a = router_part(
        row_gates_grad[:, 0],
        row_norms[:, 0],
        kv_norms[:, None],
        slots_a,
        gates_a,
        named_a,
        totals_a,
        logits_a,
        rms_a,
        [pieces[0][0] for pieces in grad_queries_all],
    )
    back_part = expert_product_back(
        [(grad_queries_all[0], query_pair, 0), (grad_queries_all[1], query_pair, feature_cuts[0])],
        bounds_a,
        everything,
        windows,
        ending=(columns_a, None, (router_rows_a, router_a), None),
        earlier=kv_terms,
    )
    back_own = (back_part[0].astype(F32) + kv_back.astype(F32) / gain_a).astype(BF16)

    def down_grads(own):
        made["down"] = weight_grad(grad_rows_m, active_all, bounds_m, row_gates_m, earlier=[own])
        return [made["down"][0]]

    back_a = shard_scatter(core_sum((back_own, back_part[1]), shards), down_grads)
    query_finish = weight_grad(rows_a, grad_queries_all, bounds_a, earlier=[back_a])[1]
    out_finish = weight_grad(
        grad_rows_a, mixture_all, bounds_a, row_gates_a, earlier=[back_a]
    )[1]
    back_a = back_a.astype(F32)
    late_rows = [late(rows, back_part[0]) for rows in (router_rows_a, router_rows_m)]
    grad_kv_weight = 0.0
    router_grads = 0.0
    for block in range(owners):
        scaled = inputs_f[block] * gain_a
        own_scaled = lax.dynamic_slice_in_dim(scaled, core * part, part, 2).astype(BF16)
        some_kv = [one if block == 0 else swap(one, "expert", 1) for one in grad_kv]
        grad_kv_weight = grad_kv_weight + jnp.stack(
            [dot32("dtk,dtf->kf", own_scaled, one) for one in some_kv], axis=1
        )
        one = jnp.einsum("det,dtk->ek", late_rows[0][:, block], scaled, precision=HIGHEST)
        two = jnp.einsum(
            "det,dtk->ek", late_rows[1][:, block], middle[block] * gain_m, precision=HIGHEST
        )
        router_grads = router_grads + jnp.concatenate([one, two])
    router_grads = total_small(router_grads, None, shard_bits)
    router_grads = lax.dynamic_slice_in_dim(router_grads, core * part, part, 1)
    own_inputs = shard_part(inputs_f[0], 1)
    grad_att_gain = total_small(jnp.sum(back_a * own_inputs, axis=(0, 1)), None, shard_bits)
    grad_att_gain = lax.dynamic_slice_in_dim(grad_att_gain, core * part, part, 0)

    def own_part(value):
        return shard_part(value, 1)

    grad_middle = (
        own_part(grad_out[0]).astype(F32)
        + own_part(back_total[0]).astype(F32) * gain_m
        - own_part(middle[0]) * own_part(shrink[:, 0])[..., None]
    )
    shrink_a = own_part(rms_a[:, 0] * rms_a[:, 0] * inner_a[:, 0] / model_width)
    grad_tokens = to_tokens(grad_middle + back_a * gain_a - own_inputs * shrink_a[..., None])
    grad_tokens = shard_gather(grad_tokens, F32)[0]

    balance_terms = jnp.stack([balance_a, balance_m])
    aux_loss = (jnp.sum(balance_terms) / EXPERTS).reshape(1)
    return (
        layer_out,
        aux_loss,
        grad_tokens,
        grad_att_gain,
        router_grads[:EXPERTS].T,
        grad_kv_weight,
        query_finish([back_a]),
        out_finish([back_a]),
        grad_mlp_gain,
        router_grads[EXPERTS:].T,
        made["gate"][1]([back_a]),
        made["up"][1]([back_a]),
        made["down"][1]([back_a]),
        balance_terms,
    )


def solution(mesh):
    rows = P(("dp", "expert"), None)
    vector = P(("dp", "expert"))
    shared = P(("dp", "expert"), None, "shard")
    weight = P("expert", "dp", "shard")
    return jax.shard_map(
        per_device,
        mesh=mesh,
        in_specs=(
            rows, vector, rows, shared, weight, weight, vector, rows,
            weight, weight, weight, rows, rows, rows,
        ),
        out_specs=(
            rows, P(), rows, vector, rows, shared, weight, weight,
            vector, rows, weight, weight, weight, P(),
        ),
        check_vma=False,
    )
```

```python
import jax
import jax.numpy as jnp
from jax import lax
from jax.experimental import pallas as pl
from jax.experimental.pallas import tpu as pltpu
from jax.sharding import PartitionSpec as P

HEAD_DIM = 128
EXPERTS = 8
TOPK = 2
EPSILON = 1e-06
AUX_WEIGHT = 0.01
MASKED = -1e30
HIGHEST = lax.Precision.HIGHEST
BF16 = jnp.bfloat16
F32 = jnp.float32
TOGETHER = 4


def dot32(spec, left, right):
    return jnp.einsum(spec, left, right, preferred_element_type=F32)


def swap(value, axis, flip):
    size = lax.axis_size(axis)
    return lax.ppermute(value, axis, [(i, i ^ flip) for i in range(size)])


def marker(*earlier):
    lasts = [value[(-1,) * value.ndim].astype(F32) for value in earlier]
    return sum((last == jnp.inf).astype(jnp.int32) for last in lasts)


def late(value, *earlier):
    return value + marker(*earlier).astype(value.dtype)


def bits_in(size):
    count = 0
    while (1 << count) < size:
        count += 1
    return count


def split_bits(value, axis, bits):
    shape = value.shape
    return value.reshape(shape[:axis] + (2,) * bits + shape[axis + 1 :])


def join_bits(value, axis, bits):
    shape = value.shape
    return value.reshape(shape[:axis] + (1 << bits,) + shape[axis + bits :])


def gather_pieces(own, order):
    value, places = own[None], [0]
    for step, bit in enumerate(reversed(order)):
        received = swap(value, "dp", 1 << bit)
        others = [place | (1 << bit) for place in places]
        if step == len(order) - 1:
            return [(value, places), (received, others)]
        value, places = jnp.concatenate([value, received]), places + others
    return [(value, places)]


def gather_directly(own):
    groups = lax.axis_size("dp")
    return [(own[None], [0])] + [(swap(own, "dp", d)[None], [d]) for d in range(1, groups)]


def in_order(pieces):
    found = {}
    for array, places in pieces:
        for number, place in enumerate(places):
            found[place] = array[number]
    return jnp.stack([found[d] for d in range(len(found))])


def gather_rows(own, order):
    return in_order(gather_pieces(own, order))


def scatter_groups(order):
    places = range(1 << len(order))
    first = 1 << order[0]
    return [
        tuple(d for d in places if d & first),
        tuple(d for d in places if not d & first),
    ]


def scatter_terms(sent, kept, order, earlier=(), passed=None):
    bits = len(order)
    received = swap(sent, "dp", 1 << order[0])
    held = [bit for bit in range(bits - 1, -1, -1) if bit != order[0]]
    terms = [kept, received]
    for bit in order[1:]:
        if len(held) == 1:
            send = added(terms, earlier, 1)
            if passed is not None:
                passed.append(send)
            return terms + [swap(send, "dp", 1 << bit)]
        parts = [split_bits(term, 0, len(held)) for term in terms]
        place = held.index(bit)
        parts = [jnp.moveaxis(term, place, 0) for term in parts]
        send = sum(term[1].astype(F32) for term in parts).astype(BF16)
        send = send.reshape((-1,) + kept.shape[1:])
        terms = [term[0].reshape(send.shape) for term in parts] if len(held) > 1 else terms
        terms = terms + [swap(send, "dp", 1 << bit)]
        held = [other for other in held if other != bit]
    return terms


def term_sum(terms):
    return sum(term[0].astype(F32) for term in terms)


def shard_part(value, axis):
    size = value.shape[axis] // lax.axis_size("shard")
    return lax.dynamic_slice_in_dim(value, lax.axis_index("shard") * size, size, axis)


def added(terms, earlier=(), number=None):
    shape = terms[0].shape
    if number is None:
        steps, out_shape = shape[0], shape
        spec = pl.BlockSpec((1,) + shape[1:], lambda i: (i, 0, 0))
        out_spec = spec
    else:
        steps, out_shape = max(1, shape[1] // 256), (1,) + shape[1:]
        block = (1, shape[1] // steps, shape[2])
        spec = pl.BlockSpec(block, lambda i: (number, i, 0))
        out_spec = pl.BlockSpec(block, lambda i: (0, i, 0))

    def kernel(*refs):
        total = refs[0][...].astype(F32)
        for more in refs[1 : len(terms)]:
            total = total + more[...].astype(F32)
        refs[-1][...] = total.astype(BF16)

    size = terms[0].size // (1 if number is None else shape[0])
    return pl.pallas_call(
        kernel,
        grid=(steps,),
        in_specs=[spec] * len(terms) + anywhere(earlier),
        out_specs=out_spec,
        out_shape=jax.ShapeDtypeStruct(out_shape, BF16),
        **params(size * len(terms), 2 * size * (len(terms) + 1), memory=8),
    )(*terms, *earlier)


def split_sum(one, two, shards, earlier=()):
    groups, count, width = one.shape
    size = count // shards
    whole = pl.BlockSpec((1, count, width), lambda i, _: (i, 0, 0))

    def kernel(index_ref, one_ref, two_ref, *refs):
        for number, out in enumerate(refs[len(earlier) :]):
            place = pl.ds(pl.multiple_of((index_ref[0] ^ number) * size, size), size)
            total = one_ref[0, place, :].astype(F32) + two_ref[0, place, :].astype(F32)
            out[0] = total.astype(BF16)

    return pl.pallas_call(
        kernel,
        grid_spec=pltpu.PrefetchScalarGridSpec(
            num_scalar_prefetch=1,
            grid=(groups,),
            in_specs=[whole] * 2 + anywhere(earlier),
            out_specs=[pl.BlockSpec((1, size, width), lambda i, _: (i, 0, 0))] * shards,
        ),
        out_shape=[jax.ShapeDtypeStruct((groups, size, width), BF16)] * shards,
        **params(one.size, 6 * one.size, memory=8),
    )(lax.axis_index("shard").reshape(1), one, two, *earlier)


def joined(parts, kind, earlier=()):
    groups, size, width = parts[0].shape
    shards = len(parts)

    def kernel(index_ref, *refs):
        out = refs[-1]
        for number in range(shards):
            place = pl.ds(pl.multiple_of((index_ref[0] ^ number) * size, size), size)
            out[0, place, :] = refs[number][0].astype(kind)

    return pl.pallas_call(
        kernel,
        grid_spec=pltpu.PrefetchScalarGridSpec(
            num_scalar_prefetch=1,
            grid=(groups,),
            in_specs=[pl.BlockSpec((1, size, width), lambda i, _: (i, 0, 0))] * shards + anywhere(earlier),
            out_specs=pl.BlockSpec((1, size * shards, width), lambda i, _: (i, 0, 0)),
        ),
        out_shape=jax.ShapeDtypeStruct((groups, size * shards, width), kind),
        **params(0, 8 * parts[0].size * shards, memory=16),
    )(lax.axis_index("shard").reshape(1), *parts, *earlier)


def stacked(arrays, earlier=()):
    rows, width = arrays[0].shape

    def kernel(*refs):
        for number in range(len(arrays)):
            refs[-1][number * rows : (number + 1) * rows] = refs[number][...]

    return pl.pallas_call(
        kernel,
        in_specs=[pl.BlockSpec(memory_space=pltpu.VMEM)] * len(arrays) + anywhere(earlier),
        out_specs=pl.BlockSpec(memory_space=pltpu.VMEM),
        out_shape=jax.ShapeDtypeStruct((rows * len(arrays), width), arrays[0].dtype),
        **params(0, 4 * arrays[0].size * len(arrays), memory=16),
    )(*arrays, *earlier)


def shard_scatter(parts, pin=None):
    far = swap(parts[3], "shard", 1)
    near = swap(parts[1], "shard", 1)
    passed = parts[2] + far
    side = swap(passed, "shard", 2)
    return added([parts[0], near, side], [] if pin is None else pin(passed))


def shard_gather(own, kind=BF16, pin=None):
    count = own.shape[0]
    both = jnp.concatenate([own, swap(own, "shard", 2)])
    more = swap(both, "shard", 1)
    parts = [both[:count], more[:count], both[count:], more[count:]]
    return joined(parts, kind, [] if pin is None else pin(own))


def core_sum(pair, shards, earlier=()):
    return split_sum(pair[0], swap(pair[1], "expert", 1), shards, earlier)


def total_pair(partial_pair, shards, scatter_pin=None, gather_pin=None, earlier=()):
    own = shard_scatter(core_sum(partial_pair, shards, earlier), scatter_pin)
    whole = shard_gather(own, BF16, gather_pin)
    return (whole, swap(whole, "expert", 1))


def total_small(value, block_axis, bits):
    received = swap(value, "expert", 1)
    if block_axis is not None:
        received = jnp.flip(received, axis=block_axis)
    value = value + received
    for bit in range(bits):
        value = value + swap(value, "shard", 1 << bit)
    return value


def both_blocks(own, axis):
    return jnp.stack([own, swap(own, "expert", 1)], axis=axis)


def spread_columns(pieces):
    return [pieces[0]] + [swap(pieces[d], "dp", d) for d in range(1, len(pieces))]


def place_columns(pieces, kind=BF16, earlier=()):
    rows, width = pieces[0].shape

    def kernel(index_ref, *refs):
        for number in range(len(pieces)):
            place = pl.ds(pl.multiple_of((index_ref[0] ^ number) * width, 128), width)
            refs[-1][0, :, place] = refs[number][...].astype(kind)

    shape = (1, rows, width * len(pieces))
    return pl.pallas_call(
        kernel,
        grid_spec=pltpu.PrefetchScalarGridSpec(
            num_scalar_prefetch=1,
            grid=(1,),
            in_specs=[pl.BlockSpec((rows, width), lambda *_: (0, 0))] * len(pieces)
            + anywhere(earlier),
            out_specs=pl.BlockSpec(shape, lambda *_: (0, 0, 0)),
        ),
        out_shape=jax.ShapeDtypeStruct(shape, kind),
        **params(0, 6 * rows * width * len(pieces), memory=12),
    )(lax.axis_index("dp").reshape(1), *pieces, *earlier)


def product(left, right, dims=((1,), (0,))):
    return lax.dot_general(left, right, (dims, ((), ())), preferred_element_type=F32)


def window_of(bounds_ref, sequence, group, rows, window):
    low = bounds_ref[sequence, 2 * group]
    high = bounds_ref[sequence, 2 * group + 1]
    base = pl.multiple_of(jnp.minimum(jnp.bitwise_and(low, -16), rows - window), 16)
    at = base + lax.broadcasted_iota(jnp.int32, (window, 1), 0)
    return (base, (at >= low) & (at < high))


def whole_block(array):
    zeros = (0,) * len(array.shape)
    return pl.BlockSpec(array.shape, lambda *_: zeros, pipeline_mode=pl.Buffered(1))


def anywhere(arrays):
    return [pl.BlockSpec(memory_space=pl.ANY) for _ in arrays]


def params(flops, moved, exps=0, memory=24):
    return dict(
        compiler_params=pltpu.CompilerParams(vmem_limit_bytes=memory << 20),
        cost_estimate=pl.CostEstimate(flops=flops, bytes_accessed=moved, transcendentals=exps),
    )


def group_specs(pair):
    own, other = pair
    last = own.shape[0] - 1
    return [
        pl.BlockSpec((1,) + own.shape[1:], lambda g, *_: (jnp.minimum(g, last), 0, 0)),
        whole_block(other),
    ]


def each_group(groups, windows, step):
    group = pl.program_id(0)

    @pl.when(group < groups - 1)
    def _():
        step(group, windows[0], 0)

    @pl.when(group == groups - 1)
    def _():
        step(group, windows[1], 1)


def chosen_rows(ref, index, base, window, mine, scale=None):
    rows = ref[index, pl.ds(base, window), :]
    keep = jnp.where(mine, 1.0, 0.0)
    if scale is None:
        return rows * keep.astype(BF16)
    return (rows.astype(F32) * (scale[index, pl.ds(base, window), :] * keep)).astype(BF16)


def expert_product(rows, pair, bounds, cuts, windows, earlier=(), first=0):
    sequences = sorted(d for group in cuts[0][1] for d in group)
    if len(sequences) > TOGETHER:
        found = [{} for _ in cuts]
        for at in range(0, len(sequences), TOGETHER):
            some = sequences[at : at + TOGETHER]
            split = [(size, [(d,) for d in some]) for size, _ in cuts]
            parts = expert_product(rows, pair, bounds, split, windows, earlier, first)
            for place, part in zip(found, parts):
                place.update({d: one[0] for d, one in zip(some, part)})
        return [
            [jnp.stack([place[d] for d in group]) for group in wanted]
            for place, (_, wanted) in zip(found, cuts)
        ]
    count, depth = rows.shape[1:]
    groups, width = pair[0].shape[0] + 1, sum(size for size, _ in cuts)
    amount = len(sequences)

    def kernel(bounds_ref, rows_ref, *refs):
        weights, outs = refs[:2], refs[2 + len(earlier) :]

        @pl.when(pl.program_id(0) == 0)
        def _():
            for out in outs:
                out[...] = jnp.zeros_like(out)

        def step(group, window, which):
            bases, picked = [], []
            for sequence in sequences:
                base, mine = window_of(bounds_ref, sequence, group, count, window)
                bases.append(base)
                picked.append(chosen_rows(rows_ref, sequence, base, window, mine))
            left = jnp.concatenate(picked, axis=0)
            start = first
            number = 0
            for size, wanted in cuts:
                part = product(left, weights[which][0, :, start : start + size]).astype(BF16)
                for some in wanted:
                    for index, sequence in enumerate(some):
                        place = sequences.index(sequence)
                        at = (index, pl.ds(bases[place], window), slice(None))
                        outs[number][at] = (
                            outs[number][at] + part[place * window : (place + 1) * window]
                        )
                    number += 1
                start += size

        each_group(groups, windows, step)

    shapes = [
        jax.ShapeDtypeStruct((len(some), count, size), BF16) for size, wanted in cuts for some in wanted
    ]
    outs = pl.pallas_call(
        kernel,
        grid_spec=pltpu.PrefetchScalarGridSpec(
            num_scalar_prefetch=1,
            grid=(groups,),
            in_specs=[whole_block(rows)] + group_specs(pair) + anywhere(earlier),
            out_specs=[whole_block(shape) for shape in shapes],
        ),
        out_shape=shapes,
        **params(
            2 * amount * groups * windows[0] * depth * width,
            2 * (pair[0].size + pair[1].size + amount * count * (depth + width)),
        ),
    )(bounds, rows, *pair, *earlier)
    outs = list(outs)
    return [[outs.pop(0) for _ in wanted] for _, wanted in cuts]


def pieces_at(pieces, sequences):
    if len(sequences) == sum(len(places) for _, places in pieces):
        return pieces
    whole = in_order(pieces)
    return [(whole[sequences[0] : sequences[-1] + 1], sequences)]


def flat_pieces(pieces, arrays, specs):
    found = {}
    for array, places in pieces:
        for number, place in enumerate(places):
            found[place] = (len(arrays), number)
        arrays.append(array)
        specs.append(whole_block(array))
    return found


def expert_product_back(parts, bounds, sequences, windows, carry=None, ending=None, earlier=()):
    total_count = len(sequences)
    if total_count > TOGETHER:
        done = []
        for at in range(0, total_count, TOGETHER):
            some = sequences[at : at + TOGETHER]
            cut = slice(at, at + TOGETHER)
            some_parts = [(pieces_at(pieces, some), pair, start) for pieces, pair, start in parts]
            some_ending = None
            if ending is not None:
                slots, gates, router, extra = ending
                some_ending = (
                    slots[cut],
                    None if gates is None else gates[cut],
                    None if router is None else (router[0][cut], router[1]),
                    None if extra is None else tuple(one[cut] for one in extra),
                )
            renamed = [
                ([(array, list(range(len(places)))) for array, places in pieces], pair, start)
                for pieces, pair, start in some_parts
            ]
            done.append(
                expert_product_back(
                    renamed,
                    bounds[cut],
                    list(range(len(some))),
                    windows,
                    None if carry is None else carry[cut],
                    some_ending,
                    earlier,
                )
            )
        if ending is None:
            return jnp.concatenate(done)
        return tuple(jnp.concatenate(one) for one in zip(*done))

    own = parts[0][1][0]
    groups, depth = own.shape[0] + 1, own.shape[1]
    count = parts[0][0][0][0].shape[1]
    arrays, specs, plan, held = [], [], [], {}
    flops, moved = 0, 4 * total_count * count * depth
    for pieces, pair, start in parts:
        if id(pair) not in held:
            held[id(pair)] = len(arrays)
            arrays += list(pair)
            specs += group_specs(pair)
            moved += 2 * (pair[0].size + pair[1].size)
        size = pieces[0][0].shape[2]
        plan.append((flat_pieces(pieces, arrays, specs), held[id(pair)], start, size))
        flops += 2 * total_count * groups * windows[0] * size * depth
        moved += 2 * total_count * count * size
    places = {}

    def operand(name, array):
        places[name] = len(arrays)
        arrays.append(array)
        specs.append(whole_block(array))

    if carry is not None:
        operand("carry", carry)
    if ending is not None:
        slots, gates, router, extra = ending
        operand("slots", slots)
        if gates is not None:
            operand("gates", gates)
        if router is not None:
            operand("router_rows", router[0])
            operand("router", router[1])
        if extra is not None:
            operand("extra0", extra[0])
            operand("extra1", extra[1])
    arrays += list(earlier)
    specs += anywhere(earlier)

    def kernel(bounds_ref, *refs):
        ins, outs = refs[: len(arrays)], refs[len(arrays) :]
        total = outs[-1]

        def step(group, window, which):
            bases, masks, sums = [], [], None
            for sequence in sequences:
                base, mine = window_of(bounds_ref, sequence, group, count, window)
                bases.append(base)
                masks.append(mine)
            for found, weight_at, start, size in plan:
                left = jnp.concatenate(
                    [
                        ins[found[sequence][0]][found[sequence][1], pl.ds(base, window), :]
                        for sequence, base in zip(sequences, bases)
                    ],
                    axis=0,
                )
                weight = ins[weight_at + which][0, :, start : start + size]
                part = product(left, weight, ((1,), (1,)))
                sums = part if sums is None else sums + part
            for number, (base, mine) in enumerate(zip(bases, masks)):
                place = (number, pl.ds(base, window), slice(None))
                part = sums[number * window : (number + 1) * window]
                total[place] = jnp.where(mine, part, total[place])

        each_group(groups, windows, step)

        @pl.when(pl.program_id(0) == groups - 1)
        def _():
            if ending is None:
                if carry is not None:
                    total[...] += ins[places["carry"]][...]
                return
            tokens = outs[0].shape[1]
            for number in range(total_count):
                rows = total[number]
                if carry is not None:
                    rows = rows + ins[places["carry"]][number]
                if gates is not None:
                    rows = rows * ins[places["gates"]][number]
                rows = rows.astype(BF16)
                for block in range(2):
                    numbers = lax.broadcasted_iota(jnp.int32, (tokens, count), 1)
                    hit = None
                    for choice in range(TOPK):
                        column = ins[places["slots"]][
                            number, block * tokens : (block + 1) * tokens, choice : choice + 1
                        ]
                        one = column == numbers
                        hit = one if hit is None else hit | one
                    value = product(jnp.where(hit, 1.0, 0.0).astype(BF16), rows)
                    if router is not None:
                        value = value + product(
                            ins[places["router_rows"]][number, block].astype(BF16),
                            ins[places["router"]][...].astype(BF16),
                            ((0,), (0,)),
                        )
                    if extra is not None:
                        value = value + ins[places["extra%d" % block]][number].astype(F32)
                    outs[block][number] = value.astype(BF16)

    if ending is None:
        out_specs = [whole_block(jax.ShapeDtypeStruct((total_count, count, depth), F32))]
        out_shape = [jax.ShapeDtypeStruct((total_count, count, depth), F32)]
        scratch = []
    else:
        tokens = ending[0].shape[1] // 2
        out_shape = [jax.ShapeDtypeStruct((total_count, tokens, depth), BF16)] * 2
        out_specs = [whole_block(one) for one in out_shape]
        scratch = [pltpu.VMEM((total_count, count, depth), F32)]
    result = pl.pallas_call(
        kernel,
        grid_spec=pltpu.PrefetchScalarGridSpec(
            num_scalar_prefetch=1,
            grid=(groups,),
            in_specs=specs,
            out_specs=out_specs,
            scratch_shapes=scratch,
        ),
        out_shape=out_shape,
        **params(flops, moved, memory=36),
    )(bounds, *arrays)
    return result[0] if ending is None else tuple(result)


def expert_grads(rows, parts, bounds, sequences, local_count, windows, scale=None, earlier=()):
    if len(sequences) > TOGETHER:
        done = []
        for at in range(0, len(sequences), TOGETHER):
            some = sequences[at : at + TOGETHER]
            cut = slice(at, at + TOGETHER)
            renamed = [
                [(array, list(range(len(some)))) for array, _ in pieces_at(pieces, some)]
                for pieces in parts
            ]
            done.append(
                expert_grads(
                    rows[cut], renamed, bounds[cut], list(range(len(some))), local_count, windows,
                    None if scale is None else scale[cut], earlier,
                )
            )
        return tuple(sum(one[1:], one[0]) for one in zip(*done))
    amount = len(sequences)
    count, depth = rows.shape[1:]
    sizes = [pieces[0][0].shape[2] for pieces in parts]
    width = sum(sizes)
    groups = local_count + 1
    arrays, specs = [rows], [whole_block(rows)]
    if scale is not None:
        arrays.append(scale)
        specs.append(whole_block(scale))
    plan = [flat_pieces(pieces, arrays, specs) for pieces in parts]
    arrays += list(earlier)
    specs += anywhere(earlier)

    def kernel(bounds_ref, *refs):
        ins, outs = refs[: len(arrays)], refs[len(arrays) :]

        def step(group, window, which):
            bases, picked = [], []
            for sequence in sequences:
                base, mine = window_of(bounds_ref, sequence, group, count, window)
                bases.append(base)
                picked.append(
                    chosen_rows(ins[0], sequence, base, window, mine, None if scale is None else ins[1])
                )
            left = jnp.concatenate(picked, axis=0)
            start = 0
            for found, size in zip(plan, sizes):
                right = jnp.concatenate(
                    [
                        ins[found[sequence][0]][found[sequence][1], pl.ds(base, window), :]
                        for sequence, base in zip(sequences, bases)
                    ],
                    axis=0,
                )
                part = product(left, right, ((0,), (0,)))
                outs[which][0, :, start : start + size] = part.astype(outs[which].dtype)
                start += size

        each_group(groups, windows, step)

    return pl.pallas_call(
        kernel,
        grid_spec=pltpu.PrefetchScalarGridSpec(
            num_scalar_prefetch=1,
            grid=(groups,),
            in_specs=specs,
            out_specs=[
                pl.BlockSpec((1, depth, width), lambda g, *_: (jnp.minimum(g, local_count - 1), 0, 0)),
                whole_block(jax.ShapeDtypeStruct((1, depth, width), BF16)),
            ],
        ),
        out_shape=[
            jax.ShapeDtypeStruct((local_count, depth, width), F32),
            jax.ShapeDtypeStruct((1, depth, width), BF16),
        ],
        **params(
            2 * amount * groups * windows[0] * depth * width,
            2 * amount * count * (depth + width) + 4 * groups * depth * width,
            memory=32,
        ),
    )(bounds, *arrays)


def add_at(array, more, index, earlier=()):
    _, depth, width = array.shape
    step = depth // 4 if depth % 64 == 0 else depth
    spec = pl.BlockSpec((1, step, width), lambda i, at: (at[0], i, 0))

    def kernel(index_ref, array_ref, more_ref, *refs):
        refs[-1][...] = array_ref[...] + more_ref[...].astype(F32)

    return pl.pallas_call(
        kernel,
        grid_spec=pltpu.PrefetchScalarGridSpec(
            num_scalar_prefetch=1,
            grid=(depth // step,),
            in_specs=[spec, pl.BlockSpec((1, step, width), lambda i, _: (0, i, 0))] + anywhere(earlier),
            out_specs=spec,
        ),
        out_shape=jax.ShapeDtypeStruct(array.shape, F32),
        input_output_aliases={1: 0},
        **params(depth * width, 10 * depth * width, memory=12),
    )(index.reshape(1), array, more, *earlier)


def slot_hits(slots_ref, number, block, tokens, rows):
    numbers = lax.broadcasted_iota(jnp.int32, (rows, tokens), 0)
    hit = None
    for choice in range(TOPK):
        line = slots_ref[number, choice : choice + 1, block * tokens : (block + 1) * tokens]
        one = line == numbers
        hit = one if hit is None else hit | one
    return jnp.where(hit, 1.0, 0.0).astype(BF16)


def dispatch(slots, rows, pairs, vectors, columns, function, earlier=()):
    groups, tokens, width = pairs[0][0].shape
    arrays = [slots]
    specs = [pl.BlockSpec((1,) + slots.shape[1:], lambda i: (i, 0, 0))]
    for pair in pairs:
        arrays += list(pair)
        specs += [pl.BlockSpec((1, tokens, width), lambda i: (i, 0, 0))] * 2
    for pair in columns:
        arrays += list(pair)
        specs += [pl.BlockSpec((1, tokens, 1), lambda i: (i, 0, 0))] * 2
    arrays += list(vectors)
    specs += [whole_block(vector) for vector in vectors]
    arrays += list(earlier)
    specs += anywhere(earlier)

    def kernel(slots_ref, *refs):
        out = refs[-1]
        total = None
        for block in range(2):
            at = 0
            values, sides = [], []
            for _ in pairs:
                values.append(refs[at + block][0].astype(F32))
                at += 2
            for _ in columns:
                sides.append(refs[at + block][0])
                at += 2
            lines = [refs[at + number][...] for number in range(len(vectors))]
            value = function(values, lines, sides).astype(BF16)
            part = product(slot_hits(slots_ref, 0, block, tokens, rows), value)
            total = part if total is None else total + part
        out[0] = total.astype(BF16)

    return pl.pallas_call(
        kernel,
        grid=(groups,),
        in_specs=specs,
        out_specs=pl.BlockSpec((1, rows, width), lambda i: (i, 0, 0)),
        out_shape=jax.ShapeDtypeStruct((groups, rows, width), BF16),
        **params(4 * groups * rows * tokens * width, 2 * groups * width * (rows + 2 * tokens * len(pairs))),
    )(*arrays)


def unit_rows(gate_terms, up_terms, grad_terms, scale, gates, earlier=()):
    count, width = gate_terms[0].shape[1:]
    step = min(count, 128)
    tile = pl.BlockSpec((step, width), lambda i: (i, 0))
    term = pl.BlockSpec((None, step, width), lambda i: (0, i, 0))
    column = pl.BlockSpec((step, 1), lambda i: (i, 0))
    lists = (gate_terms, up_terms, grad_terms)
    amount = sum(len(terms) for terms in lists)

    def kernel(*refs):
        scale_ref, gates_ref = refs[amount : amount + 2]
        active_out, gating_out, upward_out, dots_out, norms_out = refs[-5:]
        sums, at = [], 0
        for terms in lists:
            total = refs[at][...].astype(F32)
            for more in refs[at + 1 : at + len(terms)]:
                total = total + more[...].astype(F32)
            sums.append(total)
            at += len(terms)
        scale_rows = scale_ref[...]
        gating, upward, grad = sums[0] * scale_rows, sums[1] * scale_rows, sums[2]
        sigma = 1.0 / (1.0 + jnp.exp(-gating))
        silu = gating * sigma
        active = silu * upward
        active_out[...] = active.astype(BF16)
        dots_out[...] = jnp.sum(grad * active, axis=1, keepdims=True)
        grad = grad * gates_ref[...]
        grad_gating = grad * upward * sigma * (1.0 + gating * (1.0 - sigma))
        grad_upward = grad * silu
        norms_out[...] = jnp.sum(grad_gating * gating + grad_upward * upward, axis=1, keepdims=True)
        gating_out[...] = (grad_gating * scale_rows).astype(BF16)
        upward_out[...] = (grad_upward * scale_rows).astype(BF16)

    return pl.pallas_call(
        kernel,
        grid=(count // step,),
        in_specs=[term] * amount + [column] * 2 + anywhere(earlier),
        out_specs=[tile] * 3 + [column] * 2,
        out_shape=[jax.ShapeDtypeStruct((count, width), BF16)] * 3
        + [jax.ShapeDtypeStruct((count, 1), F32)] * 2,
        **params(20 * count * width, 18 * count * width, count * width),
    )(*gate_terms, *up_terms, *grad_terms, scale, gates, *earlier)


def router_statistics(pairs, gain, router, earlier=()):
    groups, tokens, width = pairs[0][0].shape
    rows = 2 * EXPERTS
    block = pl.BlockSpec((1, tokens, width), lambda i: (i, 0, 0))
    amount = 2 * len(pairs)

    def kernel(*refs):
        gain_ref, router_ref, out = refs[amount], refs[amount + 1], refs[-1]
        for number in range(2):
            value = refs[number][0].astype(F32)
            for more in range(1, len(pairs)):
                value = value + refs[2 * more + number][0].astype(F32)
            scaled = (value * gain_ref[...]).astype(BF16)
            out[0, number, :EXPERTS] = product(router_ref[...].astype(BF16), scaled, ((1,), (1,)))
            out[0, number, EXPERTS:] = lax.dot_general(
                jnp.ones((EXPERTS, width), F32),
                value * value,
                (((1,), (1,)), ((), ())),
                precision=HIGHEST,
                preferred_element_type=F32,
            )

    return pl.pallas_call(
        kernel,
        grid=(groups,),
        in_specs=[block] * amount + [whole_block(gain), whole_block(router)] + anywhere(earlier),
        out_specs=pl.BlockSpec((1, 2, rows, tokens), lambda i: (i, 0, 0, 0)),
        out_shape=jax.ShapeDtypeStruct((groups, 2, rows, tokens), F32),
        **params(8 * rows * groups * tokens * width, 2 * amount * groups * tokens * width, memory=12),
    )(*(one for pair in pairs for one in pair), gain, router, *earlier)


def softmax_rows(queries, keys, row_pos, key_pos):
    scores = product(queries, keys, ((1,), (1,))) * HEAD_DIM ** (-0.5)
    scores = jnp.where(key_pos <= row_pos, scores, MASKED)
    expo = jnp.exp(scores - jnp.max(scores, axis=1, keepdims=True))
    return expo / jnp.sum(expo, axis=1, keepdims=True)


def attention_calls(count, length, features):
    heads = features // HEAD_DIM
    rows = pl.BlockSpec((count, HEAD_DIM), lambda h: (0, h))
    places = pl.BlockSpec((length, HEAD_DIM), lambda h: (0, h))
    column = pl.BlockSpec((count, 1), lambda h: (0, 0))
    line = pl.BlockSpec((1, length), lambda h: (0, 0))

    def forward_kernel(queries, keys, values, row_pos, key_pos, *refs):
        probs = softmax_rows(queries[...], keys[...], row_pos[...], key_pos[...])
        refs[-1][...] = product(probs.astype(BF16), values[...]).astype(BF16)

    def forward(*arrays, earlier=()):
        return pl.pallas_call(
            forward_kernel,
            grid=(heads,),
            in_specs=[rows, places, places, column, line] + anywhere(earlier),
            out_specs=rows,
            out_shape=jax.ShapeDtypeStruct((count, features), BF16),
            **params(4 * count * length * features, 8 * count * features, heads * count * length),
        )(*arrays, *earlier)

    def backward_kernel(
        queries, keys, values, row_pos, key_pos, mixture, grad_mix, gates, scale, *refs
    ):
        grad_queries, grad_keys, grad_values, grad_gates, norms = refs[-5:]
        probs = softmax_rows(queries[...], keys[...], row_pos[...], key_pos[...])
        grad_raw = grad_mix[...].astype(F32)
        gate_part = jnp.sum(grad_raw * mixture[...].astype(F32), axis=1, keepdims=True)
        grad_out = (grad_raw * gates[...]).astype(BF16)
        grad_values[...] = product(probs.astype(BF16), grad_out, ((0,), (0,)))
        grad_probs = product(grad_out, values[...], ((1,), (1,)))
        inner = jnp.sum(probs * grad_probs, axis=1, keepdims=True)
        grad_scores = (probs * (grad_probs - inner)).astype(BF16)
        grad_keys[...] = product(grad_scores, queries[...], ((0,), (0,))) * HEAD_DIM ** (-0.5)
        grad = product(grad_scores, keys[...]) * HEAD_DIM ** (-0.5)
        norm_part = jnp.sum(grad * queries[...].astype(F32), axis=1, keepdims=True)
        grad_queries[...] = (grad * scale[...]).astype(BF16)

        @pl.when(pl.program_id(0) == 0)
        def _():
            grad_gates[...] = gate_part
            norms[...] = norm_part

        @pl.when(pl.program_id(0) > 0)
        def _():
            grad_gates[...] += gate_part
            norms[...] += norm_part

    def backward(*arrays, earlier=()):
        return pl.pallas_call(
            backward_kernel,
            grid=(heads,),
            in_specs=[rows, places, places, column, line, rows, rows, column, column]
            + anywhere(earlier),
            out_specs=[rows, places, places, column, column],
            out_shape=[
                jax.ShapeDtypeStruct((count, features), BF16),
                jax.ShapeDtypeStruct((length, features), F32),
                jax.ShapeDtypeStruct((length, features), F32),
                jax.ShapeDtypeStruct((count, 1), F32),
                jax.ShapeDtypeStruct((count, 1), F32),
            ],
            **params(10 * count * length * features, 20 * count * features, heads * count * length, memory=58),
        )(*arrays, *earlier)

    return forward, backward


def route_tables(routes, core, local_count, half):
    sequences, blocks, _, count = routes.shape
    experts = jnp.arange(EXPERTS, dtype=jnp.int32)[:, None]
    named = [routes[:, :, choice : choice + 1] == experts for choice in range(TOPK)]
    member = named[0]
    for more in named[1:]:
        member = member | more
    steps = jnp.arange(count, dtype=jnp.int32)
    before = (steps[:, None] < steps[None, :]).astype(BF16)
    ranks = dot32("dbet,tu->dbeu", member.astype(BF16), before)
    counts = jnp.sum(member.astype(F32), axis=3)
    first_counts = jnp.where(core == 0, counts[:, 0], counts[:, 1])[:, None, :]
    second = ((core ^ jnp.arange(blocks, dtype=jnp.int32)) == 1).astype(F32)[None, :, None]
    totals = counts[:, 0] + counts[:, 1]
    smaller = (experts > experts[:, 0][None, :]).astype(F32)
    starts = jnp.sum(totals[:, None, :] * smaller, axis=2) - (core * half).astype(F32)
    places = ranks + (starts[:, None, :] + second * first_counts)[..., None]
    slots = [jnp.sum(jnp.where(one, places, 0.0), axis=2) for one in named]
    slots = jnp.stack(slots, axis=1).astype(jnp.int32).reshape(sequences, TOPK, blocks * count)
    low = jnp.clip(starts, 0, half)
    high = jnp.clip(starts + totals, 0, half)
    limits = jnp.stack([low, high], axis=2).astype(jnp.int32)
    own = lax.dynamic_slice_in_dim(limits, core * local_count, local_count, 1)
    other = lax.dynamic_slice_in_dim(
        limits, jnp.where(core == 0, local_count, local_count - 1), 1, 1
    )
    bounds = jnp.concatenate([own, other], axis=1).reshape(sequences, 2 * (local_count + 1))
    return (slots, bounds, named, jnp.sum(totals, axis=0))


def hits(slots, half):
    numbers = jnp.arange(half, dtype=jnp.int32)[:, None]
    return [slots[:, choice : choice + 1] == numbers for choice in range(TOPK)]


def choice_rows(slots, half, values):
    total = 0.0
    for choice, hit in enumerate(hits(slots, half)):
        total = total + jnp.sum(jnp.where(hit, values[:, choice : choice + 1], 0.0), axis=2)
    return total


def choice_gates(logits, named):
    picked = [jnp.sum(jnp.where(one, logits, 0.0), axis=2) for one in named]
    return jax.nn.softmax(jnp.stack(picked, axis=1), axis=1)


def per_device(
    tokens,
    att_gain,
    att_router,
    kv_weight,
    query_weight,
    out_weight,
    mlp_gain,
    mlp_router,
    gate_weight,
    up_weight,
    down_weight,
    att_routes,
    mlp_routes,
    cotangent,
):
    owners = lax.axis_size("expert")
    groups = lax.axis_size("dp")
    shards = lax.axis_size("shard")
    bits = bits_in(groups)
    shard_bits = bits_in(shards)
    local_count = EXPERTS // owners
    count, model_width = tokens.shape
    width = model_width // groups
    part = width // owners
    capacity = 5 * count * TOPK // (4 * EXPERTS)
    half = count * TOPK
    length = owners * count
    windows = [
        min(half, (most + 30) // 16 * 16)
        for most in (owners * capacity, owners * local_count * capacity - half)
    ]
    all_tokens = count * owners * groups
    features = query_weight.shape[2]
    units = gate_weight.shape[2]
    me = lax.axis_index("dp")
    core = lax.axis_index("expert")
    order_a = list(range(bits))
    order_b = order_a[bits // 2 :] + order_a[: bits // 2]
    orders = (order_a, order_b)
    everything = list(range(groups))

    def halves_of(size):
        first = (size // 128 + 1) // 2 * 128 if size >= 256 else size // 2
        return [first, size - first]

    feature_cuts, unit_cuts = halves_of(features), halves_of(units)

    def columns(value, shift=0):
        return [
            lax.dynamic_slice_in_dim(value, (me ^ d) * width + shift, width, 1) for d in range(groups)
        ]

    def core_order(own, other, axis=0):
        return jnp.where(
            core == 0,
            jnp.concatenate([own, other], axis=axis),
            jnp.concatenate([other, own], axis=axis),
        )

    routes = jnp.stack(
        [att_routes[:, 0], att_routes[:, 1], mlp_routes[:, 0], mlp_routes[:, 1]]
    )
    routes = gather_rows(both_blocks(routes, 0), order_a)
    inputs = jnp.stack(spread_columns(columns(tokens)))
    inputs = (inputs, swap(inputs, "expert", 1))
    small = jnp.concatenate(
        [att_gain[:, None], mlp_gain[:, None], att_router, mlp_router], axis=1
    )
    small = core_order(small, swap(small, "expert", 1)).astype(F32)
    gain_a, gain_m = small[:, 0][None, :], small[:, 1][None, :]
    router_a, router_m = small[:, 2 : 2 + EXPERTS].T, small[:, 2 + EXPERTS :].T
    slots_a, bounds_a, named_a, totals_a = route_tables(
        routes[:, :, :TOPK], core, local_count, half
    )
    slots_m, bounds_m, named_m, totals_m = route_tables(
        routes[:, :, TOPK:], core, local_count, half
    )

    columns_a, columns_m = jnp.swapaxes(slots_a, 1, 2), jnp.swapaxes(slots_m, 1, 2)

    def with_other(weight, shift=0):
        mine = lax.dynamic_slice_in_dim(weight, (1 - core) * (local_count - 1) + shift, 1, 0)
        return (weight, swap(mine, "expert", 1))

    plain_values = lambda values, lines, sides: values[0]
    query_pair = with_other(query_weight)
    scaled_values = lambda values, lines, sides: values[0] * lines[0]
    rows_a = dispatch(slots_a, half, [inputs], [gain_a], [], scaled_values)
    group_lists = [scatter_groups(order) for order in orders]
    feature_plan = list(zip(feature_cuts, group_lists))
    unit_plan = list(zip(unit_cuts, group_lists))
    query_parts = expert_product(rows_a, query_pair, bounds_a, feature_plan, windows)
    query_there = query_parts[0][0]
    grad_out = jnp.stack(spread_columns(columns(cotangent, marker(query_there))))
    grad_out = (grad_out, swap(grad_out, "expert", 1))

    scaled_kv = kv_weight.astype(F32) * lax.dynamic_slice_in_dim(gain_a[0], core * part, part)[:, None, None]
    scaled_kv = scaled_kv.astype(BF16)
    own_float = tokens.astype(F32)
    own_rms = lax.rsqrt(jnp.mean(own_float * own_float, axis=1) + EPSILON)
    block_tokens = [
        jnp.concatenate(
            [
                lax.dynamic_slice_in_dim(tokens, ((me ^ d) * owners + (core ^ b)) * part, part, 1)
                for d in everything
            ],
            axis=1,
        )
        for b in range(owners)
    ]
    key_value, kv_all = [], []
    for c, order in enumerate(orders):
        found = {}
        for array, places in gather_pieces(scaled_kv[:, c], order):
            for number, place in enumerate(places):
                found[place] = array[number]
        own = stacked([found[d] for d in everything], [query_there])
        kv_all.append((own, swap(own, "expert", 1)))
        total = sum(
            dot32("tk,kf->tf", some, weight) for some, weight in zip(block_tokens, kv_all[-1])
        )
        total = (total * own_rms[:, None]).astype(BF16)
        key_value.append(jnp.concatenate([total, swap(total, "expert", 1)]))
    keys, values = key_value
    seq_rms = both_blocks(own_rms, 0)

    def own_rows(slots, token_values):
        wide = jnp.broadcast_to(token_values.reshape(1, 1, length), (1, TOPK, length))
        return choice_rows(slots[:1], half, wide)[0][:, None]

    row_rms_a = own_rows(slots_a, seq_rms)
    token_pos = (
        jnp.arange(count, dtype=jnp.int32)[None, :]
        + ((core ^ jnp.arange(owners, dtype=jnp.int32)) * count)[:, None]
    ).astype(F32)
    row_pos = own_rows(slots_a, token_pos)
    key_pos = token_pos.reshape(1, length)

    def gather_cuts(value, cuts):
        return [
            gather_pieces(value[:, : cuts[0]], order_a),
            gather_pieces(value[:, cuts[0] :], order_b),
        ]

    query_passed = []
    queries = jnp.concatenate(
        [
            term_sum(scatter_terms(*parts, order, passed=query_passed))
            for parts, order in zip(query_parts, orders)
        ],
        axis=1,
    )
    queries = (queries * row_rms_a).astype(BF16)
    attention_forward, attention_backward = attention_calls(half, length, features)
    sums_a = router_statistics([inputs], gain_a, router_a, query_passed)
    mixture = attention_forward(queries, keys, values, row_pos, key_pos, earlier=[sums_a])
    mixture_all = gather_cuts(mixture, feature_cuts)

    down_pair = with_other(down_weight, marker(query_there))
    grad_rows_m = dispatch(slots_m, half, [grad_out], [], [], plain_values, earlier=[mixture])
    grad_act_parts = expert_product(grad_rows_m, down_pair, bounds_m, unit_plan, windows)
    grad_act = [scatter_terms(*parts, order) for parts, order in zip(grad_act_parts, orders)]

    shift = marker(query_there)
    out_pair = with_other(out_weight, shift)
    shift = marker(mixture)
    gate_pair, up_pair = [with_other(weight, shift) for weight in (gate_weight, up_weight)]

    def statistics(sums):
        total = split_bits(sums, 0, bits)
        for d in range(1, groups):
            received = split_bits(swap(sums, "dp", d), 0, bits)
            turned = [bits - 1 - bit for bit in range(bits) if (d >> bit) & 1]
            total = total + jnp.flip(received, axis=turned)
        sums = join_bits(total, 0, bits)
        rms = lax.rsqrt(sums[:, :, EXPERTS] / model_width + EPSILON)
        return (rms, sums[:, :, :EXPERTS] * rms[:, :, None])

    inputs_f = [value.astype(F32) for value in inputs]
    rms_a, logits_a = statistics(sums_a)
    gates_a = choice_gates(logits_a, named_a)
    row_gates_a = choice_rows(slots_a, half, gates_a.reshape(groups, TOPK, length))[..., None]
    att_part = expert_product_back(
        [(mixture_all[0], out_pair, 0), (mixture_all[1], out_pair, feature_cuts[0])],
        bounds_a,
        everything,
        windows,
        ending=(columns_a, row_gates_a, None, None),
        earlier=[grad_act_parts[0][0]],
    )
    made = {}
    att_total = total_pair(att_part, shards, None, lambda own: [terms[1] for terms in grad_act])

    middle = [one + more.astype(F32) for one, more in zip(inputs_f, att_total)]
    rows_m = dispatch(
        slots_m,
        half,
        [inputs, att_total],
        [gain_m],
        [],
        lambda values, lines, sides: (values[0] + values[1]) * lines[0],
    )

    there = ()
    gate_parts, up_parts = [[], []], [[], []]
    for which in range(2):
        for number, size in enumerate(unit_cuts):
            for parts, pair, order in (
                (gate_parts, gate_pair, order_a), (up_parts, up_pair, order_b)
            ):
                there = expert_product(
                    rows_m,
                    pair,
                    bounds_m,
                    [(size, [scatter_groups(order)[which]])],
                    windows,
                    there,
                    sum(unit_cuts[:number]),
                )[0]
                parts[number] += there
    passed, gate_terms, up_terms = [], [], []
    for number in range(len(unit_cuts)):
        there = tuple(passed)
        gate_terms.append(scatter_terms(*gate_parts[number], order_a, there, passed))
        up_terms.append(scatter_terms(*up_parts[number], order_b, there, passed))
    rms_m, logits_m = statistics(
        router_statistics([inputs, att_total], gain_m, router_m, passed)
    )
    gates_m = choice_gates(logits_m, named_m)
    row_gates_m = choice_rows(slots_m, half, gates_m.reshape(groups, TOPK, length))[..., None]
    row_rms_m = own_rows(slots_m, rms_m[0])
    active_parts, gating_all, upward_all, there = [], [], [], ()
    row_gates_grad, row_norms = 0.0, 0.0
    for number in range(len(unit_cuts)):
        active, grad_gating, grad_upward, dots, norms = unit_rows(
            gate_terms[number], up_terms[number], grad_act[number], row_rms_m, row_gates_m[0], there
        )
        there = [active]
        active_parts.append(active)
        row_gates_grad = row_gates_grad + dots[:, 0]
        row_norms = row_norms + norms[:, 0]
        gating_all.append(gather_pieces(grad_gating, order_a))
        upward_all.append(gather_pieces(grad_upward, order_b))
    side_there = [pieces[0][0] for pieces in gating_all + upward_all]
    active_all = [
        gather_pieces(late(value, *side_there), order)
        for value, order in zip(active_parts, orders)
    ]

    def router_part(
        row_gates_grad, row_norms, more, slots, gates, named, totals, logits, rms, earlier
    ):
        by_choice = [jnp.where(hit[0], row_gates_grad[:, None], 0.0) for hit in hits(slots[:1], half)]
        by_choice = [jnp.sum(one, axis=0) for one in by_choice]
        norms = [jnp.where(hit[0], row_norms[:, None], 0.0) for hit in hits(slots[:1], half)]
        norms = sum(jnp.sum(one, axis=0) for one in norms)
        packed = jnp.stack(by_choice + [norms]).reshape(TOPK + 1, owners, count)
        packed = jnp.transpose(packed, (1, 0, 2))
        packed = jnp.concatenate([packed[:, :TOPK], packed[:, TOPK:] + more], axis=1)
        packed = in_order(gather_directly(late(packed, *earlier)))
        by_choice = jnp.transpose(packed[:, :, :TOPK], (0, 2, 1, 3))
        norms = packed[:, :, TOPK]
        picked = gates * (by_choice - jnp.sum(gates * by_choice, axis=1, keepdims=True))
        picked = sum(
            jnp.where(one, picked[:, choice][:, :, None], 0.0) for choice, one in enumerate(named)
        )
        fraction = totals / (all_tokens * TOPK)
        weighting = (AUX_WEIGHT * EXPERTS / all_tokens) * fraction[:, None]
        probs = jax.nn.softmax(logits, axis=2)
        aux = probs * (weighting - jnp.sum(probs * weighting, axis=2, keepdims=True))
        balance = EXPERTS * EXPERTS * fraction * (jnp.sum(probs, axis=(0, 1, 3)) / all_tokens)
        picked = picked + aux / (owners * shards)
        norms = norms + jnp.sum(picked * logits, axis=2)
        return (picked * rms[:, :, None], total_small(norms, 1, shard_bits), balance)

    router_rows_m, inner_m, balance_m = router_part(
        row_gates_grad, row_norms, 0.0, slots_m, gates_m, named_m, totals_m, logits_m, rms_m,
        side_there,
    )
    carry = expert_product_back(
        [(gating_all[0], gate_pair, 0), (upward_all[0], up_pair, 0)], bounds_m, everything, windows
    )
    back_part = expert_product_back(
        [(gating_all[1], gate_pair, unit_cuts[0]), (upward_all[1], up_pair, unit_cuts[0])],
        bounds_m,
        everything,
        windows,
        carry=carry,
        ending=(columns_m, None, (router_rows_m, router_m), None),
    )
    active_first = [pieces[0][0] for pieces in active_all]

    def weight_grad(rows, parts, bounds, scale=None, earlier=()):
        own, other = expert_grads(rows, parts, bounds, everything, local_count, windows, scale, earlier)
        index = (1 - core) * (local_count - 1)

        def finish(earlier):
            return add_at(own, swap(other, "expert", 1), index, earlier)

        return other, finish

    def gate_grads(own):
        made["gate"] = weight_grad(rows_m, gating_all, bounds_m, earlier=[own])
        return [made["gate"][0]]

    def up_grads(own):
        made["up"] = weight_grad(rows_m, upward_all, bounds_m, earlier=[own])
        return [made["up"][0]] + active_first

    back_total = total_pair(back_part, shards, gate_grads, up_grads)
    back_m = [value.astype(F32) for value in back_total]

    shrink = rms_m * rms_m * inner_m / model_width
    shrink_pair = (shrink[:, 0, :, None], shrink[:, 1, :, None])
    grad_rows_a = dispatch(
        slots_a,
        half,
        [grad_out, back_total, inputs, att_total],
        [gain_m],
        [shrink_pair],
        lambda values, lines, sides: values[0]
        + values[1] * lines[0]
        - (values[2] + values[3]) * sides[0],
    )
    mix_parts = expert_product(grad_rows_a, out_pair, bounds_a, feature_plan, windows)
    mlp_part = expert_product_back(
        [(active_all[0], down_pair, 0), (active_all[1], down_pair, unit_cuts[0])],
        bounds_m,
        everything,
        windows,
        ending=(columns_m, row_gates_m, None, None),
        earlier=[mix_parts[0][0]],
    )
    grad_mix = jnp.concatenate(
        [term_sum(scatter_terms(*parts, order)) for parts, order in zip(mix_parts, orders)], axis=1
    ).astype(BF16)
    layer_own = mlp_part[0] + swap(mlp_part[1], "expert", 1)
    layer_block = middle[0] + lax.psum(layer_own, "shard").astype(F32)
    layer_pieces = spread_columns([layer_block[d].astype(BF16) for d in everything])
    grad_mlp_gain = sum(
        jnp.sum(one * two, axis=(0, 1)) for one, two in zip(back_m, middle)
    )
    grad_mlp_gain = lax.dynamic_slice_in_dim(grad_mlp_gain, core * part, part, 0)
    grad_queries, grad_keys, grad_values, row_gates_grad, row_norms = attention_backward(
        queries, keys, values, row_pos, key_pos, mixture, grad_mix, row_gates_a[0], row_rms_a,
        earlier=[layer_own],
    )
    grad_queries_all = gather_cuts(grad_queries, feature_cuts)

    sent_kv = jnp.stack([grad_keys[count:], grad_values[count:]]).astype(BF16)
    received_kv = swap(sent_kv, "expert", 1).astype(F32)
    own_kv, kv_norms = [], 0.0
    for c, (grad, held) in enumerate(zip((grad_keys, grad_values), key_value)):
        total = grad[:count] + received_kv[c]
        kv_norms = kv_norms + jnp.sum(total * held[:count].astype(F32), axis=-1)
        own_kv.append((total * own_rms[:, None]).astype(BF16))
    kv_norms = jnp.stack([kv_norms, jnp.zeros_like(kv_norms)])
    kv_terms = [
        sum(dot32("tf,kf->tk", own_kv[c], kv_all[c][b]) for c in range(2)) for b in range(owners)
    ]
    kv_terms = [
        core_order(*[term[:, d * part : (d + 1) * part] for term in kv_terms], axis=1).astype(BF16)
        for d in everything
    ]
    kv_back = jnp.stack(spread_columns(kv_terms))
    gate_grad, up_grad = made["gate"][1]([grad_queries]), made["up"][1]([grad_queries])
    router_rows_a, inner_a, balance_a = router_part(
        row_gates_grad[:, 0],
        row_norms[:, 0],
        kv_norms[:, None],
        slots_a,
        gates_a,
        named_a,
        totals_a,
        logits_a,
        rms_a,
        [pieces[0][0] for pieces in grad_queries_all],
    )
    back_part = expert_product_back(
        [(grad_queries_all[0], query_pair, 0), (grad_queries_all[1], query_pair, feature_cuts[0])],
        bounds_a,
        everything,
        windows,
        ending=(columns_a, None, (router_rows_a, router_a), None),
        earlier=kv_terms + [gate_grad, up_grad],
    )
    back_own = (back_part[0].astype(F32) + kv_back.astype(F32) / gain_a).astype(BF16)

    def down_grads(own):
        made["down"] = weight_grad(grad_rows_m, active_all, bounds_m, row_gates_m, earlier=[own])
        return [made["down"][0]]

    tail_parts = core_sum((back_own, back_part[1]), shards)
    back_a = shard_scatter(tail_parts, down_grads)
    grad_kv = [
        gather_rows(late(value, tail_parts[0]), order) for value, order in zip(own_kv, orders)
    ]
    layer_out = place_columns(layer_pieces, F32, [back_a])[0]
    back_there = back_a
    back_a = back_a.astype(F32)
    late_rows = [late(rows, back_there) for rows in (router_rows_a, router_rows_m)]
    grad_kv_weight = 0.0
    router_grads = 0.0
    for block in range(owners):
        scaled = inputs_f[block] * gain_a
        own_scaled = lax.dynamic_slice_in_dim(scaled, core * part, part, 2).astype(BF16)
        some_kv = [one if block == 0 else swap(one, "expert", 1) for one in grad_kv]
        grad_kv_weight = grad_kv_weight + jnp.stack(
            [dot32("dtk,dtf->kf", own_scaled, one) for one in some_kv], axis=1
        )
        one = jnp.einsum("det,dtk->ek", late_rows[0][:, block], scaled, precision=HIGHEST)
        two = jnp.einsum(
            "det,dtk->ek", late_rows[1][:, block], middle[block] * gain_m, precision=HIGHEST
        )
        router_grads = router_grads + jnp.concatenate([one, two])
    router_grads = total_small(router_grads, None, shard_bits)
    router_grads = lax.dynamic_slice_in_dim(router_grads, core * part, part, 1)
    own_inputs = shard_part(inputs_f[0], 1)
    grad_att_gain = total_small(jnp.sum(back_a * own_inputs, axis=(0, 1)), None, shard_bits)
    grad_att_gain = lax.dynamic_slice_in_dim(grad_att_gain, core * part, part, 0)

    def own_part(value):
        return shard_part(value, 1)

    grad_middle = (
        own_part(grad_out[0]).astype(F32)
        + own_part(back_total[0]).astype(F32) * gain_m
        - own_part(middle[0]) * own_part(shrink[:, 0])[..., None]
    )
    shrink_a = own_part(rms_a[:, 0] * rms_a[:, 0] * inner_a[:, 0] / model_width)
    grad_tokens = grad_middle + back_a * gain_a - own_inputs * shrink_a[..., None]
    grad_tokens = place_columns(
        spread_columns([grad_tokens[d].astype(BF16) for d in everything])
    )
    rows_there = grad_tokens
    query_finish = weight_grad(rows_a, grad_queries_all, bounds_a, earlier=[rows_there])[1]
    out_finish = weight_grad(
        grad_rows_a, mixture_all, bounds_a, row_gates_a, earlier=[rows_there]
    )[1]
    grad_tokens = shard_gather(grad_tokens, F32)[0]

    balance_terms = jnp.stack([balance_a, balance_m])
    aux_loss = (jnp.sum(balance_terms) / EXPERTS).reshape(1)
    return (
        layer_out,
        aux_loss,
        grad_tokens,
        grad_att_gain,
        router_grads[:EXPERTS].T,
        grad_kv_weight,
        query_finish([back_a]),
        out_finish([back_a]),
        grad_mlp_gain,
        router_grads[EXPERTS:].T,
        gate_grad,
        up_grad,
        made["down"][1]([back_a]),
        balance_terms,
    )


def solution(mesh):
    rows = P(("dp", "expert"), None)
    vector = P(("dp", "expert"))
    shared = P(("dp", "expert"), None, "shard")
    weight = P("expert", "dp", "shard")
    return jax.shard_map(
        per_device,
        mesh=mesh,
        in_specs=(
            rows, vector, rows, shared, weight, weight, vector, rows,
            weight, weight, weight, rows, rows, rows,
        ),
        out_specs=(
            rows, P(), rows, vector, rows, shared, weight, weight,
            vector, rows, weight, weight, weight, P(),
        ),
        check_vma=False,
    )
```

```python
import jax
import jax.numpy as jnp
from jax import lax
from jax.experimental import pallas as pl
from jax.experimental.pallas import tpu as pltpu
from jax.sharding import PartitionSpec as P

HEAD_DIM = 128
EXPERTS = 8
TOPK = 2
EPSILON = 1e-06
AUX_WEIGHT = 0.01
MASKED = -1e30
HIGHEST = lax.Precision.HIGHEST
BF16 = jnp.bfloat16
F32 = jnp.float32
TOGETHER = 4


def dot32(spec, left, right):
    return jnp.einsum(spec, left, right, preferred_element_type=F32)


def swap(value, axis, flip):
    size = lax.axis_size(axis)
    return lax.ppermute(value, axis, [(i, i ^ flip) for i in range(size)])


def marker(*earlier):
    lasts = [value[(-1,) * value.ndim].astype(F32) for value in earlier]
    return sum((last == jnp.inf).astype(jnp.int32) for last in lasts)


def late(value, *earlier):
    return value + marker(*earlier).astype(value.dtype)


def bits_in(size):
    count = 0
    while (1 << count) < size:
        count += 1
    return count


def split_bits(value, axis, bits):
    shape = value.shape
    return value.reshape(shape[:axis] + (2,) * bits + shape[axis + 1 :])


def join_bits(value, axis, bits):
    shape = value.shape
    return value.reshape(shape[:axis] + (1 << bits,) + shape[axis + bits :])


def gather_pieces(own, order):
    value, places = own[None], [0]
    for step, bit in enumerate(reversed(order)):
        received = swap(value, "dp", 1 << bit)
        others = [place | (1 << bit) for place in places]
        if step == len(order) - 1:
            return [(value, places), (received, others)]
        value, places = jnp.concatenate([value, received]), places + others
    return [(value, places)]


def gather_directly(own):
    groups = lax.axis_size("dp")
    return [(own[None], [0])] + [(swap(own, "dp", d)[None], [d]) for d in range(1, groups)]


def in_order(pieces):
    found = {}
    for array, places in pieces:
        for number, place in enumerate(places):
            found[place] = array[number]
    return jnp.stack([found[d] for d in range(len(found))])


def gather_rows(own, order):
    return in_order(gather_pieces(own, order))


def scatter_groups(order):
    places = range(1 << len(order))
    first = 1 << order[0]
    return [
        tuple(d for d in places if d & first),
        tuple(d for d in places if not d & first),
    ]


def scatter_terms(sent, kept, order, earlier=(), passed=None):
    bits = len(order)
    received = swap(sent, "dp", 1 << order[0])
    held = [bit for bit in range(bits - 1, -1, -1) if bit != order[0]]
    terms = [kept, received]
    for bit in order[1:]:
        if len(held) == 1:
            send = added(terms, earlier, 1)
            if passed is not None:
                passed.append(send)
            return terms + [swap(send, "dp", 1 << bit)]
        parts = [split_bits(term, 0, len(held)) for term in terms]
        place = held.index(bit)
        parts = [jnp.moveaxis(term, place, 0) for term in parts]
        send = sum(term[1].astype(F32) for term in parts).astype(BF16)
        send = send.reshape((-1,) + kept.shape[1:])
        terms = [term[0].reshape(send.shape) for term in parts] if len(held) > 1 else terms
        terms = terms + [swap(send, "dp", 1 << bit)]
        held = [other for other in held if other != bit]
    return terms


def term_sum(terms):
    return sum(term[0].astype(F32) for term in terms)


def shard_part(value, axis):
    size = value.shape[axis] // lax.axis_size("shard")
    return lax.dynamic_slice_in_dim(value, lax.axis_index("shard") * size, size, axis)


def added(terms, earlier=(), number=None):
    shape = terms[0].shape
    if number is None:
        steps, out_shape = shape[0], shape
        spec = pl.BlockSpec((1,) + shape[1:], lambda i: (i, 0, 0))
        out_spec = spec
    else:
        steps, out_shape = max(1, shape[1] // 256), (1,) + shape[1:]
        block = (1, shape[1] // steps, shape[2])
        spec = pl.BlockSpec(block, lambda i: (number, i, 0))
        out_spec = pl.BlockSpec(block, lambda i: (0, i, 0))

    def kernel(*refs):
        total = refs[0][...].astype(F32)
        for more in refs[1 : len(terms)]:
            total = total + more[...].astype(F32)
        refs[-1][...] = total.astype(BF16)

    size = terms[0].size // (1 if number is None else shape[0])
    return pl.pallas_call(
        kernel,
        grid=(steps,),
        in_specs=[spec] * len(terms) + anywhere(earlier),
        out_specs=out_spec,
        out_shape=jax.ShapeDtypeStruct(out_shape, BF16),
        **params(size * len(terms), 2 * size * (len(terms) + 1), memory=8),
    )(*terms, *earlier)


def split_sum(one, two, shards, earlier=()):
    groups, count, width = one.shape
    size = count // shards
    whole = pl.BlockSpec((1, count, width), lambda i, _: (i, 0, 0))

    def kernel(index_ref, one_ref, two_ref, *refs):
        for number, out in enumerate(refs[len(earlier) :]):
            place = pl.ds(pl.multiple_of((index_ref[0] ^ number) * size, size), size)
            total = one_ref[0, place, :].astype(F32) + two_ref[0, place, :].astype(F32)
            out[0] = total.astype(BF16)

    return pl.pallas_call(
        kernel,
        grid_spec=pltpu.PrefetchScalarGridSpec(
            num_scalar_prefetch=1,
            grid=(groups,),
            in_specs=[whole] * 2 + anywhere(earlier),
            out_specs=[pl.BlockSpec((1, size, width), lambda i, _: (i, 0, 0))] * shards,
        ),
        out_shape=[jax.ShapeDtypeStruct((groups, size, width), BF16)] * shards,
        **params(one.size, 6 * one.size, memory=8),
    )(lax.axis_index("shard").reshape(1), one, two, *earlier)


def joined(parts, kind, earlier=()):
    groups, size, width = parts[0].shape
    shards = len(parts)

    def kernel(index_ref, *refs):
        out = refs[-1]
        for number in range(shards):
            place = pl.ds(pl.multiple_of((index_ref[0] ^ number) * size, size), size)
            out[0, place, :] = refs[number][0].astype(kind)

    return pl.pallas_call(
        kernel,
        grid_spec=pltpu.PrefetchScalarGridSpec(
            num_scalar_prefetch=1,
            grid=(groups,),
            in_specs=[pl.BlockSpec((1, size, width), lambda i, _: (i, 0, 0))] * shards + anywhere(earlier),
            out_specs=pl.BlockSpec((1, size * shards, width), lambda i, _: (i, 0, 0)),
        ),
        out_shape=jax.ShapeDtypeStruct((groups, size * shards, width), kind),
        **params(0, 8 * parts[0].size * shards, memory=16),
    )(lax.axis_index("shard").reshape(1), *parts, *earlier)


def stacked(arrays, earlier=()):
    rows, width = arrays[0].shape

    def kernel(*refs):
        for number in range(len(arrays)):
            refs[-1][number * rows : (number + 1) * rows] = refs[number][...]

    return pl.pallas_call(
        kernel,
        in_specs=[pl.BlockSpec(memory_space=pltpu.VMEM)] * len(arrays) + anywhere(earlier),
        out_specs=pl.BlockSpec(memory_space=pltpu.VMEM),
        out_shape=jax.ShapeDtypeStruct((rows * len(arrays), width), arrays[0].dtype),
        **params(0, 4 * arrays[0].size * len(arrays), memory=16),
    )(*arrays, *earlier)


def shard_scatter(parts, pin=None):
    far = swap(parts[3], "shard", 1)
    near = swap(parts[1], "shard", 1)
    passed = parts[2] + far
    side = swap(passed, "shard", 2)
    return added([parts[0], near, side], [] if pin is None else pin(passed))


def shard_gather(own, kind=BF16, pin=None):
    count = own.shape[0]
    both = jnp.concatenate([own, swap(own, "shard", 2)])
    more = swap(both, "shard", 1)
    parts = [both[:count], more[:count], both[count:], more[count:]]
    return joined(parts, kind, [] if pin is None else pin(own))


def core_sum(pair, shards, earlier=()):
    return split_sum(pair[0], swap(pair[1], "expert", 1), shards, earlier)


def total_pair(partial_pair, shards, scatter_pin=None, gather_pin=None, earlier=()):
    own = shard_scatter(core_sum(partial_pair, shards, earlier), scatter_pin)
    whole = shard_gather(own, BF16, gather_pin)
    return (whole, swap(whole, "expert", 1))


def total_small(value, block_axis, bits):
    received = swap(value, "expert", 1)
    if block_axis is not None:
        received = jnp.flip(received, axis=block_axis)
    value = value + received
    for bit in range(bits):
        value = value + swap(value, "shard", 1 << bit)
    return value


def both_blocks(own, axis):
    return jnp.stack([own, swap(own, "expert", 1)], axis=axis)


def spread_columns(pieces):
    return [pieces[0]] + [swap(pieces[d], "dp", d) for d in range(1, len(pieces))]


def place_columns(pieces, kind=BF16, earlier=()):
    rows, width = pieces[0].shape

    def kernel(index_ref, *refs):
        for number in range(len(pieces)):
            place = pl.ds(pl.multiple_of((index_ref[0] ^ number) * width, 128), width)
            refs[-1][0, :, place] = refs[number][...].astype(kind)

    shape = (1, rows, width * len(pieces))
    return pl.pallas_call(
        kernel,
        grid_spec=pltpu.PrefetchScalarGridSpec(
            num_scalar_prefetch=1,
            grid=(1,),
            in_specs=[pl.BlockSpec((rows, width), lambda *_: (0, 0))] * len(pieces)
            + anywhere(earlier),
            out_specs=pl.BlockSpec(shape, lambda *_: (0, 0, 0)),
        ),
        out_shape=jax.ShapeDtypeStruct(shape, kind),
        **params(0, 6 * rows * width * len(pieces), memory=12),
    )(lax.axis_index("dp").reshape(1), *pieces, *earlier)


def product(left, right, dims=((1,), (0,))):
    return lax.dot_general(left, right, (dims, ((), ())), preferred_element_type=F32)


def window_of(bounds_ref, sequence, group, rows, window):
    low = bounds_ref[sequence, 2 * group]
    high = bounds_ref[sequence, 2 * group + 1]
    base = pl.multiple_of(jnp.minimum(jnp.bitwise_and(low, -16), rows - window), 16)
    at = base + lax.broadcasted_iota(jnp.int32, (window, 1), 0)
    return (base, (at >= low) & (at < high))


def whole_block(array):
    zeros = (0,) * len(array.shape)
    return pl.BlockSpec(array.shape, lambda *_: zeros, pipeline_mode=pl.Buffered(1))


def anywhere(arrays):
    return [pl.BlockSpec(memory_space=pl.ANY) for _ in arrays]


def params(flops, moved, exps=0, memory=24):
    return dict(
        compiler_params=pltpu.CompilerParams(vmem_limit_bytes=memory << 20),
        cost_estimate=pl.CostEstimate(flops=flops, bytes_accessed=moved, transcendentals=exps),
    )


def group_specs(pair):
    own, other = pair
    last = own.shape[0] - 1
    return [
        pl.BlockSpec((1,) + own.shape[1:], lambda g, *_: (jnp.minimum(g, last), 0, 0)),
        whole_block(other),
    ]


def each_group(groups, windows, step):
    group = pl.program_id(0)

    @pl.when(group < groups - 1)
    def _():
        step(group, windows[0], 0)

    @pl.when(group == groups - 1)
    def _():
        step(group, windows[1], 1)


def chosen_rows(ref, index, base, window, mine, scale=None):
    rows = ref[index, pl.ds(base, window), :]
    keep = jnp.where(mine, 1.0, 0.0)
    if scale is None:
        return rows * keep.astype(BF16)
    return (rows.astype(F32) * (scale[index, pl.ds(base, window), :] * keep)).astype(BF16)


def expert_product(rows, pair, bounds, cuts, windows, earlier=(), first=0):
    sequences = sorted(d for group in cuts[0][1] for d in group)
    if len(sequences) > TOGETHER:
        found = [{} for _ in cuts]
        for at in range(0, len(sequences), TOGETHER):
            some = sequences[at : at + TOGETHER]
            split = [(size, [(d,) for d in some]) for size, _ in cuts]
            parts = expert_product(rows, pair, bounds, split, windows, earlier, first)
            for place, part in zip(found, parts):
                place.update({d: one[0] for d, one in zip(some, part)})
        return [
            [jnp.stack([place[d] for d in group]) for group in wanted]
            for place, (_, wanted) in zip(found, cuts)
        ]
    count, depth = rows.shape[1:]
    groups, width = pair[0].shape[0] + 1, sum(size for size, _ in cuts)
    amount = len(sequences)

    def kernel(bounds_ref, rows_ref, *refs):
        weights, outs = refs[:2], refs[2 + len(earlier) :]

        @pl.when(pl.program_id(0) == 0)
        def _():
            for out in outs:
                out[...] = jnp.zeros_like(out)

        def step(group, window, which):
            bases, picked = [], []
            for sequence in sequences:
                base, mine = window_of(bounds_ref, sequence, group, count, window)
                bases.append(base)
                picked.append(chosen_rows(rows_ref, sequence, base, window, mine))
            left = jnp.concatenate(picked, axis=0)
            start = first
            number = 0
            for size, wanted in cuts:
                part = product(left, weights[which][0, :, start : start + size]).astype(BF16)
                for some in wanted:
                    for index, sequence in enumerate(some):
                        place = sequences.index(sequence)
                        at = (index, pl.ds(bases[place], window), slice(None))
                        outs[number][at] = (
                            outs[number][at] + part[place * window : (place + 1) * window]
                        )
                    number += 1
                start += size

        each_group(groups, windows, step)

    shapes = [
        jax.ShapeDtypeStruct((len(some), count, size), BF16) for size, wanted in cuts for some in wanted
    ]
    outs = pl.pallas_call(
        kernel,
        grid_spec=pltpu.PrefetchScalarGridSpec(
            num_scalar_prefetch=1,
            grid=(groups,),
            in_specs=[whole_block(rows)] + group_specs(pair) + anywhere(earlier),
            out_specs=[whole_block(shape) for shape in shapes],
        ),
        out_shape=shapes,
        **params(
            2 * amount * groups * windows[0] * depth * width,
            2 * (pair[0].size + pair[1].size + amount * count * (depth + width)),
        ),
    )(bounds, rows, *pair, *earlier)
    outs = list(outs)
    return [[outs.pop(0) for _ in wanted] for _, wanted in cuts]


def pieces_at(pieces, sequences):
    if len(sequences) == sum(len(places) for _, places in pieces):
        return pieces
    whole = in_order(pieces)
    return [(whole[sequences[0] : sequences[-1] + 1], sequences)]


def flat_pieces(pieces, arrays, specs):
    found = {}
    for array, places in pieces:
        for number, place in enumerate(places):
            found[place] = (len(arrays), number)
        arrays.append(array)
        specs.append(whole_block(array))
    return found


def expert_product_back(parts, bounds, sequences, windows, carry=None, ending=None, earlier=()):
    total_count = len(sequences)
    if total_count > TOGETHER:
        done = []
        for at in range(0, total_count, TOGETHER):
            some = sequences[at : at + TOGETHER]
            cut = slice(at, at + TOGETHER)
            some_parts = [(pieces_at(pieces, some), pair, start) for pieces, pair, start in parts]
            some_ending = None
            if ending is not None:
                slots, gates, router, extra = ending
                some_ending = (
                    slots[cut],
                    None if gates is None else gates[cut],
                    None if router is None else (router[0][cut], router[1]),
                    None if extra is None else tuple(one[cut] for one in extra),
                )
            renamed = [
                ([(array, list(range(len(places)))) for array, places in pieces], pair, start)
                for pieces, pair, start in some_parts
            ]
            done.append(
                expert_product_back(
                    renamed,
                    bounds[cut],
                    list(range(len(some))),
                    windows,
                    None if carry is None else carry[cut],
                    some_ending,
                    earlier,
                )
            )
        if ending is None:
            return jnp.concatenate(done)
        return tuple(jnp.concatenate(one) for one in zip(*done))

    own = parts[0][1][0]
    groups, depth = own.shape[0] + 1, own.shape[1]
    count = parts[0][0][0][0].shape[1]
    arrays, specs, plan, held = [], [], [], {}
    flops, moved = 0, 4 * total_count * count * depth
    for pieces, pair, start in parts:
        if id(pair) not in held:
            held[id(pair)] = len(arrays)
            arrays += list(pair)
            specs += group_specs(pair)
            moved += 2 * (pair[0].size + pair[1].size)
        size = pieces[0][0].shape[2]
        plan.append((flat_pieces(pieces, arrays, specs), held[id(pair)], start, size))
        flops += 2 * total_count * groups * windows[0] * size * depth
        moved += 2 * total_count * count * size
    places = {}

    def operand(name, array):
        places[name] = len(arrays)
        arrays.append(array)
        specs.append(whole_block(array))

    if carry is not None:
        operand("carry", carry)
    if ending is not None:
        slots, gates, router, extra = ending
        operand("slots", slots)
        if gates is not None:
            operand("gates", gates)
        if router is not None:
            operand("router_rows", router[0])
            operand("router", router[1])
        if extra is not None:
            operand("extra0", extra[0])
            operand("extra1", extra[1])
    arrays += list(earlier)
    specs += anywhere(earlier)

    def kernel(bounds_ref, *refs):
        ins, outs = refs[: len(arrays)], refs[len(arrays) :]
        total = outs[-1]

        def step(group, window, which):
            bases, masks, sums = [], [], None
            for sequence in sequences:
                base, mine = window_of(bounds_ref, sequence, group, count, window)
                bases.append(base)
                masks.append(mine)
            for found, weight_at, start, size in plan:
                left = jnp.concatenate(
                    [
                        ins[found[sequence][0]][found[sequence][1], pl.ds(base, window), :]
                        for sequence, base in zip(sequences, bases)
                    ],
                    axis=0,
                )
                weight = ins[weight_at + which][0, :, start : start + size]
                part = product(left, weight, ((1,), (1,)))
                sums = part if sums is None else sums + part
            for number, (base, mine) in enumerate(zip(bases, masks)):
                place = (number, pl.ds(base, window), slice(None))
                part = sums[number * window : (number + 1) * window]
                total[place] = jnp.where(mine, part, total[place])

        each_group(groups, windows, step)

        @pl.when(pl.program_id(0) == groups - 1)
        def _():
            if ending is None:
                if carry is not None:
                    total[...] += ins[places["carry"]][...]
                return
            tokens = outs[0].shape[1]
            for number in range(total_count):
                rows = total[number]
                if carry is not None:
                    rows = rows + ins[places["carry"]][number]
                if gates is not None:
                    rows = rows * ins[places["gates"]][number]
                rows = rows.astype(BF16)
                for block in range(2):
                    numbers = lax.broadcasted_iota(jnp.int32, (tokens, count), 1)
                    hit = None
                    for choice in range(TOPK):
                        column = ins[places["slots"]][
                            number, block * tokens : (block + 1) * tokens, choice : choice + 1
                        ]
                        one = column == numbers
                        hit = one if hit is None else hit | one
                    value = product(jnp.where(hit, 1.0, 0.0).astype(BF16), rows)
                    if router is not None:
                        value = value + product(
                            ins[places["router_rows"]][number, block].astype(BF16),
                            ins[places["router"]][...].astype(BF16),
                            ((0,), (0,)),
                        )
                    if extra is not None:
                        value = value + ins[places["extra%d" % block]][number].astype(F32)
                    outs[block][number] = value.astype(BF16)

    if ending is None:
        out_specs = [whole_block(jax.ShapeDtypeStruct((total_count, count, depth), F32))]
        out_shape = [jax.ShapeDtypeStruct((total_count, count, depth), F32)]
        scratch = []
    else:
        tokens = ending[0].shape[1] // 2
        out_shape = [jax.ShapeDtypeStruct((total_count, tokens, depth), BF16)] * 2
        out_specs = [whole_block(one) for one in out_shape]
        scratch = [pltpu.VMEM((total_count, count, depth), F32)]
    result = pl.pallas_call(
        kernel,
        grid_spec=pltpu.PrefetchScalarGridSpec(
            num_scalar_prefetch=1,
            grid=(groups,),
            in_specs=specs,
            out_specs=out_specs,
            scratch_shapes=scratch,
        ),
        out_shape=out_shape,
        **params(flops, moved, memory=36),
    )(bounds, *arrays)
    return result[0] if ending is None else tuple(result)


def expert_grads(rows, parts, bounds, sequences, local_count, windows, scale=None, earlier=()):
    if len(sequences) > TOGETHER:
        done = []
        for at in range(0, len(sequences), TOGETHER):
            some = sequences[at : at + TOGETHER]
            cut = slice(at, at + TOGETHER)
            renamed = [
                [(array, list(range(len(some)))) for array, _ in pieces_at(pieces, some)]
                for pieces in parts
            ]
            done.append(
                expert_grads(
                    rows[cut], renamed, bounds[cut], list(range(len(some))), local_count, windows,
                    None if scale is None else scale[cut], earlier,
                )
            )
        return tuple(sum(one[1:], one[0]) for one in zip(*done))
    amount = len(sequences)
    count, depth = rows.shape[1:]
    sizes = [pieces[0][0].shape[2] for pieces in parts]
    width = sum(sizes)
    groups = local_count + 1
    arrays, specs = [rows], [whole_block(rows)]
    if scale is not None:
        arrays.append(scale)
        specs.append(whole_block(scale))
    plan = [flat_pieces(pieces, arrays, specs) for pieces in parts]
    arrays += list(earlier)
    specs += anywhere(earlier)

    def kernel(bounds_ref, *refs):
        ins, outs = refs[: len(arrays)], refs[len(arrays) :]

        def step(group, window, which):
            bases, picked = [], []
            for sequence in sequences:
                base, mine = window_of(bounds_ref, sequence, group, count, window)
                bases.append(base)
                picked.append(
                    chosen_rows(ins[0], sequence, base, window, mine, None if scale is None else ins[1])
                )
            left = jnp.concatenate(picked, axis=0)
            start = 0
            for found, size in zip(plan, sizes):
                right = jnp.concatenate(
                    [
                        ins[found[sequence][0]][found[sequence][1], pl.ds(base, window), :]
                        for sequence, base in zip(sequences, bases)
                    ],
                    axis=0,
                )
                part = product(left, right, ((0,), (0,)))
                outs[which][0, :, start : start + size] = part.astype(outs[which].dtype)
                start += size

        each_group(groups, windows, step)

    return pl.pallas_call(
        kernel,
        grid_spec=pltpu.PrefetchScalarGridSpec(
            num_scalar_prefetch=1,
            grid=(groups,),
            in_specs=specs,
            out_specs=[
                pl.BlockSpec((1, depth, width), lambda g, *_: (jnp.minimum(g, local_count - 1), 0, 0)),
                whole_block(jax.ShapeDtypeStruct((1, depth, width), BF16)),
            ],
        ),
        out_shape=[
            jax.ShapeDtypeStruct((local_count, depth, width), F32),
            jax.ShapeDtypeStruct((1, depth, width), BF16),
        ],
        **params(
            2 * amount * groups * windows[0] * depth * width,
            2 * amount * count * (depth + width) + 4 * groups * depth * width,
            memory=32,
        ),
    )(bounds, *arrays)


def add_at(array, more, index, earlier=()):
    _, depth, width = array.shape
    step = depth // 4 if depth % 64 == 0 else depth
    spec = pl.BlockSpec((1, step, width), lambda i, at: (at[0], i, 0))

    def kernel(index_ref, array_ref, more_ref, *refs):
        refs[-1][...] = array_ref[...] + more_ref[...].astype(F32)

    return pl.pallas_call(
        kernel,
        grid_spec=pltpu.PrefetchScalarGridSpec(
            num_scalar_prefetch=1,
            grid=(depth // step,),
            in_specs=[spec, pl.BlockSpec((1, step, width), lambda i, _: (0, i, 0))] + anywhere(earlier),
            out_specs=spec,
        ),
        out_shape=jax.ShapeDtypeStruct(array.shape, F32),
        input_output_aliases={1: 0},
        **params(depth * width, 10 * depth * width, memory=12),
    )(index.reshape(1), array, more, *earlier)


def slot_hits(slots_ref, number, block, tokens, rows):
    numbers = lax.broadcasted_iota(jnp.int32, (rows, tokens), 0)
    hit = None
    for choice in range(TOPK):
        line = slots_ref[number, choice : choice + 1, block * tokens : (block + 1) * tokens]
        one = line == numbers
        hit = one if hit is None else hit | one
    return jnp.where(hit, 1.0, 0.0).astype(BF16)


def dispatch(slots, rows, pairs, vectors, columns, function, earlier=()):
    groups, tokens, width = pairs[0][0].shape
    arrays = [slots]
    specs = [pl.BlockSpec((1,) + slots.shape[1:], lambda i: (i, 0, 0))]
    for pair in pairs:
        arrays += list(pair)
        specs += [pl.BlockSpec((1, tokens, width), lambda i: (i, 0, 0))] * 2
    for pair in columns:
        arrays += list(pair)
        specs += [pl.BlockSpec((1, tokens, 1), lambda i: (i, 0, 0))] * 2
    arrays += list(vectors)
    specs += [whole_block(vector) for vector in vectors]
    arrays += list(earlier)
    specs += anywhere(earlier)

    def kernel(slots_ref, *refs):
        out = refs[-1]
        total = None
        for block in range(2):
            at = 0
            values, sides = [], []
            for _ in pairs:
                values.append(refs[at + block][0].astype(F32))
                at += 2
            for _ in columns:
                sides.append(refs[at + block][0])
                at += 2
            lines = [refs[at + number][...] for number in range(len(vectors))]
            value = function(values, lines, sides).astype(BF16)
            part = product(slot_hits(slots_ref, 0, block, tokens, rows), value)
            total = part if total is None else total + part
        out[0] = total.astype(BF16)

    return pl.pallas_call(
        kernel,
        grid=(groups,),
        in_specs=specs,
        out_specs=pl.BlockSpec((1, rows, width), lambda i: (i, 0, 0)),
        out_shape=jax.ShapeDtypeStruct((groups, rows, width), BF16),
        **params(4 * groups * rows * tokens * width, 2 * groups * width * (rows + 2 * tokens * len(pairs))),
    )(*arrays)


def unit_rows(gate_terms, up_terms, grad_terms, scale, gates, earlier=()):
    count, width = gate_terms[0].shape[1:]
    step = min(count, 128)
    tile = pl.BlockSpec((step, width), lambda i: (i, 0))
    term = pl.BlockSpec((None, step, width), lambda i: (0, i, 0))
    column = pl.BlockSpec((step, 1), lambda i: (i, 0))
    lists = (gate_terms, up_terms, grad_terms)
    amount = sum(len(terms) for terms in lists)

    def kernel(*refs):
        scale_ref, gates_ref = refs[amount : amount + 2]
        active_out, gating_out, upward_out, dots_out, norms_out = refs[-5:]
        sums, at = [], 0
        for terms in lists:
            total = refs[at][...].astype(F32)
            for more in refs[at + 1 : at + len(terms)]:
                total = total + more[...].astype(F32)
            sums.append(total)
            at += len(terms)
        scale_rows = scale_ref[...]
        gating, upward, grad = sums[0] * scale_rows, sums[1] * scale_rows, sums[2]
        sigma = 1.0 / (1.0 + jnp.exp(-gating))
        silu = gating * sigma
        active = silu * upward
        active_out[...] = active.astype(BF16)
        dots_out[...] = jnp.sum(grad * active, axis=1, keepdims=True)
        grad = grad * gates_ref[...]
        grad_gating = grad * upward * sigma * (1.0 + gating * (1.0 - sigma))
        grad_upward = grad * silu
        norms_out[...] = jnp.sum(grad_gating * gating + grad_upward * upward, axis=1, keepdims=True)
        gating_out[...] = (grad_gating * scale_rows).astype(BF16)
        upward_out[...] = (grad_upward * scale_rows).astype(BF16)

    return pl.pallas_call(
        kernel,
        grid=(count // step,),
        in_specs=[term] * amount + [column] * 2 + anywhere(earlier),
        out_specs=[tile] * 3 + [column] * 2,
        out_shape=[jax.ShapeDtypeStruct((count, width), BF16)] * 3
        + [jax.ShapeDtypeStruct((count, 1), F32)] * 2,
        **params(20 * count * width, 18 * count * width, count * width),
    )(*gate_terms, *up_terms, *grad_terms, scale, gates, *earlier)


def router_statistics(pairs, gain, router, earlier=()):
    groups, tokens, width = pairs[0][0].shape
    rows = 2 * EXPERTS
    block = pl.BlockSpec((1, tokens, width), lambda i: (i, 0, 0))
    amount = 2 * len(pairs)

    def kernel(*refs):
        gain_ref, router_ref, out = refs[amount], refs[amount + 1], refs[-1]
        for number in range(2):
            value = refs[number][0].astype(F32)
            for more in range(1, len(pairs)):
                value = value + refs[2 * more + number][0].astype(F32)
            scaled = (value * gain_ref[...]).astype(BF16)
            out[0, number, :EXPERTS] = product(router_ref[...].astype(BF16), scaled, ((1,), (1,)))
            squares = value * value
            high = squares.astype(BF16)
            rest = (squares - high.astype(F32)).astype(BF16)
            ones = jnp.ones((EXPERTS, width), BF16)
            out[0, number, EXPERTS:] = product(ones, high, ((1,), (1,))) + product(
                ones, rest, ((1,), (1,))
            )

    return pl.pallas_call(
        kernel,
        grid=(groups,),
        in_specs=[block] * amount + [whole_block(gain), whole_block(router)] + anywhere(earlier),
        out_specs=pl.BlockSpec((1, 2, rows, tokens), lambda i: (i, 0, 0, 0)),
        out_shape=jax.ShapeDtypeStruct((groups, 2, rows, tokens), F32),
        **params(8 * rows * groups * tokens * width, 2 * amount * groups * tokens * width, memory=12),
    )(*(one for pair in pairs for one in pair), gain, router, *earlier)


def softmax_rows(queries, keys, row_pos, key_pos):
    scores = product(queries, keys, ((1,), (1,))) * HEAD_DIM ** (-0.5)
    scores = jnp.where(key_pos <= row_pos, scores, MASKED)
    expo = jnp.exp(scores - jnp.max(scores, axis=1, keepdims=True))
    return expo / jnp.sum(expo, axis=1, keepdims=True)


def attention_calls(count, length, features):
    heads = features // HEAD_DIM
    rows = pl.BlockSpec((count, HEAD_DIM), lambda h: (0, h))
    places = pl.BlockSpec((length, HEAD_DIM), lambda h: (0, h))
    column = pl.BlockSpec((count, 1), lambda h: (0, 0))
    line = pl.BlockSpec((1, length), lambda h: (0, 0))

    def forward_kernel(queries, keys, values, row_pos, key_pos, *refs):
        probs = softmax_rows(queries[...], keys[...], row_pos[...], key_pos[...])
        refs[-1][...] = product(probs.astype(BF16), values[...]).astype(BF16)

    def forward(*arrays, earlier=()):
        return pl.pallas_call(
            forward_kernel,
            grid=(heads,),
            in_specs=[rows, places, places, column, line] + anywhere(earlier),
            out_specs=rows,
            out_shape=jax.ShapeDtypeStruct((count, features), BF16),
            **params(4 * count * length * features, 8 * count * features, heads * count * length),
        )(*arrays, *earlier)

    def backward_kernel(
        queries, keys, values, row_pos, key_pos, mixture, grad_mix, gates, scale, *refs
    ):
        grad_queries, grad_keys, grad_values, grad_gates, norms = refs[-5:]
        probs = softmax_rows(queries[...], keys[...], row_pos[...], key_pos[...])
        grad_raw = grad_mix[...].astype(F32)
        gate_part = jnp.sum(grad_raw * mixture[...].astype(F32), axis=1, keepdims=True)
        grad_out = (grad_raw * gates[...]).astype(BF16)
        grad_values[...] = product(probs.astype(BF16), grad_out, ((0,), (0,)))
        grad_probs = product(grad_out, values[...], ((1,), (1,)))
        inner = jnp.sum(probs * grad_probs, axis=1, keepdims=True)
        grad_scores = (probs * (grad_probs - inner)).astype(BF16)
        grad_keys[...] = product(grad_scores, queries[...], ((0,), (0,))) * HEAD_DIM ** (-0.5)
        grad = product(grad_scores, keys[...]) * HEAD_DIM ** (-0.5)
        norm_part = jnp.sum(grad * queries[...].astype(F32), axis=1, keepdims=True)
        grad_queries[...] = (grad * scale[...]).astype(BF16)

        @pl.when(pl.program_id(0) == 0)
        def _():
            grad_gates[...] = gate_part
            norms[...] = norm_part

        @pl.when(pl.program_id(0) > 0)
        def _():
            grad_gates[...] += gate_part
            norms[...] += norm_part

    def backward(*arrays, earlier=()):
        return pl.pallas_call(
            backward_kernel,
            grid=(heads,),
            in_specs=[rows, places, places, column, line, rows, rows, column, column]
            + anywhere(earlier),
            out_specs=[rows, places, places, column, column],
            out_shape=[
                jax.ShapeDtypeStruct((count, features), BF16),
                jax.ShapeDtypeStruct((length, features), F32),
                jax.ShapeDtypeStruct((length, features), F32),
                jax.ShapeDtypeStruct((count, 1), F32),
                jax.ShapeDtypeStruct((count, 1), F32),
            ],
            **params(10 * count * length * features, 20 * count * features, heads * count * length, memory=58),
        )(*arrays, *earlier)

    return forward, backward


def route_tables(routes, core, local_count, half):
    sequences, blocks, _, count = routes.shape
    experts = jnp.arange(EXPERTS, dtype=jnp.int32)[:, None]
    named = [routes[:, :, choice : choice + 1] == experts for choice in range(TOPK)]
    member = named[0]
    for more in named[1:]:
        member = member | more
    steps = jnp.arange(count, dtype=jnp.int32)
    before = (steps[:, None] < steps[None, :]).astype(BF16)
    ranks = dot32("dbet,tu->dbeu", member.astype(BF16), before)
    counts = jnp.sum(member.astype(F32), axis=3)
    first_counts = jnp.where(core == 0, counts[:, 0], counts[:, 1])[:, None, :]
    second = ((core ^ jnp.arange(blocks, dtype=jnp.int32)) == 1).astype(F32)[None, :, None]
    totals = counts[:, 0] + counts[:, 1]
    smaller = (experts > experts[:, 0][None, :]).astype(F32)
    starts = jnp.sum(totals[:, None, :] * smaller, axis=2) - (core * half).astype(F32)
    places = ranks + (starts[:, None, :] + second * first_counts)[..., None]
    slots = [jnp.sum(jnp.where(one, places, 0.0), axis=2) for one in named]
    slots = jnp.stack(slots, axis=1).astype(jnp.int32).reshape(sequences, TOPK, blocks * count)
    low = jnp.clip(starts, 0, half)
    high = jnp.clip(starts + totals, 0, half)
    limits = jnp.stack([low, high], axis=2).astype(jnp.int32)
    own = lax.dynamic_slice_in_dim(limits, core * local_count, local_count, 1)
    other = lax.dynamic_slice_in_dim(
        limits, jnp.where(core == 0, local_count, local_count - 1), 1, 1
    )
    bounds = jnp.concatenate([own, other], axis=1).reshape(sequences, 2 * (local_count + 1))
    return (slots, bounds, named, jnp.sum(totals, axis=0))


def hits(slots, half):
    numbers = jnp.arange(half, dtype=jnp.int32)[:, None]
    return [slots[:, choice : choice + 1] == numbers for choice in range(TOPK)]


def choice_rows(slots, half, values):
    total = 0.0
    for choice, hit in enumerate(hits(slots, half)):
        total = total + jnp.sum(jnp.where(hit, values[:, choice : choice + 1], 0.0), axis=2)
    return total


def choice_gates(logits, named):
    first, second = [jnp.sum(jnp.where(one, logits, 0.0), axis=2) for one in named]
    return jnp.stack(
        [1.0 / (1.0 + jnp.exp(second - first)), 1.0 / (1.0 + jnp.exp(first - second))], axis=1
    )


def per_device(
    tokens,
    att_gain,
    att_router,
    kv_weight,
    query_weight,
    out_weight,
    mlp_gain,
    mlp_router,
    gate_weight,
    up_weight,
    down_weight,
    att_routes,
    mlp_routes,
    cotangent,
):
    owners = lax.axis_size("expert")
    groups = lax.axis_size("dp")
    shards = lax.axis_size("shard")
    bits = bits_in(groups)
    shard_bits = bits_in(shards)
    local_count = EXPERTS // owners
    count, model_width = tokens.shape
    width = model_width // groups
    part = width // owners
    capacity = 5 * count * TOPK // (4 * EXPERTS)
    half = count * TOPK
    length = owners * count
    windows = [
        min(half, (most + 30) // 16 * 16)
        for most in (owners * capacity, owners * local_count * capacity - half)
    ]
    all_tokens = count * owners * groups
    features = query_weight.shape[2]
    units = gate_weight.shape[2]
    me = lax.axis_index("dp")
    core = lax.axis_index("expert")
    order_a = list(range(bits))
    order_b = order_a[bits // 2 :] + order_a[: bits // 2]
    orders = (order_a, order_b)
    everything = list(range(groups))

    def halves_of(size):
        first = (size // 128 + 1) // 2 * 128 if size >= 256 else size // 2
        return [first, size - first]

    feature_cuts, unit_cuts = halves_of(features), halves_of(units)

    def columns(value, shift=0):
        return [
            lax.dynamic_slice_in_dim(value, (me ^ d) * width + shift, width, 1) for d in range(groups)
        ]

    def core_order(own, other, axis=0):
        return jnp.where(
            core == 0,
            jnp.concatenate([own, other], axis=axis),
            jnp.concatenate([other, own], axis=axis),
        )

    routes = jnp.stack(
        [att_routes[:, 0], att_routes[:, 1], mlp_routes[:, 0], mlp_routes[:, 1]]
    )
    routes = gather_rows(both_blocks(routes, 0), order_a)
    inputs = jnp.stack(spread_columns(columns(tokens)))
    inputs = (inputs, swap(inputs, "expert", 1))
    small = jnp.concatenate(
        [att_gain[:, None], mlp_gain[:, None], att_router, mlp_router], axis=1
    )
    small = core_order(small, swap(small, "expert", 1)).astype(F32)
    gain_a, gain_m = small[:, 0][None, :], small[:, 1][None, :]
    router_a, router_m = small[:, 2 : 2 + EXPERTS].T, small[:, 2 + EXPERTS :].T
    slots_a, bounds_a, named_a, totals_a = route_tables(
        routes[:, :, :TOPK], core, local_count, half
    )
    slots_m, bounds_m, named_m, totals_m = route_tables(
        routes[:, :, TOPK:], core, local_count, half
    )

    columns_a, columns_m = jnp.swapaxes(slots_a, 1, 2), jnp.swapaxes(slots_m, 1, 2)

    def with_other(weight, shift=0):
        mine = lax.dynamic_slice_in_dim(weight, (1 - core) * (local_count - 1) + shift, 1, 0)
        return (weight, swap(mine, "expert", 1))

    plain_values = lambda values, lines, sides: values[0]
    query_pair = with_other(query_weight)
    scaled_values = lambda values, lines, sides: values[0] * lines[0]
    rows_a = dispatch(slots_a, half, [inputs], [gain_a], [], scaled_values)
    group_lists = [scatter_groups(order) for order in orders]
    feature_plan = list(zip(feature_cuts, group_lists))
    unit_plan = list(zip(unit_cuts, group_lists))
    query_parts = expert_product(rows_a, query_pair, bounds_a, feature_plan, windows)
    query_there = query_parts[0][0]
    grad_out = jnp.stack(spread_columns(columns(cotangent, marker(query_there))))
    grad_out = (grad_out, swap(grad_out, "expert", 1))

    scaled_kv = kv_weight.astype(F32) * lax.dynamic_slice_in_dim(gain_a[0], core * part, part)[:, None, None]
    scaled_kv = scaled_kv.astype(BF16)
    own_float = tokens.astype(F32)
    own_rms = lax.rsqrt(jnp.mean(own_float * own_float, axis=1) + EPSILON)
    block_tokens = [
        jnp.concatenate(
            [
                lax.dynamic_slice_in_dim(tokens, ((me ^ d) * owners + (core ^ b)) * part, part, 1)
                for d in everything
            ],
            axis=1,
        )
        for b in range(owners)
    ]
    key_value, kv_all = [], []
    for c, order in enumerate(orders):
        found = {}
        for array, places in gather_pieces(scaled_kv[:, c], order):
            for number, place in enumerate(places):
                found[place] = array[number]
        own = stacked([found[d] for d in everything], [query_there])
        kv_all.append((own, swap(own, "expert", 1)))
        total = sum(
            dot32("tk,kf->tf", some, weight) for some, weight in zip(block_tokens, kv_all[-1])
        )
        total = (total * own_rms[:, None]).astype(BF16)
        key_value.append(jnp.concatenate([total, swap(total, "expert", 1)]))
    keys, values = key_value
    seq_rms = both_blocks(own_rms, 0)

    def own_rows(slots, token_values):
        wide = jnp.broadcast_to(token_values.reshape(1, 1, length), (1, TOPK, length))
        return choice_rows(slots[:1], half, wide)[0][:, None]

    row_rms_a = own_rows(slots_a, seq_rms)
    token_pos = (
        jnp.arange(count, dtype=jnp.int32)[None, :]
        + ((core ^ jnp.arange(owners, dtype=jnp.int32)) * count)[:, None]
    ).astype(F32)
    row_pos = own_rows(slots_a, token_pos)
    key_pos = token_pos.reshape(1, length)

    def gather_cuts(value, cuts):
        return [
            gather_pieces(value[:, : cuts[0]], order_a),
            gather_pieces(value[:, cuts[0] :], order_b),
        ]

    query_passed = []
    queries = jnp.concatenate(
        [
            term_sum(scatter_terms(*parts, order, passed=query_passed))
            for parts, order in zip(query_parts, orders)
        ],
        axis=1,
    )
    queries = (queries * row_rms_a).astype(BF16)
    attention_forward, attention_backward = attention_calls(half, length, features)
    sums_a = router_statistics([inputs], gain_a, router_a, query_passed)
    mixture = attention_forward(queries, keys, values, row_pos, key_pos, earlier=[sums_a])
    mixture_all = gather_cuts(mixture, feature_cuts)

    down_pair = with_other(down_weight)
    grad_rows_m = dispatch(slots_m, half, [grad_out], [], [], plain_values, earlier=[mixture])
    grad_act_parts = expert_product(grad_rows_m, down_pair, bounds_m, unit_plan, windows)
    grad_act = [scatter_terms(*parts, order) for parts, order in zip(grad_act_parts, orders)]

    out_pair = with_other(out_weight)
    shift = marker(mixture)
    gate_pair, up_pair = [with_other(weight, shift) for weight in (gate_weight, up_weight)]

    def statistics(sums):
        total = split_bits(sums, 0, bits)
        for d in range(1, groups):
            received = split_bits(swap(sums, "dp", d), 0, bits)
            turned = [bits - 1 - bit for bit in range(bits) if (d >> bit) & 1]
            total = total + jnp.flip(received, axis=turned)
        sums = join_bits(total, 0, bits)
        rms = lax.rsqrt(sums[:, :, EXPERTS] / model_width + EPSILON)
        return (rms, sums[:, :, :EXPERTS] * rms[:, :, None])

    inputs_f = [value.astype(F32) for value in inputs]
    rms_a, logits_a = statistics(sums_a)
    gates_a = choice_gates(logits_a, named_a)
    row_gates_a = choice_rows(slots_a, half, gates_a.reshape(groups, TOPK, length))[..., None]
    att_part = expert_product_back(
        [(mixture_all[0], out_pair, 0), (mixture_all[1], out_pair, feature_cuts[0])],
        bounds_a,
        everything,
        windows,
        ending=(columns_a, row_gates_a, None, None),
        earlier=[grad_act_parts[0][0]],
    )
    made = {}
    att_total = total_pair(att_part, shards, None, lambda own: [terms[1] for terms in grad_act])

    middle = [one + more.astype(F32) for one, more in zip(inputs_f, att_total)]
    rows_m = dispatch(
        slots_m,
        half,
        [inputs, att_total],
        [gain_m],
        [],
        lambda values, lines, sides: (values[0] + values[1]) * lines[0],
    )

    there = ()
    gate_parts, up_parts = [[], []], [[], []]
    for which in range(2):
        for number, size in enumerate(unit_cuts):
            for parts, pair, order in (
                (gate_parts, gate_pair, order_a), (up_parts, up_pair, order_b)
            ):
                there = expert_product(
                    rows_m,
                    pair,
                    bounds_m,
                    [(size, [scatter_groups(order)[which]])],
                    windows,
                    there,
                    sum(unit_cuts[:number]),
                )[0]
                parts[number] += there
    passed, gate_terms, up_terms = [], [], []
    for number in range(len(unit_cuts)):
        there = tuple(passed)
        gate_terms.append(scatter_terms(*gate_parts[number], order_a, there, passed))
        up_terms.append(scatter_terms(*up_parts[number], order_b, there, passed))
    rms_m, logits_m = statistics(
        router_statistics([inputs, att_total], gain_m, router_m, passed)
    )
    gates_m = choice_gates(logits_m, named_m)
    row_gates_m = choice_rows(slots_m, half, gates_m.reshape(groups, TOPK, length))[..., None]
    row_rms_m = own_rows(slots_m, rms_m[0])
    active_parts, gating_all, upward_all, there = [], [], [], ()
    row_gates_grad, row_norms = 0.0, 0.0
    for number in range(len(unit_cuts)):
        active, grad_gating, grad_upward, dots, norms = unit_rows(
            gate_terms[number], up_terms[number], grad_act[number], row_rms_m, row_gates_m[0], there
        )
        there = [active]
        active_parts.append(active)
        row_gates_grad = row_gates_grad + dots[:, 0]
        row_norms = row_norms + norms[:, 0]
        gating_all.append(gather_pieces(grad_gating, order_a))
        upward_all.append(gather_pieces(grad_upward, order_b))
    side_there = [pieces[0][0] for pieces in gating_all + upward_all]
    active_all = [
        gather_pieces(late(value, *side_there), order)
        for value, order in zip(active_parts, orders)
    ]

    def router_part(
        row_gates_grad, row_norms, more, slots, gates, named, totals, logits, rms, earlier
    ):
        by_choice = [jnp.where(hit[0], row_gates_grad[:, None], 0.0) for hit in hits(slots[:1], half)]
        by_choice = [jnp.sum(one, axis=0) for one in by_choice]
        norms = [jnp.where(hit[0], row_norms[:, None], 0.0) for hit in hits(slots[:1], half)]
        norms = sum(jnp.sum(one, axis=0) for one in norms)
        packed = jnp.stack(by_choice + [norms]).reshape(TOPK + 1, owners, count)
        packed = jnp.transpose(packed, (1, 0, 2))
        packed = jnp.concatenate([packed[:, :TOPK], packed[:, TOPK:] + more], axis=1)
        packed = in_order(gather_directly(late(packed, *earlier)))
        by_choice = jnp.transpose(packed[:, :, :TOPK], (0, 2, 1, 3))
        norms = packed[:, :, TOPK]
        picked = gates * (by_choice - jnp.sum(gates * by_choice, axis=1, keepdims=True))
        picked = sum(
            jnp.where(one, picked[:, choice][:, :, None], 0.0) for choice, one in enumerate(named)
        )
        fraction = totals / (all_tokens * TOPK)
        weighting = (AUX_WEIGHT * EXPERTS / all_tokens) * fraction[:, None]
        probs = jax.nn.softmax(logits, axis=2)
        aux = probs * (weighting - jnp.sum(probs * weighting, axis=2, keepdims=True))
        balance = EXPERTS * EXPERTS * fraction * (jnp.sum(probs, axis=(0, 1, 3)) / all_tokens)
        picked = picked + aux / (owners * shards)
        norms = norms + jnp.sum(picked * logits, axis=2)
        return (picked * rms[:, :, None], total_small(norms, 1, shard_bits), balance)

    router_rows_m, inner_m, balance_m = router_part(
        row_gates_grad, row_norms, 0.0, slots_m, gates_m, named_m, totals_m, logits_m, rms_m,
        side_there,
    )
    carry = expert_product_back(
        [(gating_all[0], gate_pair, 0), (upward_all[0], up_pair, 0)], bounds_m, everything, windows
    )
    back_part = expert_product_back(
        [(gating_all[1], gate_pair, unit_cuts[0]), (upward_all[1], up_pair, unit_cuts[0])],
        bounds_m,
        everything,
        windows,
        carry=carry,
        ending=(columns_m, None, (router_rows_m, router_m), None),
    )
    active_first = [pieces[0][0] for pieces in active_all]

    def weight_grad(rows, parts, bounds, scale=None, earlier=()):
        own, other = expert_grads(rows, parts, bounds, everything, local_count, windows, scale, earlier)
        index = (1 - core) * (local_count - 1)

        def finish(earlier):
            return add_at(own, swap(other, "expert", 1), index, earlier)

        return other, finish

    def gate_grads(own):
        made["gate"] = weight_grad(rows_m, gating_all, bounds_m, earlier=[own])
        return [made["gate"][0]]

    def up_grads(own):
        made["up"] = weight_grad(rows_m, upward_all, bounds_m, earlier=[own])
        return [made["up"][0]] + active_first

    back_total = total_pair(back_part, shards, gate_grads, up_grads)
    back_m = [value.astype(F32) for value in back_total]

    shrink = rms_m * rms_m * inner_m / model_width
    shrink_pair = (shrink[:, 0, :, None], shrink[:, 1, :, None])
    grad_rows_a = dispatch(
        slots_a,
        half,
        [grad_out, back_total, inputs, att_total],
        [gain_m],
        [shrink_pair],
        lambda values, lines, sides: values[0]
        + values[1] * lines[0]
        - (values[2] + values[3]) * sides[0],
    )
    mix_parts = expert_product(grad_rows_a, out_pair, bounds_a, feature_plan, windows)
    mlp_part = expert_product_back(
        [(active_all[0], down_pair, 0), (active_all[1], down_pair, unit_cuts[0])],
        bounds_m,
        everything,
        windows,
        ending=(columns_m, row_gates_m, None, None),
        earlier=[mix_parts[0][0]],
    )
    grad_mix = jnp.concatenate(
        [term_sum(scatter_terms(*parts, order)) for parts, order in zip(mix_parts, orders)], axis=1
    ).astype(BF16)
    layer_own = mlp_part[0] + swap(mlp_part[1], "expert", 1)
    layer_block = middle[0] + lax.psum(layer_own, "shard").astype(F32)
    layer_pieces = spread_columns([layer_block[d].astype(BF16) for d in everything])
    grad_mlp_gain = sum(
        jnp.sum(one * two, axis=(0, 1)) for one, two in zip(back_m, middle)
    )
    grad_mlp_gain = lax.dynamic_slice_in_dim(grad_mlp_gain, core * part, part, 0)
    grad_queries, grad_keys, grad_values, row_gates_grad, row_norms = attention_backward(
        queries, keys, values, row_pos, key_pos, mixture, grad_mix, row_gates_a[0], row_rms_a,
        earlier=[layer_own],
    )
    grad_queries_all = gather_cuts(grad_queries, feature_cuts)

    sent_kv = jnp.stack([grad_keys[count:], grad_values[count:]]).astype(BF16)
    received_kv = swap(sent_kv, "expert", 1).astype(F32)
    own_kv, kv_norms = [], 0.0
    for c, (grad, held) in enumerate(zip((grad_keys, grad_values), key_value)):
        total = grad[:count] + received_kv[c]
        kv_norms = kv_norms + jnp.sum(total * held[:count].astype(F32), axis=-1)
        own_kv.append((total * own_rms[:, None]).astype(BF16))
    kv_norms = jnp.stack([kv_norms, jnp.zeros_like(kv_norms)])
    kv_terms = [
        sum(dot32("tf,kf->tk", own_kv[c], kv_all[c][b]) for c in range(2)) for b in range(owners)
    ]
    kv_terms = [
        core_order(*[term[:, d * part : (d + 1) * part] for term in kv_terms], axis=1).astype(BF16)
        for d in everything
    ]
    kv_back = jnp.stack(spread_columns(kv_terms))
    gate_grad, up_grad = made["gate"][1]([grad_queries]), made["up"][1]([grad_queries])
    router_rows_a, inner_a, balance_a = router_part(
        row_gates_grad[:, 0],
        row_norms[:, 0],
        kv_norms[:, None],
        slots_a,
        gates_a,
        named_a,
        totals_a,
        logits_a,
        rms_a,
        [pieces[0][0] for pieces in grad_queries_all],
    )
    back_part = expert_product_back(
        [(grad_queries_all[0], query_pair, 0), (grad_queries_all[1], query_pair, feature_cuts[0])],
        bounds_a,
        everything,
        windows,
        ending=(columns_a, None, (router_rows_a, router_a), None),
        earlier=kv_terms + [gate_grad, up_grad],
    )
    back_own = (back_part[0].astype(F32) + kv_back.astype(F32) / gain_a).astype(BF16)

    def down_grads(own):
        made["down"] = weight_grad(grad_rows_m, active_all, bounds_m, row_gates_m, earlier=[own])
        return [made["down"][0]]

    tail_parts = core_sum((back_own, back_part[1]), shards)
    back_a = shard_scatter(tail_parts, down_grads)
    grad_kv = [
        gather_rows(late(value, tail_parts[0]), order) for value, order in zip(own_kv, orders)
    ]
    layer_out = place_columns(layer_pieces, F32, [back_a])[0]
    back_there = back_a
    back_a = back_a.astype(F32)
    late_rows = [late(rows, back_there) for rows in (router_rows_a, router_rows_m)]
    grad_kv_weight = 0.0
    router_grads = 0.0
    for block in range(owners):
        scaled = inputs_f[block] * gain_a
        own_scaled = lax.dynamic_slice_in_dim(scaled, core * part, part, 2).astype(BF16)
        some_kv = [one if block == 0 else swap(one, "expert", 1) for one in grad_kv]
        grad_kv_weight = grad_kv_weight + jnp.stack(
            [dot32("dtk,dtf->kf", own_scaled, one) for one in some_kv], axis=1
        )
        one = jnp.einsum("det,dtk->ek", late_rows[0][:, block], scaled, precision=HIGHEST)
        two = jnp.einsum(
            "det,dtk->ek", late_rows[1][:, block], middle[block] * gain_m, precision=HIGHEST
        )
        router_grads = router_grads + jnp.concatenate([one, two])
    router_grads = total_small(router_grads, None, shard_bits)
    router_grads = lax.dynamic_slice_in_dim(router_grads, core * part, part, 1)
    own_inputs = shard_part(inputs_f[0], 1)
    grad_att_gain = total_small(jnp.sum(back_a * own_inputs, axis=(0, 1)), None, shard_bits)
    grad_att_gain = lax.dynamic_slice_in_dim(grad_att_gain, core * part, part, 0)

    def own_part(value):
        return shard_part(value, 1)

    grad_middle = (
        own_part(grad_out[0]).astype(F32)
        + own_part(back_total[0]).astype(F32) * gain_m
        - own_part(middle[0]) * own_part(shrink[:, 0])[..., None]
    )
    shrink_a = own_part(rms_a[:, 0] * rms_a[:, 0] * inner_a[:, 0] / model_width)
    grad_tokens = grad_middle + back_a * gain_a - own_inputs * shrink_a[..., None]
    grad_tokens = place_columns(
        spread_columns([grad_tokens[d].astype(BF16) for d in everything])
    )
    rows_there = grad_tokens
    query_finish = weight_grad(rows_a, grad_queries_all, bounds_a, earlier=[rows_there])[1]
    out_finish = weight_grad(
        grad_rows_a, mixture_all, bounds_a, row_gates_a, earlier=[rows_there]
    )[1]
    grad_tokens = shard_gather(grad_tokens, F32)[0]

    balance_terms = jnp.stack([balance_a, balance_m])
    aux_loss = (jnp.sum(balance_terms) / EXPERTS).reshape(1)
    return (
        layer_out,
        aux_loss,
        grad_tokens,
        grad_att_gain,
        router_grads[:EXPERTS].T,
        grad_kv_weight,
        query_finish([back_a]),
        out_finish([back_a]),
        grad_mlp_gain,
        router_grads[EXPERTS:].T,
        gate_grad,
        up_grad,
        made["down"][1]([back_a]),
        balance_terms,
    )


def solution(mesh):
    rows = P(("dp", "expert"), None)
    vector = P(("dp", "expert"))
    shared = P(("dp", "expert"), None, "shard")
    weight = P("expert", "dp", "shard")
    return jax.shard_map(
        per_device,
        mesh=mesh,
        in_specs=(
            rows, vector, rows, shared, weight, weight, vector, rows,
            weight, weight, weight, rows, rows, rows,
        ),
        out_specs=(
            rows, P(), rows, vector, rows, shared, weight, weight,
            vector, rows, weight, weight, weight, P(),
        ),
        check_vma=False,
    )
```

```python
import jax
import jax.numpy as jnp
from jax import lax
from jax.experimental import pallas as pl
from jax.experimental.pallas import tpu as pltpu
from jax.sharding import PartitionSpec as P

HEAD_DIM = 128
EXPERTS = 8
TOPK = 2
EPSILON = 1e-06
AUX_WEIGHT = 0.01
MASKED = -1e30
HIGHEST = lax.Precision.HIGHEST
BF16 = jnp.bfloat16
F32 = jnp.float32
TOGETHER = 4


def dot32(spec, left, right):
    return jnp.einsum(spec, left, right, preferred_element_type=F32)


def swap(value, axis, flip):
    size = lax.axis_size(axis)
    return lax.ppermute(value, axis, [(i, i ^ flip) for i in range(size)])


def marker(*earlier):
    lasts = [value[(-1,) * value.ndim].astype(F32) for value in earlier]
    return sum((last == jnp.inf).astype(jnp.int32) for last in lasts)


def late(value, *earlier):
    return value + marker(*earlier).astype(value.dtype)


def bits_in(size):
    count = 0
    while (1 << count) < size:
        count += 1
    return count


def split_bits(value, axis, bits):
    shape = value.shape
    return value.reshape(shape[:axis] + (2,) * bits + shape[axis + 1 :])


def join_bits(value, axis, bits):
    shape = value.shape
    return value.reshape(shape[:axis] + (1 << bits,) + shape[axis + bits :])


def gather_pieces(own, order):
    value, places = own[None], [0]
    for step, bit in enumerate(reversed(order)):
        received = swap(value, "dp", 1 << bit)
        others = [place | (1 << bit) for place in places]
        if step == len(order) - 1:
            return [(value, places), (received, others)]
        value, places = jnp.concatenate([value, received]), places + others
    return [(value, places)]


def gather_directly(own):
    groups = lax.axis_size("dp")
    return [(own[None], [0])] + [(swap(own, "dp", d)[None], [d]) for d in range(1, groups)]


def in_order(pieces):
    found = {}
    for array, places in pieces:
        for number, place in enumerate(places):
            found[place] = array[number]
    return jnp.stack([found[d] for d in range(len(found))])


def gather_rows(own, order):
    return in_order(gather_pieces(own, order))


def scatter_groups(order):
    places = range(1 << len(order))
    first = 1 << order[0]
    return [
        tuple(d for d in places if d & first),
        tuple(d for d in places if not d & first),
    ]


def scatter_terms(sent, kept, order, earlier=(), passed=None):
    bits = len(order)
    received = swap(sent, "dp", 1 << order[0])
    held = [bit for bit in range(bits - 1, -1, -1) if bit != order[0]]
    terms = [kept, received]
    for bit in order[1:]:
        if len(held) == 1:
            send = added(terms, earlier, 1)
            if passed is not None:
                passed.append(send)
            return terms + [swap(send, "dp", 1 << bit)]
        parts = [split_bits(term, 0, len(held)) for term in terms]
        place = held.index(bit)
        parts = [jnp.moveaxis(term, place, 0) for term in parts]
        send = sum(term[1].astype(F32) for term in parts).astype(BF16)
        send = send.reshape((-1,) + kept.shape[1:])
        terms = [term[0].reshape(send.shape) for term in parts] if len(held) > 1 else terms
        terms = terms + [swap(send, "dp", 1 << bit)]
        held = [other for other in held if other != bit]
    return terms


def term_sum(terms):
    return sum(term[0].astype(F32) for term in terms)


def shard_part(value, axis):
    size = value.shape[axis] // lax.axis_size("shard")
    return lax.dynamic_slice_in_dim(value, lax.axis_index("shard") * size, size, axis)


def added(terms, earlier=(), number=None):
    shape = terms[0].shape
    if number is None:
        steps, out_shape = shape[0], shape
        spec = pl.BlockSpec((1,) + shape[1:], lambda i: (i, 0, 0))
        out_spec = spec
    else:
        steps, out_shape = max(1, shape[1] // 256), (1,) + shape[1:]
        block = (1, shape[1] // steps, shape[2])
        spec = pl.BlockSpec(block, lambda i: (number, i, 0))
        out_spec = pl.BlockSpec(block, lambda i: (0, i, 0))

    def kernel(*refs):
        total = refs[0][...].astype(F32)
        for more in refs[1 : len(terms)]:
            total = total + more[...].astype(F32)
        refs[-1][...] = total.astype(BF16)

    size = terms[0].size // (1 if number is None else shape[0])
    return pl.pallas_call(
        kernel,
        grid=(steps,),
        in_specs=[spec] * len(terms) + anywhere(earlier),
        out_specs=out_spec,
        out_shape=jax.ShapeDtypeStruct(out_shape, BF16),
        **params(size * len(terms), 2 * size * (len(terms) + 1), memory=8),
    )(*terms, *earlier)


def split_sum(one, two, shards, earlier=()):
    groups, count, width = one.shape
    size = count // shards
    whole = pl.BlockSpec((1, count, width), lambda i, _: (i, 0, 0))

    def kernel(index_ref, one_ref, two_ref, *refs):
        for number, out in enumerate(refs[len(earlier) :]):
            place = pl.ds(pl.multiple_of((index_ref[0] ^ number) * size, size), size)
            total = one_ref[0, place, :].astype(F32) + two_ref[0, place, :].astype(F32)
            out[0] = total.astype(BF16)

    return pl.pallas_call(
        kernel,
        grid_spec=pltpu.PrefetchScalarGridSpec(
            num_scalar_prefetch=1,
            grid=(groups,),
            in_specs=[whole] * 2 + anywhere(earlier),
            out_specs=[pl.BlockSpec((1, size, width), lambda i, _: (i, 0, 0))] * shards,
        ),
        out_shape=[jax.ShapeDtypeStruct((groups, size, width), BF16)] * shards,
        **params(one.size, 6 * one.size, memory=8),
    )(lax.axis_index("shard").reshape(1), one, two, *earlier)


def joined(parts, kind, earlier=()):
    groups, size, width = parts[0].shape
    shards = len(parts)

    def kernel(index_ref, *refs):
        out = refs[-1]
        for number in range(shards):
            place = pl.ds(pl.multiple_of((index_ref[0] ^ number) * size, size), size)
            out[0, place, :] = refs[number][0].astype(kind)

    return pl.pallas_call(
        kernel,
        grid_spec=pltpu.PrefetchScalarGridSpec(
            num_scalar_prefetch=1,
            grid=(groups,),
            in_specs=[pl.BlockSpec((1, size, width), lambda i, _: (i, 0, 0))] * shards + anywhere(earlier),
            out_specs=pl.BlockSpec((1, size * shards, width), lambda i, _: (i, 0, 0)),
        ),
        out_shape=jax.ShapeDtypeStruct((groups, size * shards, width), kind),
        **params(0, 8 * parts[0].size * shards, memory=16),
    )(lax.axis_index("shard").reshape(1), *parts, *earlier)


def stacked(arrays, earlier=()):
    rows, width = arrays[0].shape

    def kernel(*refs):
        for number in range(len(arrays)):
            refs[-1][number * rows : (number + 1) * rows] = refs[number][...]

    return pl.pallas_call(
        kernel,
        in_specs=[pl.BlockSpec(memory_space=pltpu.VMEM)] * len(arrays) + anywhere(earlier),
        out_specs=pl.BlockSpec(memory_space=pltpu.VMEM),
        out_shape=jax.ShapeDtypeStruct((rows * len(arrays), width), arrays[0].dtype),
        **params(0, 4 * arrays[0].size * len(arrays), memory=16),
    )(*arrays, *earlier)


def shard_scatter(parts, pin=None):
    far = swap(parts[3], "shard", 1)
    near = swap(parts[1], "shard", 1)
    passed = parts[2] + far
    side = swap(passed, "shard", 2)
    return added([parts[0], near, side], [] if pin is None else pin(passed))


def shard_gather(own, kind=BF16, pin=None):
    count = own.shape[0]
    both = jnp.concatenate([own, swap(own, "shard", 2)])
    more = swap(both, "shard", 1)
    parts = [both[:count], more[:count], both[count:], more[count:]]
    return joined(parts, kind, [] if pin is None else pin(own))


def core_sum(pair, shards, earlier=()):
    return split_sum(pair[0], swap(pair[1], "expert", 1), shards, earlier)


def total_pair(partial_pair, shards, scatter_pin=None, gather_pin=None, earlier=()):
    own = shard_scatter(core_sum(partial_pair, shards, earlier), scatter_pin)
    whole = shard_gather(own, BF16, gather_pin)
    return (whole, swap(whole, "expert", 1))


def total_small(value, block_axis, bits):
    received = swap(value, "expert", 1)
    if block_axis is not None:
        received = jnp.flip(received, axis=block_axis)
    value = value + received
    for bit in range(bits):
        value = value + swap(value, "shard", 1 << bit)
    return value


def both_blocks(own, axis):
    return jnp.stack([own, swap(own, "expert", 1)], axis=axis)


def spread_columns(pieces):
    return [pieces[0]] + [swap(pieces[d], "dp", d) for d in range(1, len(pieces))]


def place_columns(pieces, kind=BF16, earlier=()):
    rows, width = pieces[0].shape

    def kernel(index_ref, *refs):
        for number in range(len(pieces)):
            place = pl.ds(pl.multiple_of((index_ref[0] ^ number) * width, 128), width)
            refs[-1][0, :, place] = refs[number][...].astype(kind)

    shape = (1, rows, width * len(pieces))
    return pl.pallas_call(
        kernel,
        grid_spec=pltpu.PrefetchScalarGridSpec(
            num_scalar_prefetch=1,
            grid=(1,),
            in_specs=[pl.BlockSpec((rows, width), lambda *_: (0, 0))] * len(pieces)
            + anywhere(earlier),
            out_specs=pl.BlockSpec(shape, lambda *_: (0, 0, 0)),
        ),
        out_shape=jax.ShapeDtypeStruct(shape, kind),
        **params(0, 6 * rows * width * len(pieces), memory=12),
    )(lax.axis_index("dp").reshape(1), *pieces, *earlier)


def product(left, right, dims=((1,), (0,))):
    return lax.dot_general(left, right, (dims, ((), ())), preferred_element_type=F32)


def window_of(bounds_ref, sequence, group, rows, window):
    low = bounds_ref[sequence, 2 * group]
    high = bounds_ref[sequence, 2 * group + 1]
    base = pl.multiple_of(jnp.minimum(jnp.bitwise_and(low, -16), rows - window), 16)
    at = base + lax.broadcasted_iota(jnp.int32, (window, 1), 0)
    return (base, (at >= low) & (at < high))


def whole_block(array):
    zeros = (0,) * len(array.shape)
    return pl.BlockSpec(array.shape, lambda *_: zeros, pipeline_mode=pl.Buffered(1))


def anywhere(arrays):
    return [pl.BlockSpec(memory_space=pl.ANY) for _ in arrays]


def params(flops, moved, exps=0, memory=24):
    return dict(
        compiler_params=pltpu.CompilerParams(vmem_limit_bytes=memory << 20),
        cost_estimate=pl.CostEstimate(flops=flops, bytes_accessed=moved, transcendentals=exps),
    )


def group_specs(pair):
    own, other = pair
    last = own.shape[0] - 1
    return [
        pl.BlockSpec((1,) + own.shape[1:], lambda g, *_: (jnp.minimum(g, last), 0, 0)),
        whole_block(other),
    ]


def each_group(groups, windows, step):
    group = pl.program_id(0)

    @pl.when(group < groups - 1)
    def _():
        step(group, windows[0], 0)

    @pl.when(group == groups - 1)
    def _():
        step(group, windows[1], 1)


def chosen_rows(ref, index, base, window, mine, scale=None):
    rows = ref[index, pl.ds(base, window), :]
    keep = jnp.where(mine, 1.0, 0.0)
    if scale is None:
        return rows * keep.astype(BF16)
    return (rows.astype(F32) * (scale[index, pl.ds(base, window), :] * keep)).astype(BF16)


def expert_product(rows, pair, bounds, cuts, windows, earlier=(), first=0):
    sequences = sorted(d for group in cuts[0][1] for d in group)
    if len(sequences) > TOGETHER:
        found = [{} for _ in cuts]
        for at in range(0, len(sequences), TOGETHER):
            some = sequences[at : at + TOGETHER]
            split = [(size, [(d,) for d in some]) for size, _ in cuts]
            parts = expert_product(rows, pair, bounds, split, windows, earlier, first)
            for place, part in zip(found, parts):
                place.update({d: one[0] for d, one in zip(some, part)})
        return [
            [jnp.stack([place[d] for d in group]) for group in wanted]
            for place, (_, wanted) in zip(found, cuts)
        ]
    count, depth = rows.shape[1:]
    groups, width = pair[0].shape[0] + 1, sum(size for size, _ in cuts)
    amount = len(sequences)

    def kernel(bounds_ref, rows_ref, *refs):
        weights, outs = refs[:2], refs[2 + len(earlier) :]

        @pl.when(pl.program_id(0) == 0)
        def _():
            for out in outs:
                out[...] = jnp.zeros_like(out)

        def step(group, window, which):
            bases, picked = [], []
            for sequence in sequences:
                base, mine = window_of(bounds_ref, sequence, group, count, window)
                bases.append(base)
                picked.append(chosen_rows(rows_ref, sequence, base, window, mine))
            left = jnp.concatenate(picked, axis=0)
            start = first
            number = 0
            for size, wanted in cuts:
                part = product(left, weights[which][0, :, start : start + size]).astype(BF16)
                for some in wanted:
                    for index, sequence in enumerate(some):
                        place = sequences.index(sequence)
                        at = (index, pl.ds(bases[place], window), slice(None))
                        outs[number][at] = (
                            outs[number][at] + part[place * window : (place + 1) * window]
                        )
                    number += 1
                start += size

        each_group(groups, windows, step)

    shapes = [
        jax.ShapeDtypeStruct((len(some), count, size), BF16) for size, wanted in cuts for some in wanted
    ]
    outs = pl.pallas_call(
        kernel,
        grid_spec=pltpu.PrefetchScalarGridSpec(
            num_scalar_prefetch=1,
            grid=(groups,),
            in_specs=[whole_block(rows)] + group_specs(pair) + anywhere(earlier),
            out_specs=[whole_block(shape) for shape in shapes],
        ),
        out_shape=shapes,
        **params(
            2 * amount * groups * windows[0] * depth * width,
            2 * (pair[0].size + pair[1].size + amount * count * (depth + width)),
        ),
    )(bounds, rows, *pair, *earlier)
    outs = list(outs)
    return [[outs.pop(0) for _ in wanted] for _, wanted in cuts]


def pieces_at(pieces, sequences):
    if len(sequences) == sum(len(places) for _, places in pieces):
        return pieces
    whole = in_order(pieces)
    return [(whole[sequences[0] : sequences[-1] + 1], sequences)]


def flat_pieces(pieces, arrays, specs):
    found = {}
    for array, places in pieces:
        for number, place in enumerate(places):
            found[place] = (len(arrays), number)
        arrays.append(array)
        specs.append(whole_block(array))
    return found


def expert_product_back(parts, bounds, sequences, windows, carry=None, ending=None, earlier=()):
    total_count = len(sequences)
    if total_count > TOGETHER:
        done = []
        for at in range(0, total_count, TOGETHER):
            some = sequences[at : at + TOGETHER]
            cut = slice(at, at + TOGETHER)
            some_parts = [(pieces_at(pieces, some), pair, start) for pieces, pair, start in parts]
            some_ending = None
            if ending is not None:
                slots, gates, router, extra = ending
                some_ending = (
                    slots[cut],
                    None if gates is None else gates[cut],
                    None if router is None else (router[0][cut], router[1]),
                    None if extra is None else tuple(one[cut] for one in extra),
                )
            renamed = [
                ([(array, list(range(len(places)))) for array, places in pieces], pair, start)
                for pieces, pair, start in some_parts
            ]
            done.append(
                expert_product_back(
                    renamed,
                    bounds[cut],
                    list(range(len(some))),
                    windows,
                    None if carry is None else carry[cut],
                    some_ending,
                    earlier,
                )
            )
        if ending is None:
            return jnp.concatenate(done)
        return tuple(jnp.concatenate(one) for one in zip(*done))

    own = parts[0][1][0]
    groups, depth = own.shape[0] + 1, own.shape[1]
    count = parts[0][0][0][0].shape[1]
    arrays, specs, plan, held = [], [], [], {}
    flops, moved = 0, 4 * total_count * count * depth
    for pieces, pair, start in parts:
        if id(pair) not in held:
            held[id(pair)] = len(arrays)
            arrays += list(pair)
            specs += group_specs(pair)
            moved += 2 * (pair[0].size + pair[1].size)
        size = pieces[0][0].shape[2]
        plan.append((flat_pieces(pieces, arrays, specs), held[id(pair)], start, size))
        flops += 2 * total_count * groups * windows[0] * size * depth
        moved += 2 * total_count * count * size
    places = {}

    def operand(name, array):
        places[name] = len(arrays)
        arrays.append(array)
        specs.append(whole_block(array))

    if carry is not None:
        operand("carry", carry)
    if ending is not None:
        slots, gates, router, extra = ending
        operand("slots", slots)
        if gates is not None:
            operand("gates", gates)
        if router is not None:
            operand("router_rows", router[0])
            operand("router", router[1])
        if extra is not None:
            operand("extra0", extra[0])
            operand("extra1", extra[1])
    arrays += list(earlier)
    specs += anywhere(earlier)

    def kernel(bounds_ref, *refs):
        ins, outs = refs[: len(arrays)], refs[len(arrays) :]
        total = outs[-1]

        def step(group, window, which):
            bases, masks, sums = [], [], None
            for sequence in sequences:
                base, mine = window_of(bounds_ref, sequence, group, count, window)
                bases.append(base)
                masks.append(mine)
            for found, weight_at, start, size in plan:
                left = jnp.concatenate(
                    [
                        ins[found[sequence][0]][found[sequence][1], pl.ds(base, window), :]
                        for sequence, base in zip(sequences, bases)
                    ],
                    axis=0,
                )
                weight = ins[weight_at + which][0, :, start : start + size]
                part = product(left, weight, ((1,), (1,)))
                sums = part if sums is None else sums + part
            for number, (base, mine) in enumerate(zip(bases, masks)):
                place = (number, pl.ds(base, window), slice(None))
                part = sums[number * window : (number + 1) * window]
                total[place] = jnp.where(mine, part, total[place])

        each_group(groups, windows, step)

        @pl.when(pl.program_id(0) == groups - 1)
        def _():
            if ending is None:
                if carry is not None:
                    total[...] += ins[places["carry"]][...]
                return
            tokens = outs[0].shape[1]
            for number in range(total_count):
                rows = total[number]
                if carry is not None:
                    rows = rows + ins[places["carry"]][number]
                if gates is not None:
                    rows = rows * ins[places["gates"]][number]
                rows = rows.astype(BF16)
                for block in range(2):
                    numbers = lax.broadcasted_iota(jnp.int32, (tokens, count), 1)
                    hit = None
                    for choice in range(TOPK):
                        column = ins[places["slots"]][
                            number, block * tokens : (block + 1) * tokens, choice : choice + 1
                        ]
                        one = column == numbers
                        hit = one if hit is None else hit | one
                    value = product(jnp.where(hit, 1.0, 0.0).astype(BF16), rows)
                    if router is not None:
                        value = value + product(
                            ins[places["router_rows"]][number, block].astype(BF16),
                            ins[places["router"]][...].astype(BF16),
                            ((0,), (0,)),
                        )
                    if extra is not None:
                        value = value + ins[places["extra%d" % block]][number].astype(F32)
                    outs[block][number] = value.astype(BF16)

    if ending is None:
        out_specs = [whole_block(jax.ShapeDtypeStruct((total_count, count, depth), F32))]
        out_shape = [jax.ShapeDtypeStruct((total_count, count, depth), F32)]
        scratch = []
    else:
        tokens = ending[0].shape[1] // 2
        out_shape = [jax.ShapeDtypeStruct((total_count, tokens, depth), BF16)] * 2
        out_specs = [whole_block(one) for one in out_shape]
        scratch = [pltpu.VMEM((total_count, count, depth), F32)]
    result = pl.pallas_call(
        kernel,
        grid_spec=pltpu.PrefetchScalarGridSpec(
            num_scalar_prefetch=1,
            grid=(groups,),
            in_specs=specs,
            out_specs=out_specs,
            scratch_shapes=scratch,
        ),
        out_shape=out_shape,
        **params(flops, moved, memory=36),
    )(bounds, *arrays)
    return result[0] if ending is None else tuple(result)


def expert_grads(rows, parts, bounds, sequences, local_count, windows, scale=None, earlier=()):
    if len(sequences) > TOGETHER:
        done = []
        for at in range(0, len(sequences), TOGETHER):
            some = sequences[at : at + TOGETHER]
            cut = slice(at, at + TOGETHER)
            renamed = [
                [(array, list(range(len(some)))) for array, _ in pieces_at(pieces, some)]
                for pieces in parts
            ]
            done.append(
                expert_grads(
                    rows[cut], renamed, bounds[cut], list(range(len(some))), local_count, windows,
                    None if scale is None else scale[cut], earlier,
                )
            )
        return tuple(sum(one[1:], one[0]) for one in zip(*done))
    amount = len(sequences)
    count, depth = rows.shape[1:]
    sizes = [pieces[0][0].shape[2] for pieces in parts]
    width = sum(sizes)
    groups = local_count + 1
    arrays, specs = [rows], [whole_block(rows)]
    if scale is not None:
        arrays.append(scale)
        specs.append(whole_block(scale))
    plan = [flat_pieces(pieces, arrays, specs) for pieces in parts]
    arrays += list(earlier)
    specs += anywhere(earlier)

    def kernel(bounds_ref, *refs):
        ins, outs = refs[: len(arrays)], refs[len(arrays) :]

        def step(group, window, which):
            bases, picked = [], []
            for sequence in sequences:
                base, mine = window_of(bounds_ref, sequence, group, count, window)
                bases.append(base)
                picked.append(
                    chosen_rows(ins[0], sequence, base, window, mine, None if scale is None else ins[1])
                )
            left = jnp.concatenate(picked, axis=0)
            start = 0
            for found, size in zip(plan, sizes):
                right = jnp.concatenate(
                    [
                        ins[found[sequence][0]][found[sequence][1], pl.ds(base, window), :]
                        for sequence, base in zip(sequences, bases)
                    ],
                    axis=0,
                )
                part = product(left, right, ((0,), (0,)))
                outs[which][0, :, start : start + size] = part.astype(outs[which].dtype)
                start += size

        each_group(groups, windows, step)

    return pl.pallas_call(
        kernel,
        grid_spec=pltpu.PrefetchScalarGridSpec(
            num_scalar_prefetch=1,
            grid=(groups,),
            in_specs=specs,
            out_specs=[
                pl.BlockSpec((1, depth, width), lambda g, *_: (jnp.minimum(g, local_count - 1), 0, 0)),
                whole_block(jax.ShapeDtypeStruct((1, depth, width), BF16)),
            ],
        ),
        out_shape=[
            jax.ShapeDtypeStruct((local_count, depth, width), F32),
            jax.ShapeDtypeStruct((1, depth, width), BF16),
        ],
        **params(
            2 * amount * groups * windows[0] * depth * width,
            2 * amount * count * (depth + width) + 4 * groups * depth * width,
            memory=32,
        ),
    )(bounds, *arrays)


def add_at(array, more, index, earlier=()):
    _, depth, width = array.shape
    step = depth // 4 if depth % 64 == 0 else depth
    spec = pl.BlockSpec((1, step, width), lambda i, at: (at[0], i, 0))

    def kernel(index_ref, array_ref, more_ref, *refs):
        refs[-1][...] = array_ref[...] + more_ref[...].astype(F32)

    return pl.pallas_call(
        kernel,
        grid_spec=pltpu.PrefetchScalarGridSpec(
            num_scalar_prefetch=1,
            grid=(depth // step,),
            in_specs=[spec, pl.BlockSpec((1, step, width), lambda i, _: (0, i, 0))] + anywhere(earlier),
            out_specs=spec,
        ),
        out_shape=jax.ShapeDtypeStruct(array.shape, F32),
        input_output_aliases={1: 0},
        **params(depth * width, 10 * depth * width, memory=12),
    )(index.reshape(1), array, more, *earlier)


def slot_hits(slots_ref, number, block, tokens, rows):
    numbers = lax.broadcasted_iota(jnp.int32, (rows, tokens), 0)
    hit = None
    for choice in range(TOPK):
        line = slots_ref[number, choice : choice + 1, block * tokens : (block + 1) * tokens]
        one = line == numbers
        hit = one if hit is None else hit | one
    return jnp.where(hit, 1.0, 0.0).astype(BF16)


def dispatch(slots, rows, pairs, vectors, columns, function, earlier=()):
    groups, tokens, width = pairs[0][0].shape
    arrays = [slots]
    specs = [pl.BlockSpec((1,) + slots.shape[1:], lambda i: (i, 0, 0))]
    for pair in pairs:
        arrays += list(pair)
        specs += [pl.BlockSpec((1, tokens, width), lambda i: (i, 0, 0))] * 2
    for array in columns:
        arrays.append(array)
        specs.append(pl.BlockSpec((1, 2, tokens), lambda i: (i, 0, 0)))
    arrays += list(vectors)
    specs += [whole_block(vector) for vector in vectors]
    arrays += list(earlier)
    specs += anywhere(earlier)

    def kernel(slots_ref, *refs):
        out = refs[-1]
        total = None
        for block in range(2):
            at = 0
            values, sides = [], []
            for _ in pairs:
                values.append(refs[at + block][0].astype(F32))
                at += 2
            for _ in columns:
                line = refs[at][0, block : block + 1, :]
                down = lax.broadcasted_iota(jnp.int32, (tokens, tokens), 0)
                across = lax.broadcasted_iota(jnp.int32, (tokens, tokens), 1)
                sides.append(
                    jnp.sum(jnp.where(down == across, line, 0.0), axis=1, keepdims=True)
                )
                at += 1
            lines = [refs[at + number][...] for number in range(len(vectors))]
            value = function(values, lines, sides).astype(BF16)
            part = product(slot_hits(slots_ref, 0, block, tokens, rows), value)
            total = part if total is None else total + part
        out[0] = total.astype(BF16)

    return pl.pallas_call(
        kernel,
        grid=(groups,),
        in_specs=specs,
        out_specs=pl.BlockSpec((1, rows, width), lambda i: (i, 0, 0)),
        out_shape=jax.ShapeDtypeStruct((groups, rows, width), BF16),
        **params(4 * groups * rows * tokens * width, 2 * groups * width * (rows + 2 * tokens * len(pairs))),
    )(*arrays)


def unit_rows(gate_terms, up_terms, grad_terms, scale, gates, earlier=()):
    count, width = gate_terms[0].shape[1:]
    step = min(count, 128)
    tile = pl.BlockSpec((step, width), lambda i: (i, 0))
    term = pl.BlockSpec((None, step, width), lambda i: (0, i, 0))
    column = pl.BlockSpec((step, 1), lambda i: (i, 0))
    lists = (gate_terms, up_terms, grad_terms)
    amount = sum(len(terms) for terms in lists)

    def kernel(*refs):
        scale_ref, gates_ref = refs[amount : amount + 2]
        active_out, gating_out, upward_out, dots_out, norms_out = refs[-5:]
        sums, at = [], 0
        for terms in lists:
            total = refs[at][...].astype(F32)
            for more in refs[at + 1 : at + len(terms)]:
                total = total + more[...].astype(F32)
            sums.append(total)
            at += len(terms)
        scale_rows = scale_ref[...]
        gating, upward, grad = sums[0] * scale_rows, sums[1] * scale_rows, sums[2]
        sigma = 1.0 / (1.0 + jnp.exp(-gating))
        silu = gating * sigma
        active = silu * upward
        active_out[...] = active.astype(BF16)
        dots_out[...] = jnp.sum(grad * active, axis=1, keepdims=True)
        grad = grad * gates_ref[...]
        grad_gating = grad * upward * sigma * (1.0 + gating * (1.0 - sigma))
        grad_upward = grad * silu
        norms_out[...] = jnp.sum(grad_gating * gating + grad_upward * upward, axis=1, keepdims=True)
        gating_out[...] = (grad_gating * scale_rows).astype(BF16)
        upward_out[...] = (grad_upward * scale_rows).astype(BF16)

    return pl.pallas_call(
        kernel,
        grid=(count // step,),
        in_specs=[term] * amount + [column] * 2 + anywhere(earlier),
        out_specs=[tile] * 3 + [column] * 2,
        out_shape=[jax.ShapeDtypeStruct((count, width), BF16)] * 3
        + [jax.ShapeDtypeStruct((count, 1), F32)] * 2,
        **params(20 * count * width, 18 * count * width, count * width),
    )(*gate_terms, *up_terms, *grad_terms, scale, gates, *earlier)


def router_statistics(pairs, gain, router, earlier=()):
    groups, tokens, width = pairs[0][0].shape
    rows = 2 * EXPERTS
    block = pl.BlockSpec((1, tokens, width), lambda i: (i, 0, 0))
    amount = 2 * len(pairs)

    def kernel(*refs):
        gain_ref, router_ref, out = refs[amount], refs[amount + 1], refs[-1]
        for number in range(2):
            value = refs[number][0].astype(F32)
            for more in range(1, len(pairs)):
                value = value + refs[2 * more + number][0].astype(F32)
            scaled = (value * gain_ref[...]).astype(BF16)
            out[0, number, :EXPERTS] = product(router_ref[...].astype(BF16), scaled, ((1,), (1,)))
            squares = value * value
            high = squares.astype(BF16)
            rest = (squares - high.astype(F32)).astype(BF16)
            ones = jnp.ones((EXPERTS, width), BF16)
            out[0, number, EXPERTS:] = product(ones, high, ((1,), (1,))) + product(
                ones, rest, ((1,), (1,))
            )

    return pl.pallas_call(
        kernel,
        grid=(groups,),
        in_specs=[block] * amount + [whole_block(gain), whole_block(router)] + anywhere(earlier),
        out_specs=pl.BlockSpec((1, 2, rows, tokens), lambda i: (i, 0, 0, 0)),
        out_shape=jax.ShapeDtypeStruct((groups, 2, rows, tokens), F32),
        **params(8 * rows * groups * tokens * width, 2 * amount * groups * tokens * width, memory=12),
    )(*(one for pair in pairs for one in pair), gain, router, *earlier)


def softmax_rows(queries, keys, row_pos, key_pos):
    scores = product(queries, keys, ((1,), (1,))) * HEAD_DIM ** (-0.5)
    scores = jnp.where(key_pos <= row_pos, scores, MASKED)
    expo = jnp.exp(scores - jnp.max(scores, axis=1, keepdims=True))
    return expo / jnp.sum(expo, axis=1, keepdims=True)


def attention_calls(count, length, features):
    heads = features // HEAD_DIM
    rows = pl.BlockSpec((count, HEAD_DIM), lambda h: (0, h))
    places = pl.BlockSpec((length, HEAD_DIM), lambda h: (0, h))
    column = pl.BlockSpec((count, 1), lambda h: (0, 0))
    line = pl.BlockSpec((1, length), lambda h: (0, 0))

    def forward_kernel(queries, keys, values, row_pos, key_pos, *refs):
        probs = softmax_rows(queries[...], keys[...], row_pos[...], key_pos[...])
        refs[-1][...] = product(probs.astype(BF16), values[...]).astype(BF16)

    def forward(*arrays, earlier=()):
        return pl.pallas_call(
            forward_kernel,
            grid=(heads,),
            in_specs=[rows, places, places, column, line] + anywhere(earlier),
            out_specs=rows,
            out_shape=jax.ShapeDtypeStruct((count, features), BF16),
            **params(4 * count * length * features, 8 * count * features, heads * count * length),
        )(*arrays, *earlier)

    def backward_kernel(
        queries, keys, values, row_pos, key_pos, mixture, grad_mix, gates, scale, *refs
    ):
        grad_queries, grad_keys, grad_values, grad_gates, norms = refs[-5:]
        probs = softmax_rows(queries[...], keys[...], row_pos[...], key_pos[...])
        grad_raw = grad_mix[...].astype(F32)
        gate_part = jnp.sum(grad_raw * mixture[...].astype(F32), axis=1, keepdims=True)
        grad_out = (grad_raw * gates[...]).astype(BF16)
        grad_values[...] = product(probs.astype(BF16), grad_out, ((0,), (0,)))
        grad_probs = product(grad_out, values[...], ((1,), (1,)))
        inner = jnp.sum(probs * grad_probs, axis=1, keepdims=True)
        grad_scores = (probs * (grad_probs - inner)).astype(BF16)
        grad_keys[...] = product(grad_scores, queries[...], ((0,), (0,))) * HEAD_DIM ** (-0.5)
        grad = product(grad_scores, keys[...]) * HEAD_DIM ** (-0.5)
        norm_part = jnp.sum(grad * queries[...].astype(F32), axis=1, keepdims=True)
        grad_queries[...] = (grad * scale[...]).astype(BF16)

        @pl.when(pl.program_id(0) == 0)
        def _():
            grad_gates[...] = gate_part
            norms[...] = norm_part

        @pl.when(pl.program_id(0) > 0)
        def _():
            grad_gates[...] += gate_part
            norms[...] += norm_part

    def backward(*arrays, earlier=()):
        return pl.pallas_call(
            backward_kernel,
            grid=(heads,),
            in_specs=[rows, places, places, column, line, rows, rows, column, column]
            + anywhere(earlier),
            out_specs=[rows, places, places, column, column],
            out_shape=[
                jax.ShapeDtypeStruct((count, features), BF16),
                jax.ShapeDtypeStruct((length, features), F32),
                jax.ShapeDtypeStruct((length, features), F32),
                jax.ShapeDtypeStruct((count, 1), F32),
                jax.ShapeDtypeStruct((count, 1), F32),
            ],
            **params(10 * count * length * features, 20 * count * features, heads * count * length, memory=58),
        )(*arrays, *earlier)

    return forward, backward


def route_tables(routes, core, local_count, half):
    sequences, blocks, _, count = routes.shape
    experts = jnp.arange(EXPERTS, dtype=jnp.int32)[:, None]
    named = [routes[:, :, choice : choice + 1] == experts for choice in range(TOPK)]
    member = named[0]
    for more in named[1:]:
        member = member | more
    steps = jnp.arange(count, dtype=jnp.int32)
    before = (steps[:, None] < steps[None, :]).astype(BF16)
    ranks = dot32("dbet,tu->dbeu", member.astype(BF16), before)
    counts = jnp.sum(member.astype(F32), axis=3)
    first_counts = jnp.where(core == 0, counts[:, 0], counts[:, 1])[:, None, :]
    second = ((core ^ jnp.arange(blocks, dtype=jnp.int32)) == 1).astype(F32)[None, :, None]
    totals = counts[:, 0] + counts[:, 1]
    smaller = (experts > experts[:, 0][None, :]).astype(F32)
    starts = jnp.sum(totals[:, None, :] * smaller, axis=2) - (core * half).astype(F32)
    places = ranks + (starts[:, None, :] + second * first_counts)[..., None]
    slots = [jnp.sum(jnp.where(one, places, 0.0), axis=2) for one in named]
    slots = jnp.stack(slots, axis=1).astype(jnp.int32).reshape(sequences, TOPK, blocks * count)
    low = jnp.clip(starts, 0, half)
    high = jnp.clip(starts + totals, 0, half)
    limits = jnp.stack([low, high], axis=2).astype(jnp.int32)
    own = lax.dynamic_slice_in_dim(limits, core * local_count, local_count, 1)
    other = lax.dynamic_slice_in_dim(
        limits, jnp.where(core == 0, local_count, local_count - 1), 1, 1
    )
    bounds = jnp.concatenate([own, other], axis=1).reshape(sequences, 2 * (local_count + 1))
    return (slots, bounds, named, jnp.sum(totals, axis=0))


def hits(slots, half):
    numbers = jnp.arange(half, dtype=jnp.int32)[:, None]
    return [slots[:, choice : choice + 1] == numbers for choice in range(TOPK)]


def choice_rows(slots, half, values):
    total = 0.0
    for choice, hit in enumerate(hits(slots, half)):
        total = total + jnp.sum(jnp.where(hit, values[:, choice : choice + 1], 0.0), axis=2)
    return total


def choice_gates(logits, named):
    first, second = [jnp.sum(jnp.where(one, logits, 0.0), axis=2) for one in named]
    return jnp.stack(
        [1.0 / (1.0 + jnp.exp(second - first)), 1.0 / (1.0 + jnp.exp(first - second))], axis=1
    )


def per_device(
    tokens,
    att_gain,
    att_router,
    kv_weight,
    query_weight,
    out_weight,
    mlp_gain,
    mlp_router,
    gate_weight,
    up_weight,
    down_weight,
    att_routes,
    mlp_routes,
    cotangent,
):
    owners = lax.axis_size("expert")
    groups = lax.axis_size("dp")
    shards = lax.axis_size("shard")
    bits = bits_in(groups)
    shard_bits = bits_in(shards)
    local_count = EXPERTS // owners
    count, model_width = tokens.shape
    width = model_width // groups
    part = width // owners
    capacity = 5 * count * TOPK // (4 * EXPERTS)
    half = count * TOPK
    length = owners * count
    windows = [
        min(half, (most + 30) // 16 * 16)
        for most in (owners * capacity, owners * local_count * capacity - half)
    ]
    all_tokens = count * owners * groups
    features = query_weight.shape[2]
    units = gate_weight.shape[2]
    me = lax.axis_index("dp")
    core = lax.axis_index("expert")
    order_a = list(range(bits))
    order_b = order_a[bits // 2 :] + order_a[: bits // 2]
    orders = (order_a, order_b)
    everything = list(range(groups))

    def halves_of(size):
        first = (size // 128 + 1) // 2 * 128 if size >= 256 else size // 2
        return [first, size - first]

    feature_cuts, unit_cuts = halves_of(features), halves_of(units)

    def columns(value, shift=0):
        return [
            lax.dynamic_slice_in_dim(value, (me ^ d) * width + shift, width, 1) for d in range(groups)
        ]

    def core_order(own, other, axis=0):
        return jnp.where(
            core == 0,
            jnp.concatenate([own, other], axis=axis),
            jnp.concatenate([other, own], axis=axis),
        )

    routes = jnp.stack(
        [att_routes[:, 0], att_routes[:, 1], mlp_routes[:, 0], mlp_routes[:, 1]]
    )
    routes = gather_rows(both_blocks(routes, 0), order_a)
    inputs = jnp.stack(spread_columns(columns(tokens)))
    inputs = (inputs, swap(inputs, "expert", 1))
    small = jnp.concatenate(
        [att_gain[:, None], mlp_gain[:, None], att_router, mlp_router], axis=1
    )
    small = core_order(small, swap(small, "expert", 1)).astype(F32)
    gain_a, gain_m = small[:, 0][None, :], small[:, 1][None, :]
    router_a, router_m = small[:, 2 : 2 + EXPERTS].T, small[:, 2 + EXPERTS :].T
    slots_a, bounds_a, named_a, totals_a = route_tables(
        routes[:, :, :TOPK], core, local_count, half
    )
    slots_m, bounds_m, named_m, totals_m = route_tables(
        routes[:, :, TOPK:], core, local_count, half
    )

    columns_a, columns_m = jnp.swapaxes(slots_a, 1, 2), jnp.swapaxes(slots_m, 1, 2)

    def with_other(weight, shift=0):
        mine = lax.dynamic_slice_in_dim(weight, (1 - core) * (local_count - 1) + shift, 1, 0)
        return (weight, swap(mine, "expert", 1))

    plain_values = lambda values, lines, sides: values[0]
    query_pair = with_other(query_weight)
    scaled_values = lambda values, lines, sides: values[0] * lines[0]
    rows_a = dispatch(slots_a, half, [inputs], [gain_a], [], scaled_values)
    group_lists = [scatter_groups(order) for order in orders]
    feature_plan = list(zip(feature_cuts, group_lists))
    unit_plan = list(zip(unit_cuts, group_lists))
    query_parts = expert_product(rows_a, query_pair, bounds_a, feature_plan, windows)
    query_there = query_parts[0][0]
    grad_out = jnp.stack(spread_columns(columns(cotangent, marker(query_there))))
    grad_out = (grad_out, swap(grad_out, "expert", 1))

    scaled_kv = kv_weight.astype(F32) * lax.dynamic_slice_in_dim(gain_a[0], core * part, part)[:, None, None]
    scaled_kv = scaled_kv.astype(BF16)
    own_float = tokens.astype(F32)
    own_rms = lax.rsqrt(jnp.mean(own_float * own_float, axis=1) + EPSILON)
    block_tokens = [
        jnp.concatenate(
            [
                lax.dynamic_slice_in_dim(tokens, ((me ^ d) * owners + (core ^ b)) * part, part, 1)
                for d in everything
            ],
            axis=1,
        )
        for b in range(owners)
    ]
    key_value, kv_all = [], []
    for c, order in enumerate(orders):
        found = {}
        for array, places in gather_pieces(scaled_kv[:, c], order):
            for number, place in enumerate(places):
                found[place] = array[number]
        own = stacked([found[d] for d in everything], [query_there])
        kv_all.append((own, swap(own, "expert", 1)))
        total = sum(
            dot32("tk,kf->tf", some, weight) for some, weight in zip(block_tokens, kv_all[-1])
        )
        total = (total * own_rms[:, None]).astype(BF16)
        key_value.append(jnp.concatenate([total, swap(total, "expert", 1)]))
    keys, values = key_value
    seq_rms = both_blocks(own_rms, 0)

    def own_rows(slots, token_values):
        wide = jnp.broadcast_to(token_values.reshape(1, 1, length), (1, TOPK, length))
        return choice_rows(slots[:1], half, wide)[0][:, None]

    row_rms_a = own_rows(slots_a, seq_rms)
    token_pos = (
        jnp.arange(count, dtype=jnp.int32)[None, :]
        + ((core ^ jnp.arange(owners, dtype=jnp.int32)) * count)[:, None]
    ).astype(F32)
    row_pos = own_rows(slots_a, token_pos)
    key_pos = token_pos.reshape(1, length)

    def gather_cuts(value, cuts):
        return [
            gather_pieces(value[:, : cuts[0]], order_a),
            gather_pieces(value[:, cuts[0] :], order_b),
        ]

    query_passed = []
    queries = jnp.concatenate(
        [
            term_sum(scatter_terms(*parts, order, passed=query_passed))
            for parts, order in zip(query_parts, orders)
        ],
        axis=1,
    )
    queries = (queries * row_rms_a).astype(BF16)
    attention_forward, attention_backward = attention_calls(half, length, features)
    sums_a = router_statistics([inputs], gain_a, router_a, query_passed)
    mixture = attention_forward(queries, keys, values, row_pos, key_pos, earlier=[sums_a])
    mixture_all = gather_cuts(mixture, feature_cuts)

    down_pair = with_other(down_weight)
    grad_rows_m = dispatch(slots_m, half, [grad_out], [], [], plain_values, earlier=[mixture])
    grad_act_parts = expert_product(grad_rows_m, down_pair, bounds_m, unit_plan, windows)
    grad_act = [scatter_terms(*parts, order) for parts, order in zip(grad_act_parts, orders)]

    out_pair = with_other(out_weight)
    shift = marker(mixture)
    gate_pair, up_pair = [with_other(weight, shift) for weight in (gate_weight, up_weight)]

    def statistics(sums):
        total = split_bits(sums, 0, bits)
        for d in range(1, groups):
            received = split_bits(swap(sums, "dp", d), 0, bits)
            turned = [bits - 1 - bit for bit in range(bits) if (d >> bit) & 1]
            total = total + jnp.flip(received, axis=turned)
        sums = join_bits(total, 0, bits)
        rms = lax.rsqrt(sums[:, :, EXPERTS] / model_width + EPSILON)
        return (rms, sums[:, :, :EXPERTS] * rms[:, :, None])

    inputs_f = [value.astype(F32) for value in inputs]
    rms_a, logits_a = statistics(sums_a)
    gates_a = choice_gates(logits_a, named_a)
    row_gates_a = choice_rows(slots_a, half, gates_a.reshape(groups, TOPK, length))[..., None]
    att_part = expert_product_back(
        [(mixture_all[0], out_pair, 0), (mixture_all[1], out_pair, feature_cuts[0])],
        bounds_a,
        everything,
        windows,
        ending=(columns_a, row_gates_a, None, None),
        earlier=[grad_act_parts[0][0]],
    )
    made = {}
    att_total = total_pair(att_part, shards, None, lambda own: [terms[1] for terms in grad_act])

    middle = [one + more.astype(F32) for one, more in zip(inputs_f, att_total)]
    rows_m = dispatch(
        slots_m,
        half,
        [inputs, att_total],
        [gain_m],
        [],
        lambda values, lines, sides: (values[0] + values[1]) * lines[0],
    )

    there = ()
    gate_parts, up_parts = [[], []], [[], []]
    for which in range(2):
        for number, size in enumerate(unit_cuts):
            for parts, pair, order in (
                (gate_parts, gate_pair, order_a), (up_parts, up_pair, order_b)
            ):
                there = expert_product(
                    rows_m,
                    pair,
                    bounds_m,
                    [(size, [scatter_groups(order)[which]])],
                    windows,
                    there,
                    sum(unit_cuts[:number]),
                )[0]
                parts[number] += there
    passed, gate_terms, up_terms = [], [], []
    for number in range(len(unit_cuts)):
        there = tuple(passed)
        gate_terms.append(scatter_terms(*gate_parts[number], order_a, there, passed))
        up_terms.append(scatter_terms(*up_parts[number], order_b, there, passed))
    rms_m, logits_m = statistics(
        router_statistics([inputs, att_total], gain_m, router_m, passed)
    )
    gates_m = choice_gates(logits_m, named_m)
    row_gates_m = choice_rows(slots_m, half, gates_m.reshape(groups, TOPK, length))[..., None]
    row_rms_m = own_rows(slots_m, rms_m[0])
    active_parts, gating_all, upward_all, there = [], [], [], ()
    row_gates_grad, row_norms = 0.0, 0.0
    for number in range(len(unit_cuts)):
        active, grad_gating, grad_upward, dots, norms = unit_rows(
            gate_terms[number], up_terms[number], grad_act[number], row_rms_m, row_gates_m[0], there
        )
        there = [active]
        active_parts.append(active)
        row_gates_grad = row_gates_grad + dots[:, 0]
        row_norms = row_norms + norms[:, 0]
        gating_all.append(gather_pieces(grad_gating, order_a))
        upward_all.append(gather_pieces(grad_upward, order_b))
    side_there = [pieces[0][0] for pieces in gating_all + upward_all]
    active_all = [
        gather_pieces(late(value, *side_there), order)
        for value, order in zip(active_parts, orders)
    ]

    def router_part(
        row_gates_grad, row_norms, more, slots, gates, named, totals, logits, rms, earlier
    ):
        by_choice = [jnp.where(hit[0], row_gates_grad[:, None], 0.0) for hit in hits(slots[:1], half)]
        by_choice = [jnp.sum(one, axis=0) for one in by_choice]
        norms = [jnp.where(hit[0], row_norms[:, None], 0.0) for hit in hits(slots[:1], half)]
        norms = sum(jnp.sum(one, axis=0) for one in norms)
        packed = jnp.stack(by_choice + [norms]).reshape(TOPK + 1, owners, count)
        packed = jnp.transpose(packed, (1, 0, 2))
        packed = jnp.concatenate([packed[:, :TOPK], packed[:, TOPK:] + more], axis=1)
        packed = in_order(gather_directly(late(packed, *earlier)))
        by_choice = jnp.transpose(packed[:, :, :TOPK], (0, 2, 1, 3))
        norms = packed[:, :, TOPK]
        picked = gates * (by_choice - jnp.sum(gates * by_choice, axis=1, keepdims=True))
        picked = sum(
            jnp.where(one, picked[:, choice][:, :, None], 0.0) for choice, one in enumerate(named)
        )
        fraction = totals / (all_tokens * TOPK)
        weighting = (AUX_WEIGHT * EXPERTS / all_tokens) * fraction[:, None]
        probs = jax.nn.softmax(logits, axis=2)
        aux = probs * (weighting - jnp.sum(probs * weighting, axis=2, keepdims=True))
        balance = EXPERTS * EXPERTS * fraction * (jnp.sum(probs, axis=(0, 1, 3)) / all_tokens)
        picked = picked + aux / (owners * shards)
        norms = norms + jnp.sum(picked * logits, axis=2)
        return (picked * rms[:, :, None], total_small(norms, 1, shard_bits), balance)

    router_rows_m, inner_m, balance_m = router_part(
        row_gates_grad, row_norms, 0.0, slots_m, gates_m, named_m, totals_m, logits_m, rms_m,
        side_there,
    )
    carry = expert_product_back(
        [(gating_all[0], gate_pair, 0), (upward_all[0], up_pair, 0)], bounds_m, everything, windows
    )
    back_part = expert_product_back(
        [(gating_all[1], gate_pair, unit_cuts[0]), (upward_all[1], up_pair, unit_cuts[0])],
        bounds_m,
        everything,
        windows,
        carry=carry,
        ending=(columns_m, None, (router_rows_m, router_m), None),
    )
    active_first = [pieces[0][0] for pieces in active_all]

    def weight_grad(rows, parts, bounds, scale=None, earlier=()):
        own, other = expert_grads(rows, parts, bounds, everything, local_count, windows, scale, earlier)
        index = (1 - core) * (local_count - 1)

        def finish(earlier):
            return add_at(own, swap(other, "expert", 1), index, earlier)

        return other, finish

    def gate_grads(own):
        made["gate"] = weight_grad(rows_m, gating_all, bounds_m, earlier=[own])
        return [made["gate"][0]]

    def up_grads(own):
        made["up"] = weight_grad(rows_m, upward_all, bounds_m, earlier=[own])
        return [made["up"][0]] + active_first

    back_total = total_pair(back_part, shards, gate_grads, up_grads)
    back_m = [value.astype(F32) for value in back_total]

    shrink = rms_m * rms_m * inner_m / model_width
    grad_rows_a = dispatch(
        slots_a,
        half,
        [grad_out, back_total, inputs, att_total],
        [gain_m],
        [shrink],
        lambda values, lines, sides: values[0]
        + values[1] * lines[0]
        - (values[2] + values[3]) * sides[0],
    )
    mix_parts = expert_product(grad_rows_a, out_pair, bounds_a, feature_plan, windows)
    mlp_part = expert_product_back(
        [(active_all[0], down_pair, 0), (active_all[1], down_pair, unit_cuts[0])],
        bounds_m,
        everything,
        windows,
        ending=(columns_m, row_gates_m, None, None),
        earlier=[mix_parts[0][0]],
    )
    grad_mix = jnp.concatenate(
        [term_sum(scatter_terms(*parts, order)) for parts, order in zip(mix_parts, orders)], axis=1
    ).astype(BF16)
    layer_own = mlp_part[0] + swap(mlp_part[1], "expert", 1)
    layer_block = middle[0] + lax.psum(layer_own, "shard").astype(F32)
    layer_pieces = spread_columns([layer_block[d].astype(BF16) for d in everything])
    grad_mlp_gain = sum(
        jnp.sum(one * two, axis=(0, 1)) for one, two in zip(back_m, middle)
    )
    grad_mlp_gain = lax.dynamic_slice_in_dim(grad_mlp_gain, core * part, part, 0)
    grad_queries, grad_keys, grad_values, row_gates_grad, row_norms = attention_backward(
        queries, keys, values, row_pos, key_pos, mixture, grad_mix, row_gates_a[0], row_rms_a,
        earlier=[layer_own],
    )
    grad_queries_all = gather_cuts(grad_queries, feature_cuts)

    sent_kv = jnp.stack([grad_keys[count:], grad_values[count:]]).astype(BF16)
    received_kv = swap(sent_kv, "expert", 1).astype(F32)
    own_kv, kv_norms = [], 0.0
    for c, (grad, held) in enumerate(zip((grad_keys, grad_values), key_value)):
        total = grad[:count] + received_kv[c]
        kv_norms = kv_norms + jnp.sum(total * held[:count].astype(F32), axis=-1)
        own_kv.append((total * own_rms[:, None]).astype(BF16))
    kv_norms = jnp.stack([kv_norms, jnp.zeros_like(kv_norms)])
    kv_terms = [
        sum(dot32("tf,kf->tk", own_kv[c], kv_all[c][b]) for c in range(2)) for b in range(owners)
    ]
    kv_terms = [
        core_order(*[term[:, d * part : (d + 1) * part] for term in kv_terms], axis=1).astype(BF16)
        for d in everything
    ]
    kv_back = jnp.stack(spread_columns(kv_terms))
    gate_grad, up_grad = made["gate"][1]([grad_queries]), made["up"][1]([grad_queries])
    router_rows_a, inner_a, balance_a = router_part(
        row_gates_grad[:, 0],
        row_norms[:, 0],
        kv_norms[:, None],
        slots_a,
        gates_a,
        named_a,
        totals_a,
        logits_a,
        rms_a,
        [pieces[0][0] for pieces in grad_queries_all],
    )
    back_part = expert_product_back(
        [(grad_queries_all[0], query_pair, 0), (grad_queries_all[1], query_pair, feature_cuts[0])],
        bounds_a,
        everything,
        windows,
        ending=(columns_a, None, (router_rows_a, router_a), None),
        earlier=kv_terms + [gate_grad, up_grad],
    )
    back_own = (back_part[0].astype(F32) + kv_back.astype(F32) / gain_a).astype(BF16)

    def down_grads(own):
        made["down"] = weight_grad(grad_rows_m, active_all, bounds_m, row_gates_m, earlier=[own])
        return [made["down"][0]]

    tail_parts = core_sum((back_own, back_part[1]), shards)
    back_a = shard_scatter(tail_parts, down_grads)
    grad_kv = [
        gather_rows(late(value, tail_parts[0]), order) for value, order in zip(own_kv, orders)
    ]
    layer_out = place_columns(layer_pieces, F32, [back_a])[0]
    back_there = back_a
    back_a = back_a.astype(F32)
    late_rows = [late(rows, back_there) for rows in (router_rows_a, router_rows_m)]
    grad_kv_weight = 0.0
    router_grads = 0.0
    for block in range(owners):
        scaled = late(inputs[block], tail_parts[0]).astype(F32) * gain_a
        own_scaled = lax.dynamic_slice_in_dim(scaled, core * part, part, 2).astype(BF16)
        some_kv = [one if block == 0 else swap(one, "expert", 1) for one in grad_kv]
        grad_kv_weight = grad_kv_weight + jnp.stack(
            [dot32("dtk,dtf->kf", own_scaled, one) for one in some_kv], axis=1
        )
        one = jnp.einsum("det,dtk->ek", late_rows[0][:, block], scaled, precision=HIGHEST)
        two = jnp.einsum(
            "det,dtk->ek", late_rows[1][:, block], middle[block] * gain_m, precision=HIGHEST
        )
        router_grads = router_grads + jnp.concatenate([one, two])
    router_grads = total_small(router_grads, None, shard_bits)
    router_grads = lax.dynamic_slice_in_dim(router_grads, core * part, part, 1)
    own_inputs = shard_part(inputs_f[0], 1)
    grad_att_gain = total_small(jnp.sum(back_a * own_inputs, axis=(0, 1)), None, shard_bits)
    grad_att_gain = lax.dynamic_slice_in_dim(grad_att_gain, core * part, part, 0)

    def own_part(value):
        return shard_part(value, 1)

    grad_middle = (
        own_part(grad_out[0]).astype(F32)
        + own_part(back_total[0]).astype(F32) * gain_m
        - own_part(middle[0]) * own_part(shrink[:, 0])[..., None]
    )
    shrink_a = own_part(rms_a[:, 0] * rms_a[:, 0] * inner_a[:, 0] / model_width)
    grad_tokens = grad_middle + back_a * gain_a - own_inputs * shrink_a[..., None]
    grad_tokens = place_columns(
        spread_columns([grad_tokens[d].astype(BF16) for d in everything])
    )
    rows_there = grad_tokens
    query_finish = weight_grad(rows_a, grad_queries_all, bounds_a, earlier=[rows_there])[1]
    out_finish = weight_grad(
        grad_rows_a, mixture_all, bounds_a, row_gates_a, earlier=[rows_there]
    )[1]
    grad_tokens = shard_gather(grad_tokens, F32)[0]

    balance_terms = jnp.stack([balance_a, balance_m])
    aux_loss = (jnp.sum(balance_terms) / EXPERTS).reshape(1)
    return (
        layer_out,
        aux_loss,
        grad_tokens,
        grad_att_gain,
        router_grads[:EXPERTS].T,
        grad_kv_weight,
        query_finish([back_a]),
        out_finish([back_a]),
        grad_mlp_gain,
        router_grads[EXPERTS:].T,
        gate_grad,
        up_grad,
        made["down"][1]([back_a]),
        balance_terms,
    )


def solution(mesh):
    rows = P(("dp", "expert"), None)
    vector = P(("dp", "expert"))
    shared = P(("dp", "expert"), None, "shard")
    weight = P("expert", "dp", "shard")
    return jax.shard_map(
        per_device,
        mesh=mesh,
        in_specs=(
            rows, vector, rows, shared, weight, weight, vector, rows,
            weight, weight, weight, rows, rows, rows,
        ),
        out_specs=(
            rows, P(), rows, vector, rows, shared, weight, weight,
            vector, rows, weight, weight, weight, P(),
        ),
        check_vma=False,
    )
```
